32 devices in a mesh: dp: 4 (over y, x), mp: 8 (over z, core).
Axes of the slice: x: 2, y: 2, z: 4, core: 2. Of those that a mesh axis runs over, the one named last changes fastest.
Arguments:
- inputs: bfloat16 [8, 512, 8192], P('dp', 'mp'), may hold values from -6 to 6
- conditioning: bfloat16 [8, 8192, 80], P('dp', 'mp'), may hold values from -6 to 6
- lengths: int32 [8], P('dp'), may hold values from 2048 to 8192, as said below
- cotangent: bfloat16 [8, 2, 512, 8192], P('dp', None, 'mp'), may hold values from -6 to 6
- conv_weight: float32 [1104, 2, 512], P(None, None, 'mp'), may hold values from -0.1875 to 0.1875
- out_weight: float32 [512, 1024], P('mp'), may hold values from -0.75 to 0.75
- biases: float32 [4, 512], P(None, 'mp'), may hold values from -1.75 to 1.75
- conv_first: float32 [1104, 2, 512], P(None, None, 'mp'), may hold values from -1280 to 1280
- out_first: float32 [512, 1024], P('mp'), may hold values from -384 to 384
- bias_first: float32 [4, 512], P(None, 'mp'), may hold values from -1536 to 1536
- conv_second: float32 [1104, 2, 512], P(None, None, 'mp'), may hold values from 26214.4 to 419430.4
- out_second: float32 [512, 1024], P('mp'), may hold values from 1835.008 to 28835.84
- bias_second: float32 [4, 512], P(None, 'mp'), may hold values from 29491.2 to 471859.2
Outputs:
- layer_out: bfloat16 [8, 2, 512, 8192], P('dp', None, 'mp')
- grad_input: float32 [8, 512, 8192], P('dp', 'mp')
- grad_cond: float32 [8, 8192, 80], P('dp', 'mp')
- conv_weight_new: float32 [1104, 2, 512], P(None, None, 'mp')
- out_weight_new: float32 [512, 1024], P('mp')
- biases_new: float32 [4, 512], P(None, 'mp')
- conv_first_new: float32 [1104, 2, 512], P(None, None, 'mp')
- output_moment_renewed: float32 [512, 1024], P('mp')
- bias_first_new: float32 [4, 512], P(None, 'mp')
- conv_second_new: float32 [1104, 2, 512], P(None, None, 'mp')
- out_second_new: float32 [512, 1024], P('mp')
- bias_second_new: float32 [4, 512], P(None, 'mp')
- conv_weight_low: bfloat16 [1104, 2, 512], P(None, None, 'mp')
- out_weight_low: bfloat16 [512, 1024], P('mp')
- biases_low: bfloat16 [4, 512], P(None, 'mp')
The draws below stay inside these ranges and needn't reach their ends.
Inputs may be any that keep to these rules, and one draw needn't show every extreme that they name: `lengths`: each clip's valid length; the first clip is full and the second has 2048 samples.
All inputs are finite; a program needn't handle non-finite values.
Results may differ from the reference program's by a relative error of at most 0.012.
Values may be sent and summed in bfloat16 or wider, within the bound.
A program may use at most 320 MiB of HBM per device.

```python
import math
import jax
import jax.numpy as jnp
from jax import lax

RESIDUAL_WIDTH = 512
GH = 512
M = 80
DILATION_STEP = 32
STEP = 4
SLOT = 8192
CLIPS = 8
TOKENS = 65536


def draw_lengths(key, part):
    spread = jax.random.randint(key, (CLIPS,), SLOT // 4, SLOT + 1)
    spread = spread.at[0].set(SLOT)
    spread = spread.at[1].set(SLOT // 4)
    return spread.astype(jnp.int32)


def steps_of(own_key, shape, cuts, least, largest):
    level, own = 1.0, jax.random.fold_in(own_key, 6)
    for dim, shards_of in cuts:
        heights = jnp.exp(jax.random.uniform(jax.random.fold_in(own, dim), (shards_of,), jnp.float32, least / len(cuts), largest / len(cuts)))
        level = level * jnp.repeat(heights, shape[dim] // shards_of).reshape([-1 if axis == dim else 1 for axis in range(len(shape))])
    return level


def scatter_about(rng, dims, scale, reach, split=(), dtype=jnp.bfloat16):
    values = jax.random.normal(rng, dims, jnp.float32) * scale
    if len(split) > 0:
        values = steps_of(rng, dims, split, -0.22, 0.18) * values
    return jnp.clip(values, min=-reach, max=reach).astype(dtype)


def setup_inputs(seed: int = 0) -> dict:
    streams_of = jax.random.split(jax.random.key(seed), 14)
    return {
        "inputs": scatter_about(streams_of[0], (CLIPS, RESIDUAL_WIDTH, SLOT), 1.0, 6.0, ((0, 4), (1, 8))),
        "conditioning": scatter_about(streams_of[1], (CLIPS, SLOT, M), 1.0, 6.0, ((0, 4), (1, 8))),
        "lengths": draw_lengths(jax.random.fold_in(streams_of[13], 71), 0),
        "cotangent": scatter_about(streams_of[3], (CLIPS, 2, RESIDUAL_WIDTH, SLOT), 1.0, 6.0, ((0, 4), (2, 8))),
        "conv_weight": scatter_about(streams_of[4], (2 * RESIDUAL_WIDTH + M, 2, GH), (2 * RESIDUAL_WIDTH + M) ** -0.5, 0.1875, ((2, 8),), jnp.float32),
        "out_weight": scatter_about(streams_of[5], (GH, 2 * RESIDUAL_WIDTH), (GH // 8) ** -0.5, 0.75, ((0, 8),), jnp.float32),
        "biases": scatter_about(streams_of[6], (4, GH), 0.3, 1.75, ((1, 8),), jnp.float32),
        "conv_first": scatter_about(streams_of[7], (2 * RESIDUAL_WIDTH + M, 2, GH), ((0.8 * TOKENS) ** 0.5), 1280.0, ((2, 8),), jnp.float32),
        "out_first": scatter_about(streams_of[8], (GH, 2 * RESIDUAL_WIDTH), ((0.055 * TOKENS) ** 0.5), 384.0, ((0, 8),), jnp.float32),
        "bias_first": scatter_about(streams_of[9], (4, GH), ((0.9 * TOKENS) ** 0.5), 1536.0, ((1, 8),), jnp.float32),
        "conv_second": jnp.clip(jnp.exp(math.log(419430.4) - 2.7725887 * jax.random.uniform(streams_of[10], (2 * RESIDUAL_WIDTH + M, 2, GH), jnp.float32) ** steps_of(streams_of[10], (2 * RESIDUAL_WIDTH + M, 2, GH), ((2, 8),), -0.2, 0.2)), 26214.4, 419430.4),
        "out_second": jnp.clip(jnp.exp(math.log(28835.84) - 2.7545702 * jax.random.uniform(streams_of[11], (GH, 2 * RESIDUAL_WIDTH), jnp.float32) ** steps_of(streams_of[11], (GH, 2 * RESIDUAL_WIDTH), ((0, 8),), -0.2, 0.2)), 1835.008, 28835.84),
        "bias_second": jnp.clip(jnp.exp(math.log(471859.2) - 2.7725887 * jax.random.uniform(streams_of[12], (4, GH), jnp.float32) ** steps_of(streams_of[12], (4, GH), ((1, 8),), -0.2, 0.2)), 29491.2, 471859.2),
    }


BETA_ONE = 0.5
BETA_TWO = 0.5
EPSILON = 1e-08
WEIGHT_DECAY = 0.01
CONV_RATE = 0.03
OUT_RATE = 0.1
BIAS_RATE = 0.3

@jax.custom_vjp
def low(v):
    return lax.optimization_barrier(v.astype(jnp.bfloat16)).astype(jnp.float32)

@jax.custom_vjp
def low_back(v):
    return v

def low_keep(v):
    return (low(v), None)

def low_pass(kept, grad):
    return (grad,)

def back_keep(v):
    return (v, None)

def back_low(kept, grad):
    return (low(grad),)
low.defvjp(low_keep, low_pass)
low_back.defvjp(back_keep, back_low)

def highest(left_operand, right_op):
    return jnp.dot(left_operand, right_op, precision=lax.Precision.HIGHEST, preferred_element_type=jnp.float32)

def clip_forward(present_tap, condition, conv_weight, out_weight, biases, keep_rows):
    delayed_tap = jnp.concatenate([jnp.zeros((DILATION_STEP, RESIDUAL_WIDTH), jnp.float32), present_tap[:-DILATION_STEP]], axis=0)
    weights = low(conv_weight).reshape(2 * RESIDUAL_WIDTH + M, 2 * GH)
    outputs = low(out_weight)
    bias_low = low(biases)
    pre_act = highest(delayed_tap, weights[:RESIDUAL_WIDTH]) + highest(present_tap, weights[RESIDUAL_WIDTH:2 * RESIDUAL_WIDTH])
    pre_act = pre_act + highest(condition, weights[2 * RESIDUAL_WIDTH:]) + bias_low[0:2].reshape(2 * GH)
    pre_act = low_back(pre_act)
    hidden = keep_rows[:, None] * jnp.tanh(pre_act[:, :GH]) * jax.nn.sigmoid(pre_act[:, GH:])
    hidden = low(hidden)
    branch = highest(hidden, outputs)
    residual = present_tap + branch[:, :RESIDUAL_WIDTH] + bias_low[2]
    skipped = branch[:, RESIDUAL_WIDTH:] + bias_low[3]
    return jnp.stack([residual, skipped], axis=1)

def adamw(master, first_old, second_old, gradient, step_rate, power_one, power_two):
    first_new = BETA_ONE * first_old + (1.0 - BETA_ONE) * gradient
    second_new = BETA_TWO * second_old + (1.0 - BETA_TWO) * gradient * gradient
    first_hat = first_new / (1.0 - power_one)
    second_hat = second_new / (1.0 - power_two)
    renewed = master - step_rate * (first_hat / (jnp.sqrt(second_hat) + EPSILON) + WEIGHT_DECAY * master)
    return (renewed, first_new, second_new)

def reference(inputs, conditioning, lengths, cotangent, conv_weight, out_weight, biases, conv_first, out_first, bias_first, conv_second, out_second, bias_second):
    clips_x = jnp.transpose(inputs.astype(jnp.float32), (0, 2, 1))
    clips_c = conditioning.astype(jnp.float32)
    clips_g = jnp.transpose(cotangent.astype(jnp.float32), (0, 3, 1, 2))
    positions = lax.iota(jnp.int32, SLOT)

    def one_clip(totals, clip_item):
        present_tap, condition, backward, length = clip_item
        keep_rows = (positions < length).astype(jnp.float32)

        def run_clip(cur_in, cond_in, conv_in, out_in, bias_in):
            return clip_forward(cur_in, cond_in, conv_in, out_in, bias_in, keep_rows)
        result, pullback = jax.vjp(run_clip, present_tap, condition, conv_weight, out_weight, biases)
        gradients = pullback(backward)
        totals = (totals[0] + gradients[2], totals[1] + gradients[3], totals[2] + gradients[4])
        return (totals, (result.astype(jnp.bfloat16), gradients[0], gradients[1]))
    start = (jnp.zeros_like(conv_weight), jnp.zeros_like(out_weight), jnp.zeros_like(biases))
    totals, stacked = lax.scan(one_clip, start, (clips_x, clips_c, clips_g, lengths))
    layer_out = jnp.transpose(stacked[0], (0, 2, 3, 1))
    grad_input = jnp.transpose(stacked[1], (0, 2, 1))
    grad_cond = stacked[2]
    power_one = jnp.float32(BETA_ONE ** STEP)
    power_two = jnp.float32(BETA_TWO ** STEP)
    conv_new = adamw(conv_weight, conv_first, conv_second, totals[0], CONV_RATE, power_one, power_two)
    out_new = adamw(out_weight, out_first, out_second, totals[1], OUT_RATE, power_one, power_two)
    bias_new = adamw(biases, bias_first, bias_second, totals[2], BIAS_RATE, power_one, power_two)
    return (layer_out, grad_input, grad_cond, conv_new[0], out_new[0], bias_new[0], conv_new[1], out_new[1], bias_new[1], conv_new[2], out_new[2], bias_new[2], conv_new[0].astype(jnp.bfloat16), out_new[0].astype(jnp.bfloat16), bias_new[0].astype(jnp.bfloat16))
```

```python
import functools

import jax
import jax.numpy as jnp
from jax import lax
from jax.experimental import pallas as pl
from jax.experimental.pallas import tpu as pltpu
from jax.sharding import PartitionSpec as P

RESIDUAL_WIDTH = 512
GH = 512
DILATION_STEP = 32
STEP = 4

BETA_ONE = 0.5
BETA_TWO = 0.5
EPSILON = 1e-08
WEIGHT_DECAY = 0.01
CONV_RATE = 0.03
OUT_RATE = 0.1
BIAS_RATE = 0.3

MESH = pl.DeviceIdType.MESH
LANES = 128
KP = 1152
OUT_AT = 2 * KP
SUM_AT = OUT_AT + 1024
WIDE = 3584
BF = jnp.bfloat16
F32 = jnp.float32


def dot(a, b):
    return jnp.dot(a, b, preferred_element_type=F32)


def dot_nt(a, b):
    return lax.dot_general(a, b, (((1,), (1,)), ((), ())), preferred_element_type=F32)


def layer_kernel(
    n, d, clips, slot, sub,
    x, cot, cnd, lens, wcat, bsum,
    bro, gio, halo, gct, gw,
    xin, cin, wall, wtr, pg, gacc, bst, gst, hst, s1, r1, s2, r2,
    sem_send, sem_x, sem_c, sem_w, sem_out, sem_r1, sem_r2,
):
    g = lax.axis_index("dp")
    m = lax.axis_index("mp")
    r = RESIDUAL_WIDTH // n
    t = slot // n
    piece = WIDE // d

    def peer(k):
        return lax.rem(m + k, n)

    def lane(i, size):
        return pl.ds(pl.multiple_of(i, LANES), size)

    def rows(j):
        return pl.ds(pl.multiple_of(j * r, r), r)

    def remote(src, dst, ss, rs, gg, j):
        return pltpu.make_async_remote_copy(
            src_ref=src, dst_ref=dst, send_sem=ss, recv_sem=rs,
            device_id=(gg, j), device_id_type=MESH,
        )

    def drain(ref, sem):
        pltpu.make_async_copy(ref, ref, sem).wait()

    bar = pltpu.get_barrier_semaphore()

    @pl.loop(1, n)
    def _(k):
        pl.semaphore_signal(bar, inc=1, device_id=(g, peer(k)), device_id_type=MESH)

    @pl.loop(1, d)
    def _(k):
        pl.semaphore_signal(bar, inc=1, device_id=(lax.rem(g + k, d), m), device_id_type=MESH)

    pl.semaphore_wait(bar, n + d - 2)

    mine = lane(g * piece, piece)

    @pl.loop(1, n)
    def _(k):
        remote(wcat.at[:, mine], wall.at[rows(m), mine], sem_send.at[0], sem_w.at[0], g, peer(k)).start()

    pltpu.make_async_copy(wcat.at[:, mine], wall.at[rows(m), mine], sem_w.at[0]).start()

    for c in range(clips):
        @pl.loop(1, n)
        def _(k):
            j = peer(k)
            remote(x.at[c, :, lane(j * t, t)], xin.at[c, rows(m), pl.ds(LANES, t)],
                   sem_send.at[1], sem_x.at[c], g, j).start()
            remote(x.at[c, :, lane(lax.rem(j * t + slot - LANES, slot), LANES)], xin.at[c, rows(m), pl.ds(0, LANES)],
                   sem_send.at[2], sem_x.at[c], g, j).start()
            remote(cot.at[c, :, :, lane(j * t, t)], cin.at[c, :, rows(m), :],
                   sem_send.at[3], sem_c.at[c], g, j).start()

        pltpu.make_async_copy(x.at[c, :, lane(m * t, t)], xin.at[c, rows(m), pl.ds(LANES, t)], sem_x.at[c]).start()
        pltpu.make_async_copy(x.at[c, :, lane(lax.rem(m * t + slot - LANES, slot), LANES)],
                              xin.at[c, rows(m), pl.ds(0, LANES)], sem_x.at[c]).start()
        pltpu.make_async_copy(cot.at[c, :, :, lane(m * t, t)], cin.at[c, :, rows(m), :], sem_c.at[c]).start()

    gacc[...] = jnp.zeros_like(gacc)
    gacc[rows(m), pl.ds(SUM_AT, LANES)] = bsum[...]
    pg[...] = jnp.zeros_like(pg)

    drain(wall.at[:, mine], sem_w.at[0])

    @pl.loop(1, d)
    def _(k):
        remote(wall.at[:, mine], wall.at[:, mine], sem_send.at[4], sem_w.at[1], lax.rem(g + k, d), m).start()

    drain(wall.at[:, pl.ds(0, (d - 1) * piece)], sem_w.at[1])

    @pl.loop(0, SUM_AT // LANES)
    def _(i):
        wtr[pl.ds(pl.multiple_of(i * LANES, LANES), LANES), :] = wall[:, lane(i * LANES, LANES)].T

    def clip(c):
        drain(xin.at[c], sem_x.at[c])

        @pl.when(m == 0)
        def _():
            xin[c, :, 0:LANES] = jnp.zeros((RESIDUAL_WIDTH, LANES), BF)

        drain(cin.at[c], sem_c.at[c])
        length = lens[c]

        @pl.loop(0, t // sub)
        def _(k):
            at = pl.multiple_of(k * sub, LANES)
            now = lane(at, sub)
            off = lane(at + LANES, sub)
            xc = xin[c, :, off]
            xe = pltpu.roll(xin[c, :, lane(at, sub + LANES)], DILATION_STEP, 1)[:, LANES:]
            cd = cnd[c, :, now]
            pre_f = (dot(wall[:, 0:512], xe) + dot(wall[:, 512:1024], xc) + dot(wall[:, 1024:KP], cd))
            pre_g = (dot(wall[:, KP:KP + 512], xe) + dot(wall[:, KP + 512:KP + 1024], xc)
                     + dot(wall[:, KP + 1024:OUT_AT], cd))
            place = m * t + at + lax.broadcasted_iota(jnp.int32, (1, sub), 1)
            keep = (place < length).astype(F32)
            th = jnp.tanh(pre_f)
            sg = jax.nn.sigmoid(pre_g)
            hid = (keep * th * sg).astype(BF)
            branch = dot(wtr[OUT_AT:SUM_AT, :], hid).astype(BF)
            bst[c, 0, :, now] = branch[0:512]
            bst[c, 1, :, now] = branch[512:1024]

            @pl.loop(1, n)
            def _(q):
                j = peer(q)
                remote(bst.at[c, :, rows(j), now], bro.at[c, :, :, lane(m * t + at, sub)],
                       sem_send.at[5], sem_out.at[0], g, j).start()

            pltpu.make_async_copy(bst.at[c, :, rows(m), now], bro.at[c, :, :, lane(m * t + at, sub)],
                                  sem_out.at[0]).start()
            ct = cin[c, :, :, now].reshape(1024, sub)
            hg = dot(wall[:, OUT_AT:SUM_AT], ct) * keep
            pgf = (hg * sg * (1.0 - th * th)).astype(BF)
            pgg = (hg * th * sg * (1.0 - sg)).astype(BF)
            pg[0:512, off] = pgf
            pg[512:1024, off] = pgg
            gacc[:, 0:512] += dot_nt(pgf, xe)
            gacc[:, 512:1024] += dot_nt(pgf, xc)
            gacc[:, 1024:KP] += dot_nt(pgf, cd)
            gacc[:, KP:KP + 512] += dot_nt(pgg, xe)
            gacc[:, KP + 512:KP + 1024] += dot_nt(pgg, xc)
            gacc[:, KP + 1024:OUT_AT] += dot_nt(pgg, cd)
            gacc[:, OUT_AT:SUM_AT] += dot_nt(hid, ct)
            gct[c, :, now] = dot(wtr[1024:KP, :], pgf) + dot(wtr[KP + 1024:OUT_AT, :], pgg)

        def back(off, size):
            win = pg[:, lane(off, size + LANES)]
            pn = win[:, :size]
            pe = pltpu.roll(win, size + LANES - DILATION_STEP, 1)[:, :size]
            return (dot(wtr[512:1024, :], pn[0:512]) + dot(wtr[KP + 512:KP + 1024, :], pn[512:1024])
                    + dot(wtr[0:512, :], pe[0:512]) + dot(wtr[KP:KP + 512, :], pe[512:1024]))

        hst[c] = back(0, LANES).astype(BF)

        @pl.loop(1, n)
        def _(q):
            j = peer(q)
            remote(hst.at[c, rows(j), :], halo.at[c, :, lane(m * LANES, LANES)],
                   sem_send.at[6], sem_out.at[1], g, j).start()

        pltpu.make_async_copy(hst.at[c, rows(m), :], halo.at[c, :, lane(m * LANES, LANES)], sem_out.at[1]).start()

        @pl.loop(0, t // sub)
        def _(k):
            at = pl.multiple_of(k * sub, LANES)
            now = lane(at, sub)
            gst[c, :, now] = back(at + LANES, sub).astype(BF)

            @pl.loop(1, n)
            def _(q):
                j = peer(q)
                remote(gst.at[c, rows(j), now], gio.at[c, :, lane(m * t + at, sub)],
                       sem_send.at[7], sem_out.at[2], g, j).start()

            pltpu.make_async_copy(gst.at[c, rows(m), now], gio.at[c, :, lane(m * t + at, sub)],
                                  sem_out.at[2]).start()

    pl.loop(0, clips)(clip)

    @pl.loop(1, d)
    def _(k):
        to = lax.rem(g + k, d)
        s1[k - 1] = gacc[:, lane(to * piece, piece)].astype(BF)
        remote(s1.at[k - 1], r1.at[k - 1], sem_send.at[8], sem_r1.at[k - 1], to, m).start()

    @pl.loop(1, d)
    def _(k):
        drain(r1.at[k - 1], sem_r1.at[k - 1])
        gacc[:, mine] += r1[k - 1].astype(F32)

    s2[...] = gacc[:, mine].astype(BF)

    @pl.loop(1, n)
    def _(k):
        j = peer(k)
        remote(s2.at[rows(j), :], r2.at[k - 1], sem_send.at[9], sem_r2.at[k - 1], g, j).start()

    gw[:, mine] = gacc[rows(m), mine]

    @pl.loop(1, n)
    def _(k):
        drain(r2.at[k - 1], sem_r2.at[k - 1])
        gw[:, mine] += r2[k - 1].astype(F32)

    @pl.loop(1, d)
    def _(k):
        remote(gw.at[:, mine], gw.at[:, mine], sem_send.at[10], sem_w.at[2], lax.rem(g + k, d), m).start()

    drain(gw.at[:, pl.ds(0, (d - 1) * piece)], sem_w.at[2])

    others = pl.ds(0, (n - 1) * r)
    drain(wall.at[others, pl.ds(0, piece)], sem_send.at[0])
    drain(x.at[:, :, pl.ds(0, (n - 1) * t)], sem_send.at[1])
    drain(halo.at[:, :, pl.ds(0, (n - 1) * LANES)], sem_send.at[2])
    drain(cot.at[:, :, :, pl.ds(0, (n - 1) * t)], sem_send.at[3])
    drain(wall.at[:, pl.ds(0, (d - 1) * piece)], sem_send.at[4])
    drain(bst.at[:, :, others, :], sem_send.at[5])
    drain(hst.at[:, others, :], sem_send.at[6])
    drain(gst.at[:, others, :], sem_send.at[7])
    drain(s1, sem_send.at[8])
    drain(s2.at[others, :], sem_send.at[9])
    drain(gw.at[:, pl.ds(0, (d - 1) * piece)], sem_send.at[10])
    drain(bro, sem_out.at[0])
    drain(halo, sem_out.at[1])
    drain(gio, sem_out.at[2])


def run_layer(n, d, x, cot, cnd, lens, wcat, bsum):
    clips, r, slot = x.shape
    t = slot // n
    sub = min(256, t)
    piece = WIDE // d
    width = RESIDUAL_WIDTH
    any_spec = pl.BlockSpec(memory_space=pl.ANY)
    vmem = pl.BlockSpec(memory_space=pltpu.VMEM)
    smem = pl.BlockSpec(memory_space=pltpu.SMEM)
    dma = pltpu.SemaphoreType.DMA
    return pl.pallas_call(
        functools.partial(layer_kernel, n, d, clips, slot, sub),
        out_shape=(
            jax.ShapeDtypeStruct((clips, 2, r, slot), BF),
            jax.ShapeDtypeStruct((clips, r, slot), BF),
            jax.ShapeDtypeStruct((clips, r, n * LANES), BF),
            jax.ShapeDtypeStruct((clips, LANES, t), F32),
            jax.ShapeDtypeStruct((r, WIDE), F32),
        ),
        in_specs=[any_spec, any_spec, vmem, smem, vmem, vmem],
        out_specs=(any_spec, any_spec, any_spec, vmem, vmem),
        scratch_shapes=[
            pltpu.VMEM((clips, width, LANES + t), BF),
            pltpu.VMEM((clips, 2, width, t), BF),
            pltpu.VMEM((GH, WIDE), BF),
            pltpu.VMEM((SUM_AT, GH), BF),
            pltpu.VMEM((2 * GH, t + 2 * LANES), BF),
            pltpu.VMEM((GH, WIDE), F32),
            pltpu.VMEM((clips, 2, width, t), BF),
            pltpu.VMEM((clips, width, t), BF),
            pltpu.VMEM((clips, width, LANES), BF),
            pltpu.VMEM((d - 1, GH, piece), BF),
            pltpu.VMEM((d - 1, GH, piece), BF),
            pltpu.VMEM((GH, piece), BF),
            pltpu.VMEM((n - 1, r, piece), BF),
            dma((11,)),
            dma((clips,)),
            dma((clips,)),
            dma((3,)),
            dma((3,)),
            dma((d - 1,)),
            dma((n - 1,)),
        ],
        compiler_params=pltpu.CompilerParams(
            collective_id=0, has_side_effects=True, vmem_limit_bytes=60 << 20
        ),
    )(x, cot, cnd, lens, wcat, bsum)


def adamw(master, first_old, second_old, gradient, step_rate, power_one, power_two):
    first_new = BETA_ONE * first_old + (1.0 - BETA_ONE) * gradient
    second_new = BETA_TWO * second_old + (1.0 - BETA_TWO) * gradient * gradient
    first_hat = first_new / (1.0 - power_one)
    second_hat = second_new / (1.0 - power_two)
    renewed = master - step_rate * (
        first_hat / (jnp.sqrt(second_hat) + EPSILON) + WEIGHT_DECAY * master
    )
    return (renewed, first_new, second_new)


def per_device(
    n, d,
    inputs, conditioning, lengths, cotangent, conv_weight, out_weight, biases,
    conv_first, out_first, bias_first, conv_second, out_second, bias_second,
):
    clips, r, slot = inputs.shape
    t = slot // n
    taps = conv_weight.shape[0]
    mel = conditioning.shape[2]
    bias_low = biases.astype(BF)
    flipped = jnp.transpose(conv_weight.astype(BF), (1, 2, 0))
    flipped = jnp.concatenate(
        [flipped, bias_low[0:2, :, None], jnp.zeros((2, r, KP - taps - 1), BF)], axis=2
    )
    wcat = jnp.concatenate(
        [flipped[0], flipped[1], out_weight.astype(BF), jnp.zeros((r, WIDE - SUM_AT), BF)], axis=1
    )
    cnd = jnp.concatenate(
        [
            jnp.transpose(conditioning, (0, 2, 1)),
            jnp.ones((clips, 1, t), BF),
            jnp.zeros((clips, LANES - mel - 1, t), BF),
        ],
        axis=1,
    )
    sums = jnp.sum(cotangent.astype(F32), axis=(0, 3))
    bsum = jnp.pad(sums.T, ((0, 0), (0, LANES - 2)))
    bro, gio, halo, gct, gw = run_layer(n, d, inputs, cotangent, cnd, lengths, wcat, bsum)

    bias_out = bias_low[2:4].astype(F32)
    layer_out = jnp.stack(
        [
            inputs.astype(F32) + bro[:, 0].astype(F32) + bias_out[0][None, :, None],
            bro[:, 1].astype(F32) + bias_out[1][None, :, None],
        ],
        axis=1,
    ).astype(BF)
    edge = halo.astype(F32).reshape(clips, r, n, LANES)
    edge = jnp.concatenate([edge[:, :, 1:], jnp.zeros((clips, r, 1, LANES), F32)], axis=2)
    edge = jnp.pad(edge, ((0, 0), (0, 0), (0, 0), (t - LANES, 0))).reshape(clips, r, slot)
    grad_input = cotangent[:, 0].astype(F32) + (gio.astype(F32) + edge)
    grad_cond = jnp.transpose(gct[:, :mel], (0, 2, 1))
    conv_grad = jnp.transpose(
        jnp.stack([gw[:, :taps], gw[:, KP : KP + taps]], axis=0), (2, 0, 1)
    )
    out_grad = gw[:, OUT_AT:SUM_AT]
    bias_grad = jnp.stack(
        [gw[:, taps], gw[:, KP + taps], gw[:, SUM_AT], gw[:, SUM_AT + 1]], axis=0
    )
    power_one = jnp.float32(BETA_ONE**STEP)
    power_two = jnp.float32(BETA_TWO**STEP)
    conv_new = adamw(
        conv_weight, conv_first, conv_second, conv_grad, CONV_RATE, power_one, power_two
    )
    out_new = adamw(out_weight, out_first, out_second, out_grad, OUT_RATE, power_one, power_two)
    bias_new = adamw(biases, bias_first, bias_second, bias_grad, BIAS_RATE, power_one, power_two)
    return (
        layer_out,
        grad_input,
        grad_cond,
        conv_new[0],
        out_new[0],
        bias_new[0],
        conv_new[1],
        out_new[1],
        bias_new[1],
        conv_new[2],
        out_new[2],
        bias_new[2],
        conv_new[0].astype(BF),
        out_new[0].astype(BF),
        bias_new[0].astype(BF),
    )


def solution(mesh):
    in_specs = (
        P("dp", "mp", None),
        P("dp", "mp", None),
        P("dp"),
        P("dp", None, "mp", None),
        P(None, None, "mp"),
        P("mp", None),
        P(None, "mp"),
        P(None, None, "mp"),
        P("mp", None),
        P(None, "mp"),
        P(None, None, "mp"),
        P("mp", None),
        P(None, "mp"),
    )
    out_specs = (
        P("dp", None, "mp", None),
        P("dp", "mp", None),
        P("dp", "mp", None),
        P(None, None, "mp"),
        P("mp", None),
        P(None, "mp"),
        P(None, None, "mp"),
        P("mp", None),
        P(None, "mp"),
        P(None, None, "mp"),
        P("mp", None),
        P(None, "mp"),
        P(None, None, "mp"),
        P("mp", None),
        P(None, "mp"),
    )
    return jax.shard_map(
        functools.partial(per_device, mesh.shape["mp"], mesh.shape["dp"]),
        mesh=mesh, in_specs=in_specs, out_specs=out_specs, check_vma=False,
    )
```

```python
import functools

import jax
import jax.numpy as jnp
from jax import lax
from jax.experimental import pallas as pl
from jax.experimental.pallas import tpu as pltpu
from jax.sharding import PartitionSpec as P

RESIDUAL_WIDTH = 512
GH = 512
DILATION_STEP = 32
STEP = 4

BETA_ONE = 0.5
BETA_TWO = 0.5
EPSILON = 1e-08
WEIGHT_DECAY = 0.01
CONV_RATE = 0.03
OUT_RATE = 0.1
BIAS_RATE = 0.3

MESH = pl.DeviceIdType.MESH
LANES = 128
HALF = RESIDUAL_WIDTH // 2
KP = 1152
OUT_AT = 2 * KP
USED = OUT_AT + 2 * HALF
WIDE = 3072
AHEAD = 10
OWN = 6
SLOTS = 4
BF = jnp.bfloat16
F32 = jnp.float32


def dot(a, b):
    return jnp.dot(a, b, preferred_element_type=F32)


def dot_nt(a, b):
    return lax.dot_general(a, b, (((1,), (1,)), ((), ())), preferred_element_type=F32)


def layer_kernel(
    n, d, clips, slot, sub, mel,
    x, cot, cond, lens, wcat, bsum,
    bro, gio, gco, gw, bs,
    xin, cin, cnd, grecv, gsend, gown, wall, wtr, pg, gacc, ost, gfs, gcs, r0, r1, s2,
    sem_fx, sem_fc, sem_send, sem_xh, sem_xm, sem_c, sem_k, sem_gm, sem_o, sem_gf, sem_gc, sem_in, sem_r1,
):
    g = lax.axis_index("dp")
    m = lax.axis_index("mp")
    r = RESIDUAL_WIDTH // n
    t = slot // n
    per = t // sub
    blocks = slot // sub
    piece = WIDE // d
    half = n // 2
    band = GH // clips
    share = n // clips
    h = m // half
    first = h * half
    local = m - first
    worker = jnp.logical_and(m >= half - clips, m < half + clips)
    wc = lax.rem(m + 2 * clips * n - (half - clips), clips)
    mirror = half - clips + (1 - h) * clips + wc
    group = m // share
    own_rows = jnp.logical_and(worker, group == wc)

    def wid(hh, c):
        return half - clips + hh * clips + c

    def lane(i, size=sub):
        return pl.ds(pl.multiple_of(i, LANES), size)

    def rows(j):
        return pl.ds(pl.multiple_of(j * r, r), r)

    def remote(src, dst, ss, rs, gg, j):
        return pltpu.make_async_remote_copy(
            src_ref=src, dst_ref=dst, send_sem=ss, recv_sem=rs,
            device_id=(gg, j), device_id_type=MESH,
        )

    def drain(ref, sem):
        pltpu.make_async_copy(ref, ref, sem).wait()

    bar = pltpu.get_barrier_semaphore()

    @pl.loop(1, n)
    def _(k):
        pl.semaphore_signal(bar, inc=1, device_id=(g, lax.rem(m + k, n)), device_id_type=MESH)

    @pl.loop(1, d)
    def _(k):
        pl.semaphore_signal(bar, inc=1, device_id=(lax.rem(g + k, d), m), device_id_type=MESH)

    pl.semaphore_wait(bar, n + d - 2)

    mine = lane(g * piece, piece)
    kept = pl.ds(pl.multiple_of(wc * band, band), band)

    def send_cond():
        for hh in range(2):
            for c in range(clips):
                to = wid(hh, c)
                dst = cnd.at[pl.ds(0, mel), lane(m * t, t)]

                @pl.when(to == m)
                def _():
                    pltpu.make_async_copy(cond.at[c], dst, sem_k.at[m]).start()

                @pl.when(to != m)
                def _():
                    remote(cond.at[c], dst, sem_send.at[0], sem_k.at[m], g, to).start()

    turn = jnp.maximum(m * per - 4, 0)

    for hh in range(2):
        to = wid(hh, group)

        @pl.when(to == m)
        def _():
            pltpu.make_async_copy(wcat.at[hh, :, mine], wall.at[rows(m), mine], sem_in.at[0]).start()

        @pl.when(to != m)
        def _():
            remote(wcat.at[hh, :, mine], wall.at[rows(m), mine], sem_send.at[1], sem_in.at[0], g, to).start()

    @pl.loop(1, d)
    def _(k):
        remote(bsum, bs.at[g], sem_send.at[2], sem_in.at[3], lax.rem(g + k, d), m).start()

    pltpu.make_async_copy(bsum, bs.at[g], sem_in.at[3]).start()

    def far():
        def send_x(s):
            at = s * sub

            @pl.when(s >= SLOTS)
            def _():
                drain(x.at[:, :, pl.ds(0, sub)], sem_fx.at[lax.rem(s, SLOTS)])

            for c in range(clips):
                remote(x.at[c, :, lane(at)], xin.at[rows(m), lane(at + LANES)],
                       sem_fx.at[lax.rem(s, SLOTS)], sem_xh.at[s], g, wid(h, c)).start()

        def send_cot(s):
            at = s * sub

            @pl.when(s >= SLOTS)
            def _():
                drain(cot.at[:, :, :, pl.ds(0, sub)], sem_fc.at[lax.rem(s, SLOTS)])

            for c in range(clips):
                remote(cot.at[c, :, :, lane(at)], cin.at[:, rows(local), lane(at)],
                       sem_fc.at[lax.rem(s, SLOTS)], sem_c.at[s], g, wid(h, c)).start()

        pl.loop(0, AHEAD)(send_x)

        @pl.loop(0, blocks)
        def _(s):
            @pl.when(s == turn)
            def _():
                send_cond()

            @pl.when(s + AHEAD < blocks)
            def _():
                send_x(s + AHEAD)

            send_cot(s)

        @pl.loop(0, SLOTS)
        def _(q):
            drain(x.at[:, :, pl.ds(0, sub)], sem_fx.at[q])
            drain(cot.at[:, :, :, pl.ds(0, sub)], sem_fc.at[q])

    def work():
        def own(s):
            at = s * sub
            for k in range(1, clips):
                c = lax.rem(wc + k, clips)
                remote(x.at[c, :, lane(at)], xin.at[rows(m), lane(at + LANES)],
                       sem_send.at[3], sem_xh.at[s], g, wid(h, c)).start()
                remote(cot.at[c, :, :, lane(at)], cin.at[:, rows(local), lane(at)],
                       sem_send.at[4], sem_c.at[s], g, wid(h, c)).start()
            pltpu.make_async_copy(x.at[wc, :, lane(at)], xin.at[rows(m), lane(at + LANES)], sem_xh.at[s]).start()
            pltpu.make_async_copy(cot.at[wc, :, :, lane(at)], cin.at[:, rows(local), lane(at)], sem_c.at[s]).start()

        here = pl.ds(pl.multiple_of(h * HALF, HALF), HALF)
        there = pl.ds(pl.multiple_of((1 - h) * HALF, HALF), HALF)

        def relay(s):
            part = xin.at[here, lane(s * sub + LANES)]
            drain(part, sem_xh.at[s])
            remote(part, part, sem_send.at[5], sem_xm.at[s], g, mirror).start()

        pl.loop(0, OWN)(own)

        xin[:, 0:LANES] = jnp.zeros((RESIDUAL_WIDTH, LANES), BF)
        pg[...] = jnp.zeros_like(pg)
        cnd[mel:LANES, :] = (
            lax.broadcasted_iota(jnp.int32, (LANES - mel, slot), 0) == 0
        ).astype(F32).astype(BF)
        gacc[...] = jnp.zeros_like(gacc)

        pl.loop(0, 3)(relay)
        drain(wall.at[kept, mine], sem_in.at[0])

        @pl.loop(1, d)
        def _(k):
            remote(wall.at[kept, mine], wall.at[kept, mine], sem_send.at[6], sem_in.at[1],
                   lax.rem(g + k, d), m).start()

        pl.loop(3, OWN)(relay)
        drain(wall.at[kept, pl.ds(0, (d - 1) * piece)], sem_in.at[1])
        for k in range(1, clips):
            remote(wall.at[kept, :], wall.at[kept, :], sem_send.at[7], sem_in.at[2], g,
                   wid(h, lax.rem(wc + k, clips))).start()
        pl.loop(OWN, AHEAD)(lambda s: (own(s), relay(s))[0])
        pl.loop(AHEAD, AHEAD + OWN)(own)
        drain(wall.at[pl.ds(0, GH - band), :], sem_in.at[2])

        @pl.loop(0, USED // LANES)
        def _(i):
            wtr[pl.ds(pl.multiple_of(i * LANES, LANES), LANES), :] = wall[:, lane(i * LANES, LANES)].T

        length = lens[wc]

        def back(top):
            win = pg[...]
            pn = win[:, :sub]
            pe = pltpu.roll(win, sub + LANES - DILATION_STEP, 1)[:, :sub]

            def tap(base):
                return wtr[pl.ds(pl.multiple_of(base + top, HALF), HALF), :]

            return (dot(tap(512), pn[0:512]) + dot(wtr[pl.ds(pl.multiple_of(KP + 512 + top, LANES), HALF), :], pn[512:1024])
                    + dot(tap(0), pe[0:512]) + dot(wtr[pl.ds(pl.multiple_of(KP + top, LANES), HALF), :], pe[512:1024]))

        def give(q):
            remote(gsend.at[:, lane((q + 1) * sub)], grecv.at[:, lane(q * sub)],
                   sem_send.at[8], sem_gm.at[q], g, mirror).start()

        def combine(q):
            now = lane(q * sub)
            z = lax.rem(q, SLOTS)
            drain(grecv.at[:, now], sem_gm.at[q])

            @pl.when(q >= SLOTS)
            def _():
                drain(gfs.at[z], sem_gf.at[z])

            gfs[z] = (gown[:, lane((q + 1) * sub)].astype(F32) + grecv[:, now].astype(F32)).astype(BF)

            @pl.loop(1, half)
            def _(k):
                i = lax.rem(local + k, half)
                remote(gfs.at[z, rows(i), :], gio.at[wc, :, now], sem_gf.at[z], sem_in.at[5], g, first + i).start()

            pltpu.make_async_copy(gfs.at[z, rows(local), :], gio.at[wc, :, now], sem_gf.at[z]).start()

        @pl.loop(0, blocks)
        def _(s):
            at = s * sub
            now = lane(at)
            off = lane(at + LANES)
            z = lax.rem(s, SLOTS)

            @pl.when(s == turn)
            def _():
                send_cond()

            @pl.when(s + AHEAD + OWN < blocks)
            def _():
                own(s + AHEAD + OWN)

            @pl.when(s + AHEAD < blocks)
            def _():
                relay(s + AHEAD)

            @pl.when(lax.rem(s, per) == 0)
            def _():
                drain(cnd.at[pl.ds(0, mel), lane((s // per) * t, t)], sem_k.at[s // per])

            drain(xin.at[there, off], sem_xm.at[s])
            drain(cin.at[:, :, now], sem_c.at[s])

            xc = xin[:, off]
            xe = pltpu.roll(xin[:, lane(at, sub + LANES)], DILATION_STEP, 1)[:, LANES:]
            cd = cnd[:, now]
            pre_f = (dot(wall[:, 0:512], xe) + dot(wall[:, 512:1024], xc) + dot(wall[:, 1024:KP], cd))
            pre_g = (dot(wall[:, KP:KP + 512], xe) + dot(wall[:, KP + 512:KP + 1024], xc)
                     + dot(wall[:, KP + 1024:OUT_AT], cd))
            place = at + lax.broadcasted_iota(jnp.int32, (1, sub), 1)
            keep = (place < length).astype(F32)
            th = jnp.tanh(pre_f)
            sg = jax.nn.sigmoid(pre_g)
            hid = (keep * th * sg).astype(BF)
            branch = dot(wtr[OUT_AT:USED, :], hid).astype(BF)

            @pl.when(s >= SLOTS)
            def _():
                drain(ost.at[z], sem_o.at[z])
                drain(gcs.at[z], sem_gc.at[z])

            ost[z, 0] = branch[0:HALF]
            ost[z, 1] = branch[HALF:]

            @pl.loop(1, half)
            def _(k):
                i = lax.rem(local + k, half)
                remote(ost.at[z, :, rows(i), :], bro.at[wc, :, :, now], sem_o.at[z], sem_in.at[4], g, first + i).start()

            pltpu.make_async_copy(ost.at[z, :, rows(local), :], bro.at[wc, :, :, now], sem_o.at[z]).start()

            ct = cin[:, :, now].reshape(2 * HALF, sub)
            hg = dot(wall[:, OUT_AT:USED], ct) * keep
            pgf = (hg * sg * (1.0 - th * th)).astype(BF)
            pgg = (hg * th * sg * (1.0 - sg)).astype(BF)
            pg[0:512, sub:] = pgf[:, :LANES]
            pg[512:1024, sub:] = pgg[:, :LANES]
            gacc[:, 0:512] += dot_nt(pgf, xe)
            gacc[:, 512:1024] += dot_nt(pgf, xc)
            gacc[:, 1024:KP] += dot_nt(pgf, cd)
            gacc[:, KP:KP + 512] += dot_nt(pgg, xe)
            gacc[:, KP + 512:KP + 1024] += dot_nt(pgg, xc)
            gacc[:, KP + 1024:OUT_AT] += dot_nt(pgg, cd)
            gacc[:, OUT_AT:USED] += dot_nt(hid, ct)
            gcs[z] = (dot(wtr[1024:KP, :], pgf) + dot(wtr[KP + 1024:OUT_AT, :], pgg))[0:mel].astype(BF)
            keeper = s // per
            spot = gco.at[h * clips + wc, :, lane(at - keeper * t)]

            @pl.when(keeper == m)
            def _():
                pltpu.make_async_copy(gcs.at[z], spot, sem_gc.at[z]).start()

            @pl.when(keeper != m)
            def _():
                remote(gcs.at[z], spot, sem_gc.at[z], sem_in.at[6], g, keeper).start()

            gsend[:, now] = back((1 - h) * HALF).astype(BF)
            gown[:, now] = back(h * HALF).astype(BF)
            pg[0:512, 0:sub] = pgf
            pg[512:1024, 0:sub] = pgg

            @pl.when(lax.rem(s, 2) == 0)
            def _():
                @pl.when(s >= 2)
                def _():
                    give(s // 2 - 1)

                @pl.when(s >= 10)
                def _():
                    combine(s // 2 - 5)

        pg[:, sub:] = jnp.zeros((2 * GH, LANES), BF)
        gsend[:, pl.ds(slot, sub)] = back((1 - h) * HALF).astype(BF)
        gown[:, pl.ds(slot, sub)] = back(h * HALF).astype(BF)

        s0 = cin.at[0, :, pl.ds(0, WIDE)]
        for k in range(1, clips):
            to = lax.rem(wc + k, clips)
            s0[...] = gacc[pl.ds(pl.multiple_of(to * band, band), band), :].astype(BF)
            remote(s0, r0.at[k - 1], sem_send.at[9], sem_in.at[7], g, wid(h, to)).start()

        pl.loop(blocks // 2 - 1, blocks)(give)
        mid = blocks // 2 - 5
        step = (blocks - mid) // 4
        pl.loop(mid, mid + step)(combine)
        drain(r0, sem_in.at[7])
        for k in range(1, clips):
            gacc[kept, :] += r0[k - 1].astype(F32)

        @pl.loop(1, d)
        def _(k):
            to = lax.rem(g + k, d)
            src = cin.at[1, :, lane((k - 1) * piece, piece)]
            src[...] = gacc[kept, lane(to * piece, piece)].astype(BF)
            remote(src, r1.at[k - 1], sem_send.at[10], sem_r1.at[k - 1], to, m).start()

        pl.loop(mid + step, mid + 2 * step)(combine)

        @pl.loop(1, d)
        def _(k):
            drain(r1.at[k - 1], sem_r1.at[k - 1])
            gacc[kept, mine] += r1[k - 1].astype(F32)

        s2[...] = gacc[kept, mine].astype(BF)

        @pl.loop(0, share)
        def _(k):
            j = wc * share + k

            @pl.when(j == m)
            def _():
                pltpu.make_async_copy(s2.at[rows(k), :], gw.at[h, :, mine], sem_in.at[8]).start()

            @pl.when(j != m)
            def _():
                remote(s2.at[rows(k), :], gw.at[h, :, mine], sem_send.at[11], sem_in.at[8], g, j).start()

        pl.loop(mid + 2 * step, mid + 3 * step)(combine)
        share_out()
        pl.loop(mid + 3 * step, blocks)(combine)

        @pl.loop(0, SLOTS)
        def _(q):
            drain(ost.at[q], sem_o.at[q])
            drain(gcs.at[q], sem_gc.at[q])
            drain(gfs.at[q], sem_gf.at[q])

        drain(x.at[pl.ds(0, clips - 1)], sem_send.at[3])
        drain(cot.at[pl.ds(0, clips - 1)], sem_send.at[4])
        drain(xin.at[pl.ds(0, HALF), pl.ds(0, slot)], sem_send.at[5])
        drain(wall.at[kept, pl.ds(0, (d - 1) * piece)], sem_send.at[6])
        drain(wall.at[pl.ds(0, GH - band), :], sem_send.at[7])
        drain(gsend.at[:, pl.ds(0, slot)], sem_send.at[8])
        drain(r0, sem_send.at[9])
        drain(r1, sem_send.at[10])

    def share_out():
        drain(gw.at[:, :, mine], sem_in.at[8])

        @pl.loop(1, d)
        def _(k):
            remote(gw.at[:, :, mine], gw.at[:, :, mine], sem_send.at[12], sem_in.at[9], lax.rem(g + k, d), m).start()

    @pl.when(worker)
    def _():
        work()
        drain(gco.at[pl.ds(0, 2 * clips - 1)], sem_send.at[0])
        drain(bro.at[pl.ds(0, clips - 1)], sem_in.at[4])
        drain(gio.at[pl.ds(0, clips - 1)], sem_in.at[5])
        drain(gco.at[pl.ds(0, 2 * clips - 1)], sem_in.at[6])

        @pl.when(own_rows)
        def _():
            drain(wcat.at[0, :, mine], sem_send.at[1])
            drain(s2.at[pl.ds(0, (share - 1) * r), :], sem_send.at[11])

        @pl.when(jnp.logical_not(own_rows))
        def _():
            drain(wcat.at[:, :, mine], sem_send.at[1])
            drain(s2, sem_send.at[11])

    @pl.when(jnp.logical_not(worker))
    def _():
        far()
        share_out()
        drain(gco, sem_send.at[0])
        drain(wcat.at[:, :, mine], sem_send.at[1])
        drain(bro, sem_in.at[4])
        drain(gio, sem_in.at[5])
        drain(gco, sem_in.at[6])

    drain(gw.at[:, :, pl.ds(0, (d - 1) * piece)], sem_in.at[9])
    drain(gw.at[:, :, pl.ds(0, (d - 1) * piece)], sem_send.at[12])
    drain(bs, sem_in.at[3])
    drain(bs.at[pl.ds(0, d - 1)], sem_send.at[2])


def run_layer(n, d, x, cot, cond, lens, wcat, bsum):
    clips, r, slot = x.shape
    mel = cond.shape[1]
    t = slot // n
    sub = min(256, t)
    blocks = slot // sub
    piece = WIDE // d
    width = RESIDUAL_WIDTH
    band = GH // clips
    any_spec = pl.BlockSpec(memory_space=pl.ANY)
    vmem = pl.BlockSpec(memory_space=pltpu.VMEM)
    smem = pl.BlockSpec(memory_space=pltpu.SMEM)
    dma = pltpu.SemaphoreType.DMA
    return pl.pallas_call(
        functools.partial(layer_kernel, n, d, clips, slot, sub, mel),
        out_shape=(
            jax.ShapeDtypeStruct((clips, 2, r, slot), BF),
            jax.ShapeDtypeStruct((clips, r, slot), BF),
            jax.ShapeDtypeStruct((2 * clips, mel, t), BF),
            jax.ShapeDtypeStruct((2, r, WIDE), BF),
            jax.ShapeDtypeStruct((d, r, LANES), F32),
        ),
        in_specs=[any_spec, any_spec, any_spec, smem, vmem, vmem],
        out_specs=(any_spec, any_spec, any_spec, vmem, vmem),
        scratch_shapes=[
            pltpu.VMEM((width, LANES + slot), BF),
            pltpu.VMEM((2, HALF, slot), BF),
            pltpu.VMEM((LANES, slot), BF),
            pltpu.VMEM((HALF, slot), BF),
            pltpu.VMEM((HALF, slot + sub), BF),
            pltpu.VMEM((HALF, slot + sub), BF),
            pltpu.VMEM((GH, WIDE), BF),
            pltpu.VMEM((USED, GH), BF),
            pltpu.VMEM((2 * GH, sub + LANES), BF),
            pltpu.VMEM((GH, WIDE), F32),
            pltpu.VMEM((SLOTS, 2, HALF, sub), BF),
            pltpu.VMEM((SLOTS, HALF, sub), BF),
            pltpu.VMEM((SLOTS, mel, sub), BF),
            pltpu.VMEM((clips - 1, band, WIDE), BF),
            pltpu.VMEM((d - 1, band, piece), BF),
            pltpu.VMEM((band, piece), BF),
            dma((SLOTS,)),
            dma((SLOTS,)),
            dma((13,)),
            dma((blocks,)),
            dma((blocks,)),
            dma((blocks,)),
            dma((n,)),
            dma((blocks,)),
            dma((SLOTS,)),
            dma((SLOTS,)),
            dma((SLOTS,)),
            dma((10,)),
            dma((d - 1,)),
        ],
        compiler_params=pltpu.CompilerParams(
            collective_id=0, has_side_effects=True, vmem_limit_bytes=60 << 20
        ),
    )(x, cot, cond, lens, wcat, bsum)


def adamw(master, first_old, second_old, gradient, step_rate, power_one, power_two):
    first_new = BETA_ONE * first_old + (1.0 - BETA_ONE) * gradient
    second_new = BETA_TWO * second_old + (1.0 - BETA_TWO) * gradient * gradient
    first_hat = first_new / (1.0 - power_one)
    second_hat = second_new / (1.0 - power_two)
    renewed = master - step_rate * (
        first_hat / (jnp.sqrt(second_hat) + EPSILON) + WEIGHT_DECAY * master
    )
    return (renewed, first_new, second_new)


def per_device(
    n, d,
    inputs, conditioning, lengths, cotangent, conv_weight, out_weight, biases,
    conv_first, out_first, bias_first, conv_second, out_second, bias_second,
):
    clips, r, slot = inputs.shape
    taps = conv_weight.shape[0]
    bias_low = biases.astype(BF)
    flipped = jnp.transpose(conv_weight.astype(BF), (1, 2, 0))
    flipped = jnp.concatenate(
        [flipped, bias_low[0:2, :, None], jnp.zeros((2, r, KP - taps - 1), BF)], axis=2
    )
    out_low = out_weight.astype(BF).reshape(r, 2, 2, HALF)
    wcat = jnp.stack(
        [
            jnp.concatenate(
                [
                    flipped[0],
                    flipped[1],
                    out_low[:, 0, side],
                    out_low[:, 1, side],
                    jnp.zeros((r, WIDE - USED), BF),
                ],
                axis=1,
            )
            for side in range(2)
        ],
        axis=0,
    )
    cond = jnp.transpose(conditioning, (0, 2, 1))
    sums = jnp.sum(cotangent.astype(F32), axis=(0, 3))
    bsum = jnp.pad(sums.T, ((0, 0), (0, LANES - 2)))
    bro, gio, gco, gw, bs = run_layer(n, d, inputs, cotangent, cond, lengths, wcat, bsum)

    bias_out = bias_low[2:4].astype(F32)
    layer_out = jnp.stack(
        [
            inputs.astype(F32) + bro[:, 0].astype(F32) + bias_out[0][None, :, None],
            bro[:, 1].astype(F32) + bias_out[1][None, :, None],
        ],
        axis=1,
    ).astype(BF)
    grad_input = cotangent[:, 0].astype(F32) + gio.astype(F32)
    grad_cond = jnp.transpose(gco[:clips].astype(F32) + gco[clips:].astype(F32), (0, 2, 1))
    gsum = gw[0, :, :OUT_AT].astype(F32) + gw[1, :, :OUT_AT].astype(F32)
    conv_grad = jnp.transpose(
        jnp.stack([gsum[:, :taps], gsum[:, KP : KP + taps]], axis=0), (2, 0, 1)
    )
    out_grad = jnp.stack(
        [gw[:, :, OUT_AT : OUT_AT + HALF], gw[:, :, OUT_AT + HALF : USED]], axis=0
    )
    out_grad = jnp.transpose(out_grad, (2, 0, 1, 3)).reshape(r, 4 * HALF).astype(F32)
    bsums = jnp.sum(bs, axis=0)
    bias_grad = jnp.stack([gsum[:, taps], gsum[:, KP + taps], bsums[:, 0], bsums[:, 1]], axis=0)
    power_one = jnp.float32(BETA_ONE**STEP)
    power_two = jnp.float32(BETA_TWO**STEP)
    conv_new = adamw(
        conv_weight, conv_first, conv_second, conv_grad, CONV_RATE, power_one, power_two
    )
    out_new = adamw(out_weight, out_first, out_second, out_grad, OUT_RATE, power_one, power_two)
    bias_new = adamw(biases, bias_first, bias_second, bias_grad, BIAS_RATE, power_one, power_two)
    return (
        layer_out,
        grad_input,
        grad_cond,
        conv_new[0],
        out_new[0],
        bias_new[0],
        conv_new[1],
        out_new[1],
        bias_new[1],
        conv_new[2],
        out_new[2],
        bias_new[2],
        conv_new[0].astype(BF),
        out_new[0].astype(BF),
        bias_new[0].astype(BF),
    )


def solution(mesh):
    in_specs = (
        P("dp", "mp", None),
        P("dp", "mp", None),
        P("dp"),
        P("dp", None, "mp", None),
        P(None, None, "mp"),
        P("mp", None),
        P(None, "mp"),
        P(None, None, "mp"),
        P("mp", None),
        P(None, "mp"),
        P(None, None, "mp"),
        P("mp", None),
        P(None, "mp"),
    )
    out_specs = (
        P("dp", None, "mp", None),
        P("dp", "mp", None),
        P("dp", "mp", None),
        P(None, None, "mp"),
        P("mp", None),
        P(None, "mp"),
        P(None, None, "mp"),
        P("mp", None),
        P(None, "mp"),
        P(None, None, "mp"),
        P("mp", None),
        P(None, "mp"),
        P(None, None, "mp"),
        P("mp", None),
        P(None, "mp"),
    )
    return jax.shard_map(
        functools.partial(per_device, mesh.shape["mp"], mesh.shape["dp"]),
        mesh=mesh, in_specs=in_specs, out_specs=out_specs, check_vma=False,
    )
```

```python
import functools

import jax
import jax.numpy as jnp
from jax import lax
from jax.experimental import pallas as pl
from jax.experimental.pallas import tpu as pltpu
from jax.sharding import PartitionSpec as P

RESIDUAL_WIDTH = 512
GH = 512
DILATION_STEP = 32
STEP = 4

BETA_ONE = 0.5
BETA_TWO = 0.5
EPSILON = 1e-08
WEIGHT_DECAY = 0.01
CONV_RATE = 0.03
OUT_RATE = 0.1
BIAS_RATE = 0.3

MESH = pl.DeviceIdType.MESH
LANES = 128
HALF = RESIDUAL_WIDTH // 2
KP = 1152
OUT_AT = 2 * KP
USED = OUT_AT + 2 * HALF
WIDE = 3072
AHEAD = 16
OWN = 6
DIRECT = 6
GIVE = 14
LAG = 8
SLOTS = 4
LATE = 12
POSTS = 8
BF = jnp.bfloat16
F32 = jnp.float32


def dot(a, b):
    return jnp.dot(a, b, preferred_element_type=F32)


def dot_nt(a, b):
    return lax.dot_general(a, b, (((1,), (1,)), ((), ())), preferred_element_type=F32)


def layer_kernel(
    n, d, clips, slot, sub, mel,
    x, cot, cond, lens, wcat,
    bro, gio, gco, gw,
    xin, cin, cnd, grecv, gsend, gown, wall, wfw, wtr, pg, gacc, csum, ost, gfs, gk, kr, r0, r1, s2, r2,
    sem_fx, sem_fc, sem_send, sem_xh, sem_xm, sem_c, sem_k, sem_km, sem_kr, sem_gm, sem_gv, sem_o, sem_gf, sem_in, sem_r1,
):
    g = lax.axis_index("dp")
    m = lax.axis_index("mp")
    r = RESIDUAL_WIDTH // n
    t = slot // n
    per = t // sub
    blocks = slot // sub
    piece = WIDE // d
    half = n // 2
    band = GH // clips
    h = m // half
    first = h * half
    local = m - first
    worker = jnp.logical_and(m >= half - clips, m < half + clips)
    wc = lax.rem(m + 2 * clips * n - (half - clips), clips)
    mirror = half - clips + (1 - h) * clips + wc
    hub = jnp.logical_and(worker, wc == h)
    shared = (g + 1) * piece <= OUT_AT

    def wid(hh, c):
        return half - clips + hh * clips + c

    def lane(i, size=sub):
        return pl.ds(pl.multiple_of(i, LANES), size)

    def rows(j):
        return pl.ds(pl.multiple_of(j * r, r), r)

    def remote(src, dst, ss, rs, gg, j):
        return pltpu.make_async_remote_copy(
            src_ref=src, dst_ref=dst, send_sem=ss, recv_sem=rs,
            device_id=(gg, j), device_id_type=MESH,
        )

    def others(body):
        if half <= 4:
            for k in range(1, half):
                body(lax.rem(local + k, half))
        else:
            pl.loop(1, half)(lambda k: body(lax.rem(local + k, half)))

    def drain(ref, sem):
        pltpu.make_async_copy(ref, ref, sem).wait()

    def whole(ref, count, sem):
        drain(ref.at[0, :, pl.ds(0, count * piece)] if count <= d else ref.at[:, :, pl.ds(0, count // 2 * piece)], sem)

    bar = pltpu.get_barrier_semaphore()

    @pl.loop(1, half)
    def _(k):
        pl.semaphore_signal(bar, inc=1, device_id=(g, first + lax.rem(local + k, half)), device_id_type=MESH)

    @pl.loop(1, d)
    def _(k):
        pl.semaphore_signal(bar, inc=1, device_id=(lax.rem(g + k, d), m), device_id_type=MESH)

    @pl.when(worker)
    def _():
        for c in range(clips):
            pl.semaphore_signal(bar, inc=1, device_id=(g, wid(1 - h, c)), device_id_type=MESH)
        pl.semaphore_wait(bar, half + d - 2 + clips)

    @pl.when(jnp.logical_not(worker))
    def _():
        pl.semaphore_wait(bar, half + d - 2)

    mine = lane(g * piece, piece)
    kept = pl.ds(pl.multiple_of(wc * band, band), band)

    def send_cond(s):
        @pl.when(s // per == m)
        def _():
            dst = cnd.at[pl.ds(0, mel), lane(s * sub)]
            for c in range(clips):
                to = wid(h, c)
                part = cond.at[c, :, lane(s * sub - m * t)]

                @pl.when(to == m)
                def _():
                    pltpu.make_async_copy(part, dst, sem_k.at[s]).start()

                @pl.when(to != m)
                def _():
                    remote(part, dst, sem_send.at[0], sem_k.at[s], g, to).start()

    def in_half(s):
        return s // (blocks // 2) == h

    def weights():
        @pl.when(hub)
        def _():
            pltpu.make_async_copy(wcat.at[h, :, mine], wall.at[rows(m), mine], sem_in.at[0]).start()
            pltpu.make_async_copy(wcat.at[1 - h, :, mine], wfw.at[rows(local), :], sem_in.at[3]).start()

        @pl.when(jnp.logical_not(hub))
        def _():
            remote(wcat.at[h, :, mine], wall.at[rows(m), mine], sem_send.at[1], sem_in.at[0], g, wid(h, h)).start()
            remote(wcat.at[1 - h, :, mine], wfw.at[rows(local), :], sem_send.at[1], sem_in.at[3], g, wid(h, h)).start()

    def far():
        def send_x(s):
            at = s * sub

            @pl.when(s >= SLOTS)
            def _():
                drain(x.at[:, :, pl.ds(0, sub)], sem_fx.at[lax.rem(s, SLOTS)])

            for c in range(clips):
                remote(x.at[c, :, lane(at)], xin.at[rows(m), lane(at + LANES)],
                       sem_fx.at[lax.rem(s, SLOTS)], sem_xh.at[s], g, wid(h, c)).start()
            send_cond(s)

        def send_cot(s):
            at = s * sub

            @pl.when(s >= SLOTS)
            def _():
                drain(cot.at[:, :, :, pl.ds(0, sub)], sem_fc.at[lax.rem(s, SLOTS)])

            for c in range(clips):
                remote(cot.at[c, :, :, lane(at)], cin.at[:, rows(local), lane(at)],
                       sem_fc.at[lax.rem(s, SLOTS)], sem_c.at[s], g, wid(h, c)).start()

        pl.loop(0, 2)(send_x)
        weights()
        pl.loop(2, AHEAD)(send_x)

        @pl.loop(0, blocks)
        def _(s):
            @pl.when(s + AHEAD < blocks)
            def _():
                send_x(s + AHEAD)

            send_cot(s)

        @pl.loop(0, SLOTS)
        def _(q):
            drain(x.at[:, :, pl.ds(0, sub)], sem_fx.at[q])
            drain(cot.at[:, :, :, pl.ds(0, sub)], sem_fc.at[q])

    def work():
        def own(s):
            at = s * sub
            for k in range(1, clips):
                c = lax.rem(wc + k, clips)
                remote(x.at[c, :, lane(at)], xin.at[rows(m), lane(at + LANES)],
                       sem_send.at[3], sem_xh.at[s], g, wid(h, c)).start()
                remote(cot.at[c, :, :, lane(at)], cin.at[:, rows(local), lane(at)],
                       sem_send.at[4], sem_c.at[s], g, wid(h, c)).start()
            pltpu.make_async_copy(x.at[wc, :, lane(at)], xin.at[rows(m), lane(at + LANES)], sem_xh.at[s]).start()
            pltpu.make_async_copy(cot.at[wc, :, :, lane(at)], cin.at[:, rows(local), lane(at)], sem_c.at[s]).start()
            send_cond(s)

        here = pl.ds(pl.multiple_of(h * HALF, HALF), HALF)
        there = pl.ds(pl.multiple_of((1 - h) * HALF, HALF), HALF)

        def direct(s):
            at = s * sub
            for k in range(clips):
                c = lax.rem(wc + k, clips)
                remote(x.at[c, :, lane(at)], xin.at[rows(m), lane(at + LANES)],
                       sem_send.at[17], sem_xm.at[s], g, wid(1 - h, c)).start()

        far_rows = pl.ds(pl.multiple_of(h * (HALF + clips * r), r), HALF - clips * r)

        def relay(s):
            part = xin.at[far_rows, lane(s * sub + LANES)]
            drain(xin.at[here, lane(s * sub + LANES)], sem_xh.at[s])
            remote(part, part, sem_send.at[5], sem_xm.at[s], g, mirror).start()

            @pl.when(s + DIRECT < blocks)
            def _():
                direct(s + DIRECT)

            @pl.when(in_half(s))
            def _():
                also = cnd.at[pl.ds(0, mel), lane(s * sub)]
                drain(also, sem_k.at[s])
                remote(also, also, sem_send.at[12], sem_km.at[s], g, mirror).start()

        pl.loop(0, DIRECT)(direct)
        weights()
        pl.loop(0, AHEAD + OWN)(own)

        xin[:, 0:LANES] = jnp.zeros((RESIDUAL_WIDTH, LANES), BF)
        pg[...] = jnp.zeros_like(pg)
        cnd[mel:LANES, :] = (
            lax.broadcasted_iota(jnp.int32, (LANES - mel, slot), 0) == 0
        ).astype(F32).astype(BF)
        gacc[...] = jnp.zeros_like(gacc)
        csum[...] = jnp.zeros_like(csum)

        pl.loop(0, 2)(relay)
        drain(wall.at[kept, mine], sem_in.at[0])

        @pl.when(hub)
        def _():
            drain(wfw, sem_in.at[3])
            remote(wfw, wall.at[kept, mine], sem_send.at[2], sem_in.at[0], g, mirror).start()

        @pl.loop(1, d)
        def _(k):
            remote(wall.at[kept, mine], wall.at[kept, mine], sem_send.at[6], sem_in.at[1],
                   lax.rem(g + k, d), m).start()

        pl.loop(2, 9)(relay)
        drain(wall.at[kept, pl.ds(0, (d - 1) * piece)], sem_in.at[1])
        for k in range(1, clips):
            remote(wall.at[kept, :], wall.at[kept, :], sem_send.at[7], sem_in.at[2], g,
                   wid(h, lax.rem(wc + k, clips))).start()
        pl.loop(9, AHEAD)(relay)
        drain(wall.at[pl.ds(0, GH - band), :], sem_in.at[2])

        @pl.loop(0, USED // LANES)
        def _(i):
            wtr[pl.ds(pl.multiple_of(i * LANES, LANES), LANES), :] = wall[:, lane(i * LANES, LANES)].T

        length = lens[wc]

        def back(top):
            win = pg[...]
            pn = win[:, :sub]
            pe = pltpu.roll(win, sub + LANES - DILATION_STEP, 1)[:, :sub]

            def tap(base):
                return wtr[pl.ds(pl.multiple_of(base + top, HALF), HALF), :]

            return (dot(tap(512), pn[0:512]) + dot(wtr[pl.ds(pl.multiple_of(KP + 512 + top, LANES), HALF), :], pn[512:1024])
                    + dot(tap(0), pe[0:512]) + dot(wtr[pl.ds(pl.multiple_of(KP + top, LANES), HALF), :], pe[512:1024]))

        def gone(q):
            drain(gsend.at[:, pl.ds(0, sub)], sem_gv.at[lax.rem(q, POSTS)])

        def give(q):
            remote(gsend.at[:, lane((q + 1) * sub)], grecv.at[:, lane(q * sub)],
                   sem_gv.at[lax.rem(q, POSTS)], sem_gm.at[q], g, mirror).start()

        def add_cond(s):
            now = lane(s * sub)
            keeper = s // per
            spot = gco.at[wc, :, lane(s * sub - keeper * t)]
            drain(kr.at[:, now], sem_kr.at[s])
            gk[:, now] = (gk[:, now].astype(F32) + kr[:, now].astype(F32)).astype(BF)

            @pl.when(keeper == m)
            def _():
                pltpu.make_async_copy(gk.at[:, now], spot, sem_send.at[13]).start()

            @pl.when(keeper != m)
            def _():
                remote(gk.at[:, now], spot, sem_send.at[14], sem_in.at[6], g, keeper).start()

        def combine(q):
            now = lane(q * sub)
            z = lax.rem(q, SLOTS)
            drain(grecv.at[:, now], sem_gm.at[q])

            @pl.when(q >= SLOTS)
            def _():
                drain(gfs.at[z], sem_gf.at[z])

            gfs[z] = (gown[:, lane((q + 1) * sub)].astype(F32) + grecv[:, now].astype(F32)).astype(BF)

            @others
            def _(i):
                remote(gfs.at[z, rows(i), :], gio.at[wc, :, now], sem_gf.at[z], sem_in.at[5], g, first + i).start()

            pltpu.make_async_copy(gfs.at[z, rows(local), :], gio.at[wc, :, now], sem_gf.at[z]).start()

        def send_results(s):
            now = lane(s * sub)
            z = lax.rem(s, SLOTS)

            @others
            def _(i):
                remote(ost.at[z, :, rows(i), :], bro.at[wc, :, :, now], sem_o.at[z], sem_in.at[10], g, first + i).start()

            pltpu.make_async_copy(ost.at[z, :, rows(local), :], bro.at[wc, :, :, now], sem_o.at[z]).start()

            @pl.when(jnp.logical_not(in_half(s)))
            def _():
                remote(gk.at[:, now], kr.at[:, now], sem_send.at[8], sem_kr.at[s], g, mirror).start()

        @pl.loop(0, blocks)
        def _(s):
            at = s * sub
            now = lane(at)
            off = lane(at + LANES)
            z = lax.rem(s, SLOTS)

            @pl.when(s + AHEAD + OWN < blocks)
            def _():
                own(s + AHEAD + OWN)

            @pl.when(s + AHEAD < blocks)
            def _():
                relay(s + AHEAD)

            @pl.when(s >= 1)
            def _():
                send_results(s - 1)

            @pl.when(s >= GIVE + POSTS)
            def _():
                gone(s - GIVE - POSTS)

            @pl.when(s >= GIVE)
            def _():
                give(s - GIVE)

            @pl.when(s >= GIVE + LAG)
            def _():
                combine(s - GIVE - LAG)

            @pl.when(jnp.logical_and(s >= LATE, in_half(s - LATE)))
            def _():
                add_cond(s - LATE)

            @pl.when(jnp.logical_not(in_half(s)))
            def _():
                drain(cnd.at[pl.ds(0, mel), now], sem_km.at[s])

            @pl.when(s >= SLOTS)
            def _():
                drain(ost.at[z], sem_o.at[z])

            drain(xin.at[there, off], sem_xm.at[s])
            drain(cin.at[:, :, now], sem_c.at[s])

            xc = xin[:, off]
            xe = pltpu.roll(xin[:, lane(at, sub + LANES)], DILATION_STEP, 1)[:, LANES:]
            cd = cnd[:, now]
            pre_f = (dot(wall[:, 0:512], xe) + dot(wall[:, 512:1024], xc) + dot(wall[:, 1024:KP], cd))
            pre_g = (dot(wall[:, KP:KP + 512], xe) + dot(wall[:, KP + 512:KP + 1024], xc)
                     + dot(wall[:, KP + 1024:OUT_AT], cd))
            place = at + lax.broadcasted_iota(jnp.int32, (1, sub), 1)
            keep = (place < length).astype(F32)
            th = jnp.tanh(pre_f)
            sg = jax.nn.sigmoid(pre_g)
            hid = (keep * th * sg).astype(BF)
            branch = dot(wtr[OUT_AT:USED, :], hid)
            offset = wall[here, USED:USED + LANES].astype(F32)
            ost[z, 0] = (xin[here, off].astype(F32) + branch[0:HALF] + offset[:, 0:1]).astype(BF)
            ost[z, 1] = (branch[HALF:] + offset[:, 1:2]).astype(BF)
            ct = cin[:, :, now].reshape(2 * HALF, sub)
            for q in range(sub // LANES):
                csum[...] += ct[:, q * LANES:(q + 1) * LANES].astype(F32)
            hg = dot(wall[:, OUT_AT:USED], ct) * keep
            pgf = (hg * sg * (1.0 - th * th)).astype(BF)
            pgg = (hg * th * sg * (1.0 - sg)).astype(BF)
            pg[0:512, sub:] = pgf[:, :LANES]
            pg[512:1024, sub:] = pgg[:, :LANES]
            gacc[:, 0:512] += dot_nt(pgf, xe)
            gacc[:, 512:1024] += dot_nt(pgf, xc)
            gacc[:, 1024:KP] += dot_nt(pgf, cd)
            gacc[:, KP:KP + 512] += dot_nt(pgg, xe)
            gacc[:, KP + 512:KP + 1024] += dot_nt(pgg, xc)
            gacc[:, KP + 1024:OUT_AT] += dot_nt(pgg, cd)
            gacc[:, OUT_AT:USED] += dot_nt(hid, ct)
            gk[:, now] = (dot(wtr[1024:KP, :], pgf) + dot(wtr[KP + 1024:OUT_AT, :], pgg))[0:mel].astype(BF)
            gsend[:, now] = back((1 - h) * HALF).astype(BF)
            gown[:, now] = back(h * HALF).astype(BF)
            pg[0:512, 0:sub] = pgf
            pg[512:1024, 0:sub] = pgg

        send_results(blocks - 1)
        pg[:, sub:] = jnp.zeros((2 * GH, LANES), BF)
        gsend[:, pl.ds(slot, sub)] = back((1 - h) * HALF).astype(BF)
        gown[:, pl.ds(slot, sub)] = back(h * HALF).astype(BF)

        def spread(part, dst, sem):
            @others
            def _(i):
                remote(part.at[rows(i), :], dst, sem, sem_in.at[8], g, first + i).start()

            pltpu.make_async_copy(part.at[rows(local), :], dst, sem_in.at[8]).start()

        spot = lax.broadcasted_iota(jnp.int32, (HALF, LANES), 1)
        total = jnp.sum(csum[...], axis=1, keepdims=True)
        gacc[here, USED:USED + LANES] = jnp.where(spot == 0, total[0:HALF], jnp.where(spot == 1, total[HALF:], 0.0))

        s0 = cin.at[0, :, pl.ds(0, WIDE)]
        for k in range(1, clips):
            to = lax.rem(wc + k, clips)
            s0[...] = gacc[pl.ds(pl.multiple_of(to * band, band), band), :].astype(BF)
            remote(s0, r0.at[k - 1], sem_send.at[9], sem_in.at[7], g, wid(h, to)).start()

        start = blocks - GIVE
        pl.loop(start - POSTS, start - SLOTS)(gone)

        def tail(q):
            gone(q - SLOTS)
            give(q)
            combine(q - LAG)
            more = q + GIVE - LATE

            @pl.when(jnp.logical_and(more < blocks, in_half(more)))
            def _():
                add_cond(more)

        pl.loop(start, start + 2)(tail)
        drain(r0, sem_in.at[7])
        for k in range(1, clips):
            gacc[kept, :] += r0[k - 1].astype(F32)

        @pl.loop(1, d)
        def _(k):
            to = lax.rem(g + k, d)
            src = cin.at[1, :, lane((k - 1) * piece, piece)]
            src[...] = gacc[kept, lane(to * piece, piece)].astype(BF)
            remote(src, r1.at[k - 1], sem_send.at[10], sem_r1.at[k - 1], to, m).start()

        pl.loop(start + 2, start + 7)(tail)

        @pl.loop(1, d)
        def _(k):
            drain(r1.at[k - 1], sem_r1.at[k - 1])
            gacc[kept, mine] += r1[k - 1].astype(F32)

        s2[...] = gacc[kept, mine].astype(BF)

        @pl.when(jnp.logical_not(hub))
        def _():
            remote(s2, r2, sem_send.at[11], sem_in.at[4], g, mirror).start()

        pl.loop(start + 7, start + 13)(tail)

        @pl.when(hub)
        def _():
            drain(r2, sem_in.at[4])

            @pl.when(shared)
            def _():
                s2[...] = (gacc[kept, mine] + r2[...].astype(F32)).astype(BF)
                spread(s2, gw.at[0, :, mine], sem_send.at[11])

            @pl.when(jnp.logical_not(shared))
            def _():
                spread(s2, gw.at[h, :, mine], sem_send.at[11])
                spread(r2, gw.at[1 - h, :, mine], sem_send.at[15])

        pl.loop(start + 13, blocks)(tail)
        share_out()
        pl.loop(blocks - SLOTS, blocks)(gone)
        pl.loop(blocks - LAG, blocks)(combine)

        @pl.loop(0, SLOTS)
        def _(q):
            drain(ost.at[q], sem_o.at[q])
            drain(gfs.at[q], sem_gf.at[q])

        drain(x.at[pl.ds(0, clips - 1)], sem_send.at[3])
        drain(cot.at[pl.ds(0, clips - 1)], sem_send.at[4])
        drain(xin.at[pl.ds(0, HALF - clips * r), pl.ds(0, slot)], sem_send.at[5])
        drain(x, sem_send.at[17])
        drain(wall.at[kept, pl.ds(0, (d - 1) * piece)], sem_send.at[6])
        drain(wall.at[pl.ds(0, GH - band), :], sem_send.at[7])
        drain(gk.at[:, pl.ds(0, slot // 2)], sem_send.at[8])
        drain(cnd.at[pl.ds(0, mel), pl.ds(0, slot // 2)], sem_send.at[12])
        drain(gk.at[:, pl.ds(0, t)], sem_send.at[13])
        drain(gk.at[:, pl.ds(0, slot // 2 - t)], sem_send.at[14])
        drain(r0, sem_send.at[9])
        drain(r1, sem_send.at[10])

    def share_out():
        @pl.when(shared)
        def _():
            drain(gw.at[0, :, mine], sem_in.at[8])
            share(gw.at[0, :, mine])

        @pl.when(jnp.logical_not(shared))
        def _():
            drain(gw.at[:, :, mine], sem_in.at[8])
            share(gw.at[:, :, mine])

    def share(part):
        @pl.loop(1, d)
        def _(k):
            remote(part, part, sem_send.at[16], sem_in.at[9], lax.rem(g + k, d), m).start()

    @pl.when(worker)
    def _():
        work()
        drain(cond.at[pl.ds(0, clips - 1)], sem_send.at[0])
        drain(bro.at[pl.ds(0, clips - 1)], sem_in.at[10])
        drain(gio.at[pl.ds(0, clips - 1)], sem_in.at[5])
        drain(gco.at[pl.ds(0, clips - 1)], sem_in.at[6])

        @pl.when(hub)
        def _():
            drain(wfw, sem_send.at[2])
            drain(s2.at[pl.ds(0, HALF - r), :], sem_send.at[11])

            @pl.when(jnp.logical_not(shared))
            def _():
                drain(r2.at[pl.ds(0, HALF - r), :], sem_send.at[15])

        @pl.when(jnp.logical_not(hub))
        def _():
            drain(wcat.at[:, :, mine], sem_send.at[1])
            drain(s2, sem_send.at[11])

    @pl.when(jnp.logical_not(worker))
    def _():
        far()
        share_out()
        drain(cond, sem_send.at[0])
        drain(wcat.at[:, :, mine], sem_send.at[1])
        drain(bro, sem_in.at[10])
        drain(gio, sem_in.at[5])
        drain(gco, sem_in.at[6])

    own_piece = 2 * d - OUT_AT // piece

    @pl.when(shared)
    def _():
        whole(gw, own_piece - 1, sem_in.at[9])
        whole(gw, d - 1, sem_send.at[16])

    @pl.when(jnp.logical_not(shared))
    def _():
        whole(gw, own_piece - 2, sem_in.at[9])
        whole(gw, 2 * (d - 1), sem_send.at[16])


def run_layer(n, d, x, cot, cond, lens, wcat):
    clips, r, slot = x.shape
    mel = cond.shape[1]
    t = slot // n
    sub = min(256, t)
    blocks = slot // sub
    piece = WIDE // d
    width = RESIDUAL_WIDTH
    band = GH // clips
    any_spec = pl.BlockSpec(memory_space=pl.ANY)
    vmem = pl.BlockSpec(memory_space=pltpu.VMEM)
    smem = pl.BlockSpec(memory_space=pltpu.SMEM)
    dma = pltpu.SemaphoreType.DMA
    return pl.pallas_call(
        functools.partial(layer_kernel, n, d, clips, slot, sub, mel),
        out_shape=(
            jax.ShapeDtypeStruct((clips, 2, r, slot), BF),
            jax.ShapeDtypeStruct((clips, r, slot), BF),
            jax.ShapeDtypeStruct((clips, mel, t), BF),
            jax.ShapeDtypeStruct((2, r, WIDE), BF),
        ),
        in_specs=[any_spec, any_spec, any_spec, smem, vmem],
        out_specs=(any_spec, any_spec, any_spec, vmem),
        scratch_shapes=[
            pltpu.VMEM((width, LANES + slot), BF),
            pltpu.VMEM((2, HALF, slot), BF),
            pltpu.VMEM((LANES, slot), BF),
            pltpu.VMEM((HALF, slot), BF),
            pltpu.VMEM((HALF, slot + sub), BF),
            pltpu.VMEM((HALF, slot + sub), BF),
            pltpu.VMEM((GH, WIDE), BF),
            pltpu.VMEM((HALF, piece), BF),
            pltpu.VMEM((USED, GH), BF),
            pltpu.VMEM((2 * GH, sub + LANES), BF),
            pltpu.VMEM((GH, WIDE), F32),
            pltpu.VMEM((2 * HALF, LANES), F32),
            pltpu.VMEM((SLOTS, 2, HALF, sub), BF),
            pltpu.VMEM((SLOTS, HALF, sub), BF),
            pltpu.VMEM((mel, slot), BF),
            pltpu.VMEM((mel, slot), BF),
            pltpu.VMEM((clips - 1, band, WIDE), BF),
            pltpu.VMEM((d - 1, band, piece), BF),
            pltpu.VMEM((band, piece), BF),
            pltpu.VMEM((band, piece), BF),
            dma((SLOTS,)),
            dma((SLOTS,)),
            dma((18,)),
            dma((blocks,)),
            dma((blocks,)),
            dma((blocks,)),
            dma((blocks,)),
            dma((blocks,)),
            dma((blocks,)),
            dma((blocks,)),
            dma((POSTS,)),
            dma((SLOTS,)),
            dma((SLOTS,)),
            dma((11,)),
            dma((d - 1,)),
        ],
        compiler_params=pltpu.CompilerParams(
            collective_id=0, has_side_effects=True, vmem_limit_bytes=60 << 20
        ),
    )(x, cot, cond, lens, wcat)


def adamw(master, first_old, second_old, gradient, step_rate, power_one, power_two):
    first_new = BETA_ONE * first_old + (1.0 - BETA_ONE) * gradient
    second_new = BETA_TWO * second_old + (1.0 - BETA_TWO) * gradient * gradient
    first_hat = first_new / (1.0 - power_one)
    second_hat = second_new / (1.0 - power_two)
    renewed = master - step_rate * (
        first_hat / (jnp.sqrt(second_hat) + EPSILON) + WEIGHT_DECAY * master
    )
    return (renewed, first_new, second_new)


def per_device(
    n, d,
    inputs, conditioning, lengths, cotangent, conv_weight, out_weight, biases,
    conv_first, out_first, bias_first, conv_second, out_second, bias_second,
):
    clips, r, slot = inputs.shape
    taps = conv_weight.shape[0]
    bias_low = biases.astype(BF)
    flipped = jnp.transpose(conv_weight.astype(BF), (1, 2, 0))
    flipped = jnp.concatenate(
        [flipped, bias_low[0:2, :, None], jnp.zeros((2, r, KP - taps - 1), BF)], axis=2
    )
    out_low = out_weight.astype(BF).reshape(r, 2, 2, HALF)
    wcat = jnp.stack(
        [
            jnp.concatenate(
                [
                    flipped[0],
                    flipped[1],
                    out_low[:, 0, side],
                    out_low[:, 1, side],
                    bias_low[2:4].T,
                    jnp.zeros((r, WIDE - USED - 2), BF),
                ],
                axis=1,
            )
            for side in range(2)
        ],
        axis=0,
    )
    cond = jnp.transpose(conditioning, (0, 2, 1))
    layer_out, gio, gco, gw = run_layer(n, d, inputs, cotangent, cond, lengths, wcat)

    grad_input = cotangent[:, 0].astype(F32) + gio.astype(F32)
    grad_cond = jnp.transpose(gco.astype(F32), (0, 2, 1))
    gsum = gw[0].astype(F32)
    both = gsum[:, USED : USED + 2] + gw[1, :, USED : USED + 2].astype(F32)
    conv_grad = jnp.transpose(
        jnp.stack([gsum[:, :taps], gsum[:, KP : KP + taps]], axis=0), (2, 0, 1)
    )
    out_grad = jnp.stack(
        [gw[:, :, OUT_AT : OUT_AT + HALF], gw[:, :, OUT_AT + HALF : USED]], axis=0
    )
    out_grad = jnp.transpose(out_grad, (2, 0, 1, 3)).reshape(r, 4 * HALF).astype(F32)
    bias_grad = jnp.stack(
        [gsum[:, taps], gsum[:, KP + taps], both[:, 0], both[:, 1]], axis=0
    )
    power_one = jnp.float32(BETA_ONE**STEP)
    power_two = jnp.float32(BETA_TWO**STEP)
    conv_new = adamw(
        conv_weight, conv_first, conv_second, conv_grad, CONV_RATE, power_one, power_two
    )
    out_new = adamw(out_weight, out_first, out_second, out_grad, OUT_RATE, power_one, power_two)
    bias_new = adamw(biases, bias_first, bias_second, bias_grad, BIAS_RATE, power_one, power_two)
    return (
        layer_out,
        grad_input,
        grad_cond,
        conv_new[0],
        out_new[0],
        bias_new[0],
        conv_new[1],
        out_new[1],
        bias_new[1],
        conv_new[2],
        out_new[2],
        bias_new[2],
        conv_new[0].astype(BF),
        out_new[0].astype(BF),
        bias_new[0].astype(BF),
    )


def solution(mesh):
    in_specs = (
        P("dp", "mp", None),
        P("dp", "mp", None),
        P("dp"),
        P("dp", None, "mp", None),
        P(None, None, "mp"),
        P("mp", None),
        P(None, "mp"),
        P(None, None, "mp"),
        P("mp", None),
        P(None, "mp"),
        P(None, None, "mp"),
        P("mp", None),
        P(None, "mp"),
    )
    out_specs = (
        P("dp", None, "mp", None),
        P("dp", "mp", None),
        P("dp", "mp", None),
        P(None, None, "mp"),
        P("mp", None),
        P(None, "mp"),
        P(None, None, "mp"),
        P("mp", None),
        P(None, "mp"),
        P(None, None, "mp"),
        P("mp", None),
        P(None, "mp"),
        P(None, None, "mp"),
        P("mp", None),
        P(None, "mp"),
    )
    return jax.shard_map(
        functools.partial(per_device, mesh.shape["mp"], mesh.shape["dp"]),
        mesh=mesh, in_specs=in_specs, out_specs=out_specs, check_vma=False,
    )
```

```python
import functools

import jax
import jax.numpy as jnp
from jax import lax
from jax.experimental import pallas as pl
from jax.experimental.pallas import tpu as pltpu
from jax.sharding import PartitionSpec as P

RESIDUAL_WIDTH = 512
GH = 512
DILATION_STEP = 32
STEP = 4

BETA_ONE = 0.5
BETA_TWO = 0.5
EPSILON = 1e-08
WEIGHT_DECAY = 0.01
CONV_RATE = 0.03
OUT_RATE = 0.1
BIAS_RATE = 0.3

MESH = pl.DeviceIdType.MESH
LANES = 128
HALF = RESIDUAL_WIDTH // 2
KP = 1152
OUT_AT = 2 * KP
USED = OUT_AT + 2 * HALF
WIDE = 3072
AHEAD = 16
OWN = 6
DIRECT = 6
GIVE = 14
LAG = 8
SLOTS = 4
LATE = 12
POSTS = 8
BF = jnp.bfloat16
F32 = jnp.float32


def dot(a, b):
    return jnp.dot(a, b, preferred_element_type=F32)


def dot_nt(a, b):
    return lax.dot_general(a, b, (((1,), (1,)), ((), ())), preferred_element_type=F32)


def layer_kernel(
    n, d, clips, slot, sub, mel,
    x, cot, cond, lens, conv, proj, bias,
    bro, gio, gco, gw,
    convf, turn, xin, cin, cnd, grecv, gsend, gown, wall, wtr, pg, gacc, csum, ost, gfs, gk, kr, r0, r1, s2, r2,
    sem_fx, sem_fc, sem_send, sem_xh, sem_xm, sem_c, sem_k, sem_km, sem_kr, sem_gm, sem_gv, sem_o, sem_gf, sem_in, sem_r1, sem_pre,
):
    g = lax.axis_index("dp")
    m = lax.axis_index("mp")
    r = RESIDUAL_WIDTH // n
    t = slot // n
    per = t // sub
    blocks = slot // sub
    piece = WIDE // d
    half = n // 2
    band = GH // clips
    h = m // half
    first = h * half
    local = m - first
    worker = jnp.logical_and(m >= half - clips, m < half + clips)
    wc = lax.rem(m + 2 * clips * n - (half - clips), clips)
    mirror = half - clips + (1 - h) * clips + wc
    hub = jnp.logical_and(worker, wc == h)
    shared = (g + 1) * piece <= OUT_AT

    def wid(hh, c):
        return half - clips + hh * clips + c

    def lane(i, size=sub):
        return pl.ds(pl.multiple_of(i, LANES), size)

    def rows(j):
        return pl.ds(pl.multiple_of(j * r, r), r)

    def remote(src, dst, ss, rs, gg, j):
        return pltpu.make_async_remote_copy(
            src_ref=src, dst_ref=dst, send_sem=ss, recv_sem=rs,
            device_id=(gg, j), device_id_type=MESH,
        )

    def others(body):
        if half <= 4:
            for k in range(1, half):
                body(lax.rem(local + k, half))
        else:
            pl.loop(1, half)(lambda k: body(lax.rem(local + k, half)))

    def drain(ref, sem):
        pltpu.make_async_copy(ref, ref, sem).wait()

    def whole(ref, count, sem):
        drain(ref.at[0, :, pl.ds(0, count * piece)] if count <= d else ref.at[:, :, pl.ds(0, count // 2 * piece)], sem)

    projf = gacc.at[pl.ds(0, r), pl.ds(0, proj.shape[1])]
    pltpu.make_async_copy(conv, convf, sem_pre.at[0]).start()
    pltpu.make_async_copy(proj, projf, sem_pre.at[1]).start()

    bar = pltpu.get_barrier_semaphore()

    @pl.loop(1, half)
    def _(k):
        pl.semaphore_signal(bar, inc=1, device_id=(g, first + lax.rem(local + k, half)), device_id_type=MESH)

    @pl.loop(1, d)
    def _(k):
        pl.semaphore_signal(bar, inc=1, device_id=(lax.rem(g + k, d), m), device_id_type=MESH)

    @pl.when(worker)
    def _():
        for c in range(clips):
            pl.semaphore_signal(bar, inc=1, device_id=(g, wid(1 - h, c)), device_id_type=MESH)
        pl.semaphore_wait(bar, half + d - 2 + clips)

    @pl.when(jnp.logical_not(worker))
    def _():
        pl.semaphore_wait(bar, half + d - 2)

    mine = lane(g * piece, piece)

    def laid(hh):
        return gsend.at[rows(hh), pl.ds(0, WIDE)]

    def laid_piece(hh):
        return gsend.at[rows(hh), mine]
    kept = pl.ds(pl.multiple_of(wc * band, band), band)

    def send_cond(s):
        @pl.when(s // per == m)
        def _():
            dst = cnd.at[pl.ds(0, mel), lane(s * sub)]
            for c in range(clips):
                to = wid(h, c)
                part = cond.at[c, :, lane(s * sub - m * t)]

                @pl.when(to == m)
                def _():
                    pltpu.make_async_copy(part, dst, sem_k.at[s]).start()

                @pl.when(to != m)
                def _():
                    remote(part, dst, sem_send.at[0], sem_k.at[s], g, to).start()

    def later(s):
        return lane(lax.rem(s, blocks // 2) * sub)

    def in_half(s):
        return s // (blocks // 2) == h

    def weights():
        taps = convf.shape[2]
        drain(convf, sem_pre.at[0])
        drain(projf, sem_pre.at[1])
        wide = projf[...]
        turn[...] = jnp.zeros_like(turn)
        turn[0:4, 0:r] = bias[...]
        column = turn[...].T
        spot = lax.broadcasted_iota(jnp.int32, (r, LANES), 1)
        for hh in range(2):
            form = laid(hh)
            for q in range(2):
                base = q * KP
                form[:, base:base + 1024] = convf[q, :, 0:1024].astype(BF)
                form[:, base + 1024:base + KP] = jnp.where(
                    spot == taps - 1024, column[0:r, q:q + 1], 0.0).astype(BF)
                form[:, base + 1024:base + taps] = convf[q, :, 1024:taps].astype(BF)
                form[:, OUT_AT + q * HALF:OUT_AT + (q + 1) * HALF] = wide[
                    :, (2 * q + hh) * HALF:(2 * q + hh + 1) * HALF].astype(BF)
            form[:, USED:USED + LANES] = jnp.where(
                spot == 0, column[0:r, 2:3], jnp.where(spot == 1, column[0:r, 3:4], 0.0)).astype(BF)
            form[:, USED + LANES:] = jnp.zeros((r, WIDE - USED - LANES), BF)

        @pl.when(hub)
        def _():
            pltpu.make_async_copy(laid_piece(h), wall.at[rows(m), mine], sem_in.at[0]).start()
            pltpu.make_async_copy(laid_piece(1 - h), s2.at[rows(local), :], sem_in.at[3]).start()

        @pl.when(jnp.logical_not(hub))
        def _():
            remote(laid_piece(h), wall.at[rows(m), mine], sem_send.at[1], sem_in.at[0], g, wid(h, h)).start()
            remote(laid_piece(1 - h), s2.at[rows(local), :], sem_send.at[1], sem_in.at[3], g, wid(h, h)).start()

    def far():
        def send_x(s):
            at = s * sub

            @pl.when(s >= SLOTS)
            def _():
                drain(x.at[:, :, pl.ds(0, sub)], sem_fx.at[lax.rem(s, SLOTS)])

            for c in range(clips):
                remote(x.at[c, :, lane(at)], xin.at[rows(m), lane(at + LANES)],
                       sem_fx.at[lax.rem(s, SLOTS)], sem_xh.at[s], g, wid(h, c)).start()
            send_cond(s)

        def send_cot(s):
            at = s * sub

            @pl.when(s >= SLOTS)
            def _():
                drain(cot.at[:, :, :, pl.ds(0, sub)], sem_fc.at[lax.rem(s, SLOTS)])

            for c in range(clips):
                remote(cot.at[c, :, :, lane(at)], cin.at[:, rows(local), lane(at)],
                       sem_fc.at[lax.rem(s, SLOTS)], sem_c.at[s], g, wid(h, c)).start()

        pl.loop(0, 2)(send_x)
        weights()
        pl.loop(2, AHEAD)(send_x)

        @pl.loop(0, blocks)
        def _(s):
            @pl.when(s + AHEAD < blocks)
            def _():
                send_x(s + AHEAD)

            send_cot(s)

        @pl.loop(0, SLOTS)
        def _(q):
            drain(x.at[:, :, pl.ds(0, sub)], sem_fx.at[q])
            drain(cot.at[:, :, :, pl.ds(0, sub)], sem_fc.at[q])

    def work():
        def own(s):
            at = s * sub
            for k in range(1, clips):
                c = lax.rem(wc + k, clips)
                remote(x.at[c, :, lane(at)], xin.at[rows(m), lane(at + LANES)],
                       sem_send.at[3], sem_xh.at[s], g, wid(h, c)).start()
                remote(cot.at[c, :, :, lane(at)], cin.at[:, rows(local), lane(at)],
                       sem_send.at[4], sem_c.at[s], g, wid(h, c)).start()
            pltpu.make_async_copy(x.at[wc, :, lane(at)], xin.at[rows(m), lane(at + LANES)], sem_xh.at[s]).start()
            pltpu.make_async_copy(cot.at[wc, :, :, lane(at)], cin.at[:, rows(local), lane(at)], sem_c.at[s]).start()
            send_cond(s)

        here = pl.ds(pl.multiple_of(h * HALF, HALF), HALF)
        there = pl.ds(pl.multiple_of((1 - h) * HALF, HALF), HALF)

        def direct(s):
            at = s * sub
            for k in range(clips):
                c = lax.rem(wc + k, clips)
                remote(x.at[c, :, lane(at)], xin.at[rows(m), lane(at + LANES)],
                       sem_send.at[17], sem_xm.at[s], g, wid(1 - h, c)).start()

        far_rows = pl.ds(pl.multiple_of(h * (HALF + clips * r), r), HALF - clips * r)

        def relay(s):
            part = xin.at[far_rows, lane(s * sub + LANES)]
            drain(xin.at[here, lane(s * sub + LANES)], sem_xh.at[s])
            remote(part, part, sem_send.at[5], sem_xm.at[s], g, mirror).start()

            @pl.when(s + DIRECT < blocks)
            def _():
                direct(s + DIRECT)

            @pl.when(in_half(s))
            def _():
                also = cnd.at[pl.ds(0, mel), lane(s * sub)]
                drain(also, sem_k.at[s])
                remote(also, also, sem_send.at[12], sem_km.at[s], g, mirror).start()

        pl.loop(0, DIRECT)(direct)
        weights()
        pl.loop(0, AHEAD + OWN)(own)

        xin[:, 0:LANES] = jnp.zeros((RESIDUAL_WIDTH, LANES), BF)
        pg[...] = jnp.zeros_like(pg)
        cnd[mel:LANES, :] = (
            lax.broadcasted_iota(jnp.int32, (LANES - mel, slot), 0) == 0
        ).astype(F32).astype(BF)
        gacc[...] = jnp.zeros_like(gacc)
        csum[...] = jnp.zeros_like(csum)

        pl.loop(0, 2)(relay)
        drain(wall.at[kept, mine], sem_in.at[0])

        @pl.when(hub)
        def _():
            drain(s2, sem_in.at[3])
            remote(s2, wall.at[kept, mine], sem_send.at[2], sem_in.at[0], g, mirror).start()

        @pl.loop(1, d)
        def _(k):
            remote(wall.at[kept, mine], wall.at[kept, mine], sem_send.at[6], sem_in.at[1],
                   lax.rem(g + k, d), m).start()

        pl.loop(2, 9)(relay)
        drain(wall.at[kept, pl.ds(0, (d - 1) * piece)], sem_in.at[1])
        for k in range(1, clips):
            remote(wall.at[kept, :], wall.at[kept, :], sem_send.at[7], sem_in.at[2], g,
                   wid(h, lax.rem(wc + k, clips))).start()
        pl.loop(9, AHEAD)(relay)
        drain(wall.at[pl.ds(0, GH - band), :], sem_in.at[2])

        @pl.when(hub)
        def _():
            drain(s2, sem_send.at[2])

        @pl.when(jnp.logical_not(hub))
        def _():
            drain(gsend.at[pl.ds(0, 2 * r), mine], sem_send.at[1])


        @pl.loop(0, USED // LANES)
        def _(i):
            wtr[pl.ds(pl.multiple_of(i * LANES, LANES), LANES), :] = wall[:, lane(i * LANES, LANES)].T

        length = lens[wc]

        def back(top):
            win = pg[...]
            pn = win[:, :sub]
            pe = pltpu.roll(win, sub + LANES - DILATION_STEP, 1)[:, :sub]

            def tap(base):
                return wtr[pl.ds(pl.multiple_of(base + top, HALF), HALF), :]

            return (dot(tap(512), pn[0:512]) + dot(wtr[pl.ds(pl.multiple_of(KP + 512 + top, LANES), HALF), :], pn[512:1024])
                    + dot(tap(0), pe[0:512]) + dot(wtr[pl.ds(pl.multiple_of(KP + top, LANES), HALF), :], pe[512:1024]))

        def gone(q):
            drain(gsend.at[:, pl.ds(0, sub)], sem_gv.at[lax.rem(q, POSTS)])

        def give(q):
            remote(gsend.at[:, lane((q + 1) * sub)], grecv.at[:, lane(q * sub)],
                   sem_gv.at[lax.rem(q, POSTS)], sem_gm.at[q], g, mirror).start()

        def add_cond(s):
            now = lane(s * sub)
            keeper = s // per
            spot = gco.at[wc, :, lane(s * sub - keeper * t)]
            drain(kr.at[:, later(s)], sem_kr.at[s])
            gk[:, now] = (gk[:, now].astype(F32) + kr[:, later(s)].astype(F32)).astype(BF)

            @pl.when(keeper == m)
            def _():
                pltpu.make_async_copy(gk.at[:, now], spot, sem_send.at[13]).start()

            @pl.when(keeper != m)
            def _():
                remote(gk.at[:, now], spot, sem_send.at[14], sem_in.at[6], g, keeper).start()

        def combine(q):
            now = lane(q * sub)
            z = lax.rem(q, SLOTS)
            drain(grecv.at[:, now], sem_gm.at[q])

            @pl.when(q >= SLOTS)
            def _():
                drain(gfs.at[z], sem_gf.at[z])

            gfs[z] = (gown[:, lane((q + 1) * sub)].astype(F32) + grecv[:, now].astype(F32)).astype(BF)

            @others
            def _(i):
                remote(gfs.at[z, rows(i), :], gio.at[wc, :, now], sem_gf.at[z], sem_in.at[5], g, first + i).start()

            pltpu.make_async_copy(gfs.at[z, rows(local), :], gio.at[wc, :, now], sem_gf.at[z]).start()

        def send_results(s):
            now = lane(s * sub)
            z = lax.rem(s, SLOTS)

            @others
            def _(i):
                remote(ost.at[z, :, rows(i), :], bro.at[wc, :, :, now], sem_o.at[z], sem_in.at[10], g, first + i).start()

            pltpu.make_async_copy(ost.at[z, :, rows(local), :], bro.at[wc, :, :, now], sem_o.at[z]).start()

            @pl.when(jnp.logical_not(in_half(s)))
            def _():
                remote(gk.at[:, now], kr.at[:, later(s)], sem_send.at[8], sem_kr.at[s], g, mirror).start()

        @pl.loop(0, blocks)
        def _(s):
            at = s * sub
            now = lane(at)
            off = lane(at + LANES)
            z = lax.rem(s, SLOTS)

            @pl.when(s + AHEAD + OWN < blocks)
            def _():
                own(s + AHEAD + OWN)

            @pl.when(s + AHEAD < blocks)
            def _():
                relay(s + AHEAD)

            @pl.when(s >= 1)
            def _():
                send_results(s - 1)

            @pl.when(s >= GIVE + POSTS)
            def _():
                gone(s - GIVE - POSTS)

            @pl.when(s >= GIVE)
            def _():
                give(s - GIVE)

            @pl.when(s >= GIVE + LAG)
            def _():
                combine(s - GIVE - LAG)

            @pl.when(jnp.logical_and(s >= LATE, in_half(s - LATE)))
            def _():
                add_cond(s - LATE)

            @pl.when(jnp.logical_not(in_half(s)))
            def _():
                drain(cnd.at[pl.ds(0, mel), now], sem_km.at[s])

            @pl.when(s >= SLOTS)
            def _():
                drain(ost.at[z], sem_o.at[z])

            drain(xin.at[there, off], sem_xm.at[s])
            drain(cin.at[:, :, now], sem_c.at[s])

            xc = xin[:, off]
            xe = pltpu.roll(xin[:, lane(at, sub + LANES)], DILATION_STEP, 1)[:, LANES:]
            cd = cnd[:, now]
            pre_f = (dot(wall[:, 0:512], xe) + dot(wall[:, 512:1024], xc) + dot(wall[:, 1024:KP], cd))
            pre_g = (dot(wall[:, KP:KP + 512], xe) + dot(wall[:, KP + 512:KP + 1024], xc)
                     + dot(wall[:, KP + 1024:OUT_AT], cd))
            place = at + lax.broadcasted_iota(jnp.int32, (1, sub), 1)
            keep = (place < length).astype(F32)
            th = jnp.tanh(pre_f)
            sg = jax.nn.sigmoid(pre_g)
            hid = (keep * th * sg).astype(BF)
            branch = dot(wtr[OUT_AT:USED, :], hid)
            offset = wall[here, USED:USED + LANES].astype(F32)
            ost[z, 0] = (xin[here, off].astype(F32) + branch[0:HALF] + offset[:, 0:1]).astype(BF)
            ost[z, 1] = (branch[HALF:] + offset[:, 1:2]).astype(BF)
            ct = cin[:, :, now].reshape(2 * HALF, sub)
            for q in range(sub // LANES):
                csum[...] += ct[:, q * LANES:(q + 1) * LANES].astype(F32)
            hg = dot(wall[:, OUT_AT:USED], ct) * keep
            pgf = (hg * sg * (1.0 - th * th)).astype(BF)
            pgg = (hg * th * sg * (1.0 - sg)).astype(BF)
            pg[0:512, sub:] = pgf[:, :LANES]
            pg[512:1024, sub:] = pgg[:, :LANES]
            gacc[:, 0:512] += dot_nt(pgf, xe)
            gacc[:, 512:1024] += dot_nt(pgf, xc)
            gacc[:, 1024:KP] += dot_nt(pgf, cd)
            gacc[:, KP:KP + 512] += dot_nt(pgg, xe)
            gacc[:, KP + 512:KP + 1024] += dot_nt(pgg, xc)
            gacc[:, KP + 1024:OUT_AT] += dot_nt(pgg, cd)
            gacc[:, OUT_AT:USED] += dot_nt(hid, ct)
            gk[:, now] = (dot(wtr[1024:KP, :], pgf) + dot(wtr[KP + 1024:OUT_AT, :], pgg))[0:mel].astype(BF)
            gsend[:, now] = back((1 - h) * HALF).astype(BF)
            gown[:, now] = back(h * HALF).astype(BF)
            pg[0:512, 0:sub] = pgf
            pg[512:1024, 0:sub] = pgg

        send_results(blocks - 1)
        pg[:, sub:] = jnp.zeros((2 * GH, LANES), BF)
        gsend[:, pl.ds(slot, sub)] = back((1 - h) * HALF).astype(BF)
        gown[:, pl.ds(slot, sub)] = back(h * HALF).astype(BF)

        def spread(part, dst, sem):
            @others
            def _(i):
                remote(part.at[rows(i), :], dst, sem, sem_in.at[8], g, first + i).start()

            pltpu.make_async_copy(part.at[rows(local), :], dst, sem_in.at[8]).start()

        spot = lax.broadcasted_iota(jnp.int32, (HALF, LANES), 1)
        total = jnp.sum(csum[...], axis=1, keepdims=True)
        gacc[here, USED:USED + LANES] = jnp.where(spot == 0, total[0:HALF], jnp.where(spot == 1, total[HALF:], 0.0))

        s0 = cin.at[0, :, pl.ds(0, WIDE)]
        for k in range(1, clips):
            to = lax.rem(wc + k, clips)
            s0[...] = gacc[pl.ds(pl.multiple_of(to * band, band), band), :].astype(BF)
            remote(s0, r0.at[k - 1], sem_send.at[9], sem_in.at[7], g, wid(h, to)).start()

        start = blocks - GIVE
        pl.loop(start - POSTS, start - SLOTS)(gone)

        def tail(q):
            gone(q - SLOTS)
            give(q)
            combine(q - LAG)
            more = q + GIVE - LATE

            @pl.when(jnp.logical_and(more < blocks, in_half(more)))
            def _():
                add_cond(more)

        pl.loop(start, start + 2)(tail)
        drain(r0, sem_in.at[7])
        for k in range(1, clips):
            gacc[kept, :] += r0[k - 1].astype(F32)

        @pl.loop(1, d)
        def _(k):
            to = lax.rem(g + k, d)
            src = cin.at[1, :, lane((k - 1) * piece, piece)]
            src[...] = gacc[kept, lane(to * piece, piece)].astype(BF)
            remote(src, r1.at[k - 1], sem_send.at[10], sem_r1.at[k - 1], to, m).start()

        pl.loop(start + 2, start + 7)(tail)

        @pl.loop(1, d)
        def _(k):
            drain(r1.at[k - 1], sem_r1.at[k - 1])
            gacc[kept, mine] += r1[k - 1].astype(F32)

        s2[...] = gacc[kept, mine].astype(BF)

        @pl.when(jnp.logical_not(hub))
        def _():
            remote(s2, r2, sem_send.at[11], sem_in.at[4], g, mirror).start()

        pl.loop(start + 7, start + 13)(tail)

        @pl.when(hub)
        def _():
            drain(r2, sem_in.at[4])

            @pl.when(shared)
            def _():
                s2[...] = (gacc[kept, mine] + r2[...].astype(F32)).astype(BF)
                spread(s2, gw.at[0, :, mine], sem_send.at[11])

            @pl.when(jnp.logical_not(shared))
            def _():
                spread(s2, gw.at[h, :, mine], sem_send.at[11])
                spread(r2, gw.at[1 - h, :, mine], sem_send.at[15])

        pl.loop(start + 13, blocks)(tail)
        share_out()
        pl.loop(blocks - SLOTS, blocks)(gone)
        pl.loop(blocks - LAG, blocks)(combine)

        @pl.loop(0, SLOTS)
        def _(q):
            drain(ost.at[q], sem_o.at[q])
            drain(gfs.at[q], sem_gf.at[q])

        drain(x.at[pl.ds(0, clips - 1)], sem_send.at[3])
        drain(cot.at[pl.ds(0, clips - 1)], sem_send.at[4])
        drain(xin.at[pl.ds(0, HALF - clips * r), pl.ds(0, slot)], sem_send.at[5])
        drain(x, sem_send.at[17])
        drain(wall.at[kept, pl.ds(0, (d - 1) * piece)], sem_send.at[6])
        drain(wall.at[pl.ds(0, GH - band), :], sem_send.at[7])
        drain(gk.at[:, pl.ds(0, slot // 2)], sem_send.at[8])
        drain(cnd.at[pl.ds(0, mel), pl.ds(0, slot // 2)], sem_send.at[12])
        drain(gk.at[:, pl.ds(0, t)], sem_send.at[13])
        drain(gk.at[:, pl.ds(0, slot // 2 - t)], sem_send.at[14])
        drain(r0, sem_send.at[9])
        drain(r1, sem_send.at[10])

    def share_out():
        @pl.when(shared)
        def _():
            drain(gw.at[0, :, mine], sem_in.at[8])
            share(gw.at[0, :, mine])

        @pl.when(jnp.logical_not(shared))
        def _():
            drain(gw.at[:, :, mine], sem_in.at[8])
            share(gw.at[:, :, mine])

    def share(part):
        @pl.loop(1, d)
        def _(k):
            remote(part, part, sem_send.at[16], sem_in.at[9], lax.rem(g + k, d), m).start()

    @pl.when(worker)
    def _():
        work()
        drain(cond.at[pl.ds(0, clips - 1)], sem_send.at[0])
        drain(bro.at[pl.ds(0, clips - 1)], sem_in.at[10])
        drain(gio.at[pl.ds(0, clips - 1)], sem_in.at[5])
        drain(gco.at[pl.ds(0, clips - 1)], sem_in.at[6])

        @pl.when(hub)
        def _():
            drain(s2.at[pl.ds(0, HALF - r), :], sem_send.at[11])

            @pl.when(jnp.logical_not(shared))
            def _():
                drain(r2.at[pl.ds(0, HALF - r), :], sem_send.at[15])

        @pl.when(jnp.logical_not(hub))
        def _():
            drain(s2, sem_send.at[11])

    @pl.when(jnp.logical_not(worker))
    def _():
        far()
        share_out()
        drain(cond, sem_send.at[0])
        drain(gsend.at[pl.ds(0, 2 * r), mine], sem_send.at[1])
        drain(bro, sem_in.at[10])
        drain(gio, sem_in.at[5])
        drain(gco, sem_in.at[6])

    own_piece = 2 * d - OUT_AT // piece

    @pl.when(shared)
    def _():
        whole(gw, own_piece - 1, sem_in.at[9])
        whole(gw, d - 1, sem_send.at[16])

    @pl.when(jnp.logical_not(shared))
    def _():
        whole(gw, own_piece - 2, sem_in.at[9])
        whole(gw, 2 * (d - 1), sem_send.at[16])


def run_layer(n, d, x, cot, cond, lens, conv, proj, bias):
    clips, r, slot = x.shape
    mel = cond.shape[1]
    t = slot // n
    sub = min(256, t)
    blocks = slot // sub
    piece = WIDE // d
    width = RESIDUAL_WIDTH
    band = GH // clips
    any_spec = pl.BlockSpec(memory_space=pltpu.HBM)
    vmem = pl.BlockSpec(memory_space=pltpu.VMEM)
    smem = pl.BlockSpec(memory_space=pltpu.SMEM)
    dma = pltpu.SemaphoreType.DMA
    return pl.pallas_call(
        functools.partial(layer_kernel, n, d, clips, slot, sub, mel),
        out_shape=(
            jax.ShapeDtypeStruct((clips, 2, r, slot), BF),
            jax.ShapeDtypeStruct((clips, r, slot), BF),
            jax.ShapeDtypeStruct((clips, mel, t), BF),
            jax.ShapeDtypeStruct((2, r, WIDE), BF),
        ),
        in_specs=[any_spec, any_spec, any_spec, smem, any_spec, any_spec, vmem],
        out_specs=(any_spec, any_spec, any_spec, vmem),
        scratch_shapes=[
            pltpu.VMEM(conv.shape, F32),
            pltpu.VMEM((8, LANES), F32),
            pltpu.VMEM((width, LANES + slot), BF),
            pltpu.VMEM((2, HALF, slot), BF),
            pltpu.VMEM((LANES, slot), BF),
            pltpu.VMEM((HALF, slot), BF),
            pltpu.VMEM((HALF, slot + sub), BF),
            pltpu.VMEM((HALF, slot + sub), BF),
            pltpu.VMEM((GH, WIDE), BF),
            pltpu.VMEM((USED, GH), BF),
            pltpu.VMEM((2 * GH, sub + LANES), BF),
            pltpu.VMEM((GH, WIDE), F32),
            pltpu.VMEM((2 * HALF, LANES), F32),
            pltpu.VMEM((SLOTS, 2, HALF, sub), BF),
            pltpu.VMEM((SLOTS, HALF, sub), BF),
            pltpu.VMEM((mel, slot), BF),
            pltpu.VMEM((mel, slot // 2), BF),
            pltpu.VMEM((clips - 1, band, WIDE), BF),
            pltpu.VMEM((d - 1, band, piece), BF),
            pltpu.VMEM((band, piece), BF),
            pltpu.VMEM((band, piece), BF),
            dma((SLOTS,)),
            dma((SLOTS,)),
            dma((18,)),
            dma((blocks,)),
            dma((blocks,)),
            dma((blocks,)),
            dma((blocks,)),
            dma((blocks,)),
            dma((blocks,)),
            dma((blocks,)),
            dma((POSTS,)),
            dma((SLOTS,)),
            dma((SLOTS,)),
            dma((11,)),
            dma((d - 1,)),
            dma((2,)),
        ],
        compiler_params=pltpu.CompilerParams(
            collective_id=0, has_side_effects=True, vmem_limit_bytes=60 << 20
        ),
    )(x, cot, cond, lens, conv, proj, bias)


def adamw(master, first_old, second_old, gradient, step_rate, power_one, power_two):
    first_new = BETA_ONE * first_old + (1.0 - BETA_ONE) * gradient
    second_new = BETA_TWO * second_old + (1.0 - BETA_TWO) * gradient * gradient
    first_hat = first_new / (1.0 - power_one)
    second_hat = second_new / (1.0 - power_two)
    renewed = master - step_rate * (
        first_hat / (jnp.sqrt(second_hat) + EPSILON) + WEIGHT_DECAY * master
    )
    return (renewed, first_new, second_new)


def finish_kernel(
    taps, span,
    lo, gio, cot, gco, gw, cw, cm, cv, ow, om, ov, bw, bm, bv,
    lo_out, gi_out, gc_out, cw_out, ow_out, bw_out, cm_out, om_out, bm_out, cv_out, ov_out, bv_out,
    cl_out, ol_out, bl_out,
    lo_v, gio_v, cot_v, gi_v, gco_v, gc_v, gw_v, conv_v, convl_v, proj_v, projl_v,
    sem_lo, sem_gi, sem_cot, sem_small, sem_out,
):
    clips, r, slot = gio.shape
    parts = slot // span
    power_one = jnp.float32(BETA_ONE**STEP)
    power_two = jnp.float32(BETA_TWO**STEP)

    small = [
        pltpu.make_async_copy(src, dst, sem_small.at[i])
        for i, (src, dst) in enumerate(
            [(gw, gw_v), (gco, gco_v)]
            + [(a, conv_v.at[q]) for q, a in enumerate((cw, cm, cv))]
            + [(a, proj_v.at[q]) for q, a in enumerate((ow, om, ov))]
        )
    ]
    blocks = [(c, slice(p * span, (p + 1) * span)) for c in range(clips) for p in range(parts)]
    loads = [
        (
            pltpu.make_async_copy(gio.at[c, :, at], gio_v.at[c, :, at], sem_gi.at[i]),
            pltpu.make_async_copy(cot.at[c, 0, :, at], cot_v.at[c, :, at], sem_cot.at[i]),
            pltpu.make_async_copy(lo.at[c, :, :, at], lo_v.at[c, :, :, at], sem_lo.at[i]),
        )
        for i, (c, at) in enumerate(blocks)
    ]
    for copy in small[:5]:
        copy.start()
    for load in loads[:2]:
        for copy in load:
            copy.start()
    for copy in small[5:]:
        copy.start()
    for load in loads[2:]:
        for copy in load:
            copy.start()

    stores = []

    def store(src, dst):
        copy = pltpu.make_async_copy(src, dst, sem_out.at[len(stores)])
        copy.start()
        stores.append(copy)

    def block(i):
        c, at = blocks[i]
        one, two, three = loads[i]
        three.wait()
        store(lo_v.at[c, :, :, at], lo_out.at[c, :, :, at])
        one.wait()
        two.wait()
        gi_v[c, :, at] = cot_v[c, :, at].astype(F32) + gio_v[c, :, at].astype(F32)
        store(gi_v.at[c, :, at], gi_out.at[c, :, at])

    block(0)
    for copy in small[:5]:
        copy.wait()
    gc_v[...] = gco_v[...].astype(F32)
    store(gc_v, gc_out)
    for q in range(2):
        w, m, v = adamw(conv_v[0, q], conv_v[1, q], conv_v[2, q], gw_v[0, :, q * KP:q * KP + taps].astype(F32),
                        CONV_RATE, power_one, power_two)
        conv_v[0, q], conv_v[1, q], conv_v[2, q] = w, m, v
        convl_v[q] = w.astype(BF)
    for i, dst in enumerate((cw_out, cm_out, cv_out)):
        store(conv_v.at[i], dst)
    store(convl_v, cl_out)
    block(1)
    for copy in small[5:]:
        copy.wait()
    for q in range(4):
        at = slice(q * HALF, (q + 1) * HALF)
        from_at = OUT_AT + q // 2 * HALF
        w, m, v = adamw(proj_v[0, :, at], proj_v[1, :, at], proj_v[2, :, at],
                        gw_v[q % 2, :, from_at:from_at + HALF].astype(F32), OUT_RATE, power_one, power_two)
        proj_v[0, :, at], proj_v[1, :, at], proj_v[2, :, at] = w, m, v
        projl_v[:, at] = w.astype(BF)
    for i, dst in enumerate((ow_out, om_out, ov_out)):
        store(proj_v.at[i], dst)
    store(projl_v, ol_out)
    spot = lax.broadcasted_iota(jnp.int32, (r, LANES), 1)
    last = taps - 1024
    sums = gw_v[0, :, USED:USED + LANES].astype(F32) + gw_v[1, :, USED:USED + LANES].astype(F32)
    columns = (
        gw_v[0, :, 1024:KP].astype(F32)[:, last:last + 1],
        gw_v[0, :, KP + 1024:OUT_AT].astype(F32)[:, last:last + 1],
        sums[:, 0:1],
        sums[:, 1:2],
    )
    table = jnp.zeros((r, LANES), F32)
    for i, column in enumerate(columns):
        table = jnp.where(spot == i, column, table)
    w, m, v = adamw(bw[...], bm[...], bv[...], table.T[0:4], BIAS_RATE, power_one, power_two)
    bw_out[...], bm_out[...], bv_out[...] = w, m, v
    bl_out[...] = w.astype(BF)
    for i in range(2, len(blocks)):
        block(i)
    for copy in stores:
        copy.wait()


def finish(lo, gio, cot, gco, gw, conv, proj, bias):
    clips, r, slot = gio.shape
    taps = conv[0].shape[2]
    span = 2048
    count = clips * (slot // span)
    any_spec = pl.BlockSpec(memory_space=pltpu.HBM)
    vmem = pl.BlockSpec(memory_space=pltpu.VMEM)
    dma = pltpu.SemaphoreType.DMA

    def like(a, dtype=None):
        return jax.ShapeDtypeStruct(a.shape, dtype or a.dtype)

    trio = [like(conv[0]), like(proj[0]), like(bias[0])]
    return pl.pallas_call(
        functools.partial(finish_kernel, taps, span),
        out_shape=[like(lo), like(gio, F32), like(gco, F32)] + trio * 3
        + [like(a, BF) for a in (conv[0], proj[0], bias[0])],
        in_specs=[any_spec] * 11 + [vmem] * 3,
        out_specs=[any_spec] * 3 + [any_spec, any_spec, vmem] * 4,
        scratch_shapes=[
            pltpu.VMEM(lo.shape, BF),
            pltpu.VMEM(gio.shape, BF),
            pltpu.VMEM(gio.shape, BF),
            pltpu.VMEM(gio.shape, F32),
            pltpu.VMEM(gco.shape, BF),
            pltpu.VMEM(gco.shape, F32),
            pltpu.VMEM(gw.shape, BF),
            pltpu.VMEM((3, *conv[0].shape), F32),
            pltpu.VMEM(conv[0].shape, BF),
            pltpu.VMEM((3, *proj[0].shape), F32),
            pltpu.VMEM(proj[0].shape, BF),
            dma((count,)),
            dma((count,)),
            dma((count,)),
            dma((8,)),
            dma((2 * count + 9,)),
        ],
        compiler_params=pltpu.CompilerParams(vmem_limit_bytes=24 << 20),
    )(lo, gio, cot, gco, gw, *conv, *proj, *bias)


def per_device(
    n, d,
    inputs, conditioning, lengths, cotangent, conv_weight, out_weight, biases,
    conv_first, out_first, bias_first, conv_second, out_second, bias_second,
):
    conv = [jnp.transpose(a, (1, 2, 0)) for a in (conv_weight, conv_first, conv_second)]
    proj = [out_weight, out_first, out_second]
    bias = [biases, bias_first, bias_second]
    cond = jnp.transpose(conditioning, (0, 2, 1))
    lo, gio, gco, gw = run_layer(n, d, inputs, cotangent, cond, lengths, conv[0], proj[0], bias[0])
    outs = finish(lo, gio, cotangent, gco, gw, conv, proj, bias)
    layer_out, grad_input, grad_cond = outs[:3]
    news = [jnp.transpose(a, (2, 0, 1)) if i % 3 == 0 else a for i, a in enumerate(outs[3:])]
    return (layer_out, grad_input, jnp.transpose(grad_cond, (0, 2, 1)), *news)


def solution(mesh):
    in_specs = (
        P("dp", "mp", None),
        P("dp", "mp", None),
        P("dp"),
        P("dp", None, "mp", None),
        P(None, None, "mp"),
        P("mp", None),
        P(None, "mp"),
        P(None, None, "mp"),
        P("mp", None),
        P(None, "mp"),
        P(None, None, "mp"),
        P("mp", None),
        P(None, "mp"),
    )
    out_specs = (
        P("dp", None, "mp", None),
        P("dp", "mp", None),
        P("dp", "mp", None),
        P(None, None, "mp"),
        P("mp", None),
        P(None, "mp"),
        P(None, None, "mp"),
        P("mp", None),
        P(None, "mp"),
        P(None, None, "mp"),
        P("mp", None),
        P(None, "mp"),
        P(None, None, "mp"),
        P("mp", None),
        P(None, "mp"),
    )
    return jax.shard_map(
        functools.partial(per_device, mesh.shape["mp"], mesh.shape["dp"]),
        mesh=mesh, in_specs=in_specs, out_specs=out_specs, check_vma=False,
    )
```

```python
import functools

import jax
import jax.numpy as jnp
from jax import lax
from jax.experimental import pallas as pl
from jax.experimental.pallas import tpu as pltpu
from jax.sharding import PartitionSpec as P

RESIDUAL_WIDTH = 512
GH = 512
DILATION_STEP = 32
STEP = 4

BETA_ONE = 0.5
BETA_TWO = 0.5
EPSILON = 1e-08
WEIGHT_DECAY = 0.01
CONV_RATE = 0.03
OUT_RATE = 0.1
BIAS_RATE = 0.3

MESH = pl.DeviceIdType.MESH
LANES = 128
HALF = RESIDUAL_WIDTH // 2
KP = 1152
OUT_AT = 2 * KP
USED = OUT_AT + 2 * HALF
WIDE = 3072
AHEAD = 16
OWN = 6
DIRECT = 6
GIVE = 14
LAG = 8
SLOTS = 4
LATE = 12
POSTS = 8
BF = jnp.bfloat16
F32 = jnp.float32


def dot(a, b):
    return jnp.dot(a, b, preferred_element_type=F32)


def dot_nt(a, b):
    return lax.dot_general(a, b, (((1,), (1,)), ((), ())), preferred_element_type=F32)


def layer_kernel(
    n, d, clips, slot, sub, mel,
    x, cot, cond, lens, conv, proj, bias,
    bro, gio, gco, gw,
    convf, turn, xin, cin, cnd, grecv, gsend, gown, wall, wtr, pg, gacc, csum, ost, gfs, gk, kr, r0, r1, s2, r2,
    sem_fx, sem_fc, sem_send, sem_xh, sem_xm, sem_c, sem_k, sem_km, sem_kr, sem_gm, sem_gv, sem_o, sem_gf, sem_in, sem_r1, sem_pre,
):
    g = lax.axis_index("dp")
    m = lax.axis_index("mp")
    r = RESIDUAL_WIDTH // n
    t = slot // n
    per = t // sub
    blocks = slot // sub
    piece = WIDE // d
    half = n // 2
    band = GH // clips
    h = m // half
    first = h * half
    local = m - first
    worker = jnp.logical_and(m >= half - clips, m < half + clips)
    wc = lax.rem(m + 2 * clips * n - (half - clips), clips)
    mirror = half - clips + (1 - h) * clips + wc
    hub = jnp.logical_and(worker, wc == h)
    shared = (g + 1) * piece <= OUT_AT

    def wid(hh, c):
        return half - clips + hh * clips + c

    def lane(i, size=sub):
        return pl.ds(pl.multiple_of(i, LANES), size)

    def rows(j):
        return pl.ds(pl.multiple_of(j * r, r), r)

    def remote(src, dst, ss, rs, gg, j):
        return pltpu.make_async_remote_copy(
            src_ref=src, dst_ref=dst, send_sem=ss, recv_sem=rs,
            device_id=(gg, j), device_id_type=MESH,
        )

    def others(body):
        if half <= 4:
            for k in range(1, half):
                body(lax.rem(local + k, half))
        else:
            pl.loop(1, half)(lambda k: body(lax.rem(local + k, half)))

    def drain(ref, sem):
        pltpu.make_async_copy(ref, ref, sem).wait()

    def whole(ref, count, sem):
        drain(ref.at[0, :, pl.ds(0, count * piece)] if count <= d else ref.at[:, :, pl.ds(0, count // 2 * piece)], sem)

    projf = gacc.at[pl.ds(0, r), pl.ds(0, proj.shape[1])]
    pltpu.make_async_copy(conv, convf, sem_pre.at[0]).start()
    pltpu.make_async_copy(proj, projf, sem_pre.at[1]).start()

    bar = pltpu.get_barrier_semaphore()

    @pl.loop(1, half)
    def _(k):
        pl.semaphore_signal(bar, inc=1, device_id=(g, first + lax.rem(local + k, half)), device_id_type=MESH)

    @pl.loop(1, d)
    def _(k):
        pl.semaphore_signal(bar, inc=1, device_id=(lax.rem(g + k, d), m), device_id_type=MESH)

    @pl.when(worker)
    def _():
        for c in range(clips):
            pl.semaphore_signal(bar, inc=1, device_id=(g, wid(1 - h, c)), device_id_type=MESH)
        pl.semaphore_wait(bar, half + d - 2 + clips)

    @pl.when(jnp.logical_not(worker))
    def _():
        pl.semaphore_wait(bar, half + d - 2)

    mine = lane(g * piece, piece)

    def laid(hh):
        return gsend.at[rows(hh), pl.ds(0, WIDE)]

    def laid_piece(hh):
        return gsend.at[rows(hh), mine]
    kept = pl.ds(pl.multiple_of(wc * band, band), band)

    def send_cond(s):
        @pl.when(s // per == m)
        def _():
            dst = cnd.at[pl.ds(0, mel), lane(s * sub)]
            for c in range(clips):
                to = wid(h, c)
                part = cond.at[c, :, lane(s * sub - m * t)]

                @pl.when(to == m)
                def _():
                    pltpu.make_async_copy(part, dst, sem_k.at[s]).start()

                @pl.when(to != m)
                def _():
                    remote(part, dst, sem_send.at[0], sem_k.at[s], g, to).start()

    def later(s):
        return lane(lax.rem(s, blocks // 2) * sub)

    def in_half(s):
        return s // (blocks // 2) == h

    def weights():
        taps = convf.shape[2]
        drain(convf, sem_pre.at[0])
        drain(projf, sem_pre.at[1])
        wide = projf[...]
        turn[...] = jnp.zeros_like(turn)
        turn[0:4, 0:r] = bias[...]
        column = turn[...].T
        spot = lax.broadcasted_iota(jnp.int32, (r, LANES), 1)
        for hh in range(2):
            form = laid(hh)
            for q in range(2):
                base = q * KP
                form[:, base:base + 1024] = convf[q, :, 0:1024].astype(BF)
                form[:, base + 1024:base + KP] = jnp.where(
                    spot == taps - 1024, column[0:r, q:q + 1], 0.0).astype(BF)
                form[:, base + 1024:base + taps] = convf[q, :, 1024:taps].astype(BF)
                form[:, OUT_AT + q * HALF:OUT_AT + (q + 1) * HALF] = wide[
                    :, (2 * q + hh) * HALF:(2 * q + hh + 1) * HALF].astype(BF)
            form[:, USED:USED + LANES] = jnp.where(
                spot == 0, column[0:r, 2:3], jnp.where(spot == 1, column[0:r, 3:4], 0.0)).astype(BF)
            form[:, USED + LANES:] = jnp.zeros((r, WIDE - USED - LANES), BF)

        @pl.when(hub)
        def _():
            pltpu.make_async_copy(laid_piece(h), wall.at[rows(m), mine], sem_in.at[0]).start()
            pltpu.make_async_copy(laid_piece(1 - h), s2.at[rows(local), :], sem_in.at[3]).start()

        @pl.when(jnp.logical_not(hub))
        def _():
            remote(laid_piece(h), wall.at[rows(m), mine], sem_send.at[1], sem_in.at[0], g, wid(h, h)).start()
            remote(laid_piece(1 - h), s2.at[rows(local), :], sem_send.at[1], sem_in.at[3], g, wid(h, h)).start()

    def far():
        def send_x(s):
            at = s * sub

            @pl.when(s >= SLOTS)
            def _():
                drain(x.at[:, :, pl.ds(0, sub)], sem_fx.at[lax.rem(s, SLOTS)])

            for c in range(clips):
                remote(x.at[c, :, lane(at)], xin.at[rows(m), lane(at + LANES)],
                       sem_fx.at[lax.rem(s, SLOTS)], sem_xh.at[s], g, wid(h, c)).start()
            send_cond(s)

        def send_cot(s):
            at = s * sub

            @pl.when(s >= SLOTS)
            def _():
                drain(cot.at[:, :, :, pl.ds(0, sub)], sem_fc.at[lax.rem(s, SLOTS)])

            for c in range(clips):
                remote(cot.at[c, :, :, lane(at)], cin.at[:, rows(local), lane(at)],
                       sem_fc.at[lax.rem(s, SLOTS)], sem_c.at[s], g, wid(h, c)).start()

        pl.loop(0, 2)(send_x)
        weights()
        pl.loop(2, AHEAD)(send_x)

        @pl.loop(0, blocks)
        def _(s):
            @pl.when(s + AHEAD < blocks)
            def _():
                send_x(s + AHEAD)

            send_cot(s)

        @pl.loop(0, SLOTS)
        def _(q):
            drain(x.at[:, :, pl.ds(0, sub)], sem_fx.at[q])
            drain(cot.at[:, :, :, pl.ds(0, sub)], sem_fc.at[q])

    def work():
        def own(s):
            at = s * sub
            for k in range(1, clips):
                c = lax.rem(wc + k, clips)
                remote(x.at[c, :, lane(at)], xin.at[rows(m), lane(at + LANES)],
                       sem_send.at[3], sem_xh.at[s], g, wid(h, c)).start()
                remote(cot.at[c, :, :, lane(at)], cin.at[:, rows(local), lane(at)],
                       sem_send.at[4], sem_c.at[s], g, wid(h, c)).start()
            pltpu.make_async_copy(x.at[wc, :, lane(at)], xin.at[rows(m), lane(at + LANES)], sem_xh.at[s]).start()
            pltpu.make_async_copy(cot.at[wc, :, :, lane(at)], cin.at[:, rows(local), lane(at)], sem_c.at[s]).start()
            send_cond(s)

        here = pl.ds(pl.multiple_of(h * HALF, HALF), HALF)
        there = pl.ds(pl.multiple_of((1 - h) * HALF, HALF), HALF)

        def direct(s):
            at = s * sub
            for k in range(clips):
                c = lax.rem(wc + k, clips)
                remote(x.at[c, :, lane(at)], xin.at[rows(m), lane(at + LANES)],
                       sem_send.at[17], sem_xm.at[s], g, wid(1 - h, c)).start()

        far_rows = pl.ds(pl.multiple_of(h * (HALF + clips * r), r), HALF - clips * r)

        def relay(s):
            part = xin.at[far_rows, lane(s * sub + LANES)]
            drain(xin.at[here, lane(s * sub + LANES)], sem_xh.at[s])
            remote(part, part, sem_send.at[5], sem_xm.at[s], g, mirror).start()

            @pl.when(s + DIRECT < blocks)
            def _():
                direct(s + DIRECT)

            @pl.when(in_half(s))
            def _():
                also = cnd.at[pl.ds(0, mel), lane(s * sub)]
                drain(also, sem_k.at[s])
                remote(also, also, sem_send.at[12], sem_km.at[s], g, mirror).start()

        pl.loop(0, DIRECT)(direct)
        weights()
        pl.loop(0, AHEAD + OWN)(own)

        xin[:, 0:LANES] = jnp.zeros((RESIDUAL_WIDTH, LANES), BF)
        pg[...] = jnp.zeros_like(pg)
        cnd[mel:LANES, :] = (
            lax.broadcasted_iota(jnp.int32, (LANES - mel, slot), 0) == 0
        ).astype(F32).astype(BF)
        gacc[...] = jnp.zeros_like(gacc)
        csum[...] = jnp.zeros_like(csum)

        pl.loop(0, 2)(relay)
        drain(wall.at[kept, mine], sem_in.at[0])

        @pl.when(hub)
        def _():
            drain(s2, sem_in.at[3])
            remote(s2, wall.at[kept, mine], sem_send.at[2], sem_in.at[0], g, mirror).start()

        @pl.loop(1, d)
        def _(k):
            remote(wall.at[kept, mine], wall.at[kept, mine], sem_send.at[6], sem_in.at[1],
                   lax.rem(g + k, d), m).start()

        pl.loop(2, 9)(relay)
        drain(wall.at[kept, pl.ds(0, (d - 1) * piece)], sem_in.at[1])
        for k in range(1, clips):
            remote(wall.at[kept, :], wall.at[kept, :], sem_send.at[7], sem_in.at[2], g,
                   wid(h, lax.rem(wc + k, clips))).start()
        pl.loop(9, AHEAD)(relay)
        drain(wall.at[pl.ds(0, GH - band), :], sem_in.at[2])

        @pl.when(hub)
        def _():
            drain(s2, sem_send.at[2])

        @pl.when(jnp.logical_not(hub))
        def _():
            drain(gsend.at[pl.ds(0, 2 * r), mine], sem_send.at[1])


        @pl.loop(0, USED // LANES)
        def _(i):
            wtr[pl.ds(pl.multiple_of(i * LANES, LANES), LANES), :] = wall[:, lane(i * LANES, LANES)].T

        length = lens[wc]

        def back(top):
            win = pg[...]
            pn = win[:, :sub]
            pe = pltpu.roll(win, sub + LANES - DILATION_STEP, 1)[:, :sub]

            def tap(base):
                return wtr[pl.ds(pl.multiple_of(base + top, HALF), HALF), :]

            return (dot(tap(512), pn[0:512]) + dot(wtr[pl.ds(pl.multiple_of(KP + 512 + top, LANES), HALF), :], pn[512:1024])
                    + dot(tap(0), pe[0:512]) + dot(wtr[pl.ds(pl.multiple_of(KP + top, LANES), HALF), :], pe[512:1024]))

        def gone(q):
            drain(gsend.at[:, pl.ds(0, sub)], sem_gv.at[lax.rem(q, POSTS)])

        def give(q):
            remote(gsend.at[:, lane((q + 1) * sub)], grecv.at[:, lane(q * sub)],
                   sem_gv.at[lax.rem(q, POSTS)], sem_gm.at[q], g, mirror).start()

        def add_cond(s):
            now = lane(s * sub)
            keeper = s // per
            spot = gco.at[wc, :, lane(s * sub - keeper * t)]
            drain(kr.at[:, later(s)], sem_kr.at[s])
            gk[:, now] = (gk[:, now].astype(F32) + kr[:, later(s)].astype(F32)).astype(BF)

            @pl.when(keeper == m)
            def _():
                pltpu.make_async_copy(gk.at[:, now], spot, sem_send.at[13]).start()

            @pl.when(keeper != m)
            def _():
                remote(gk.at[:, now], spot, sem_send.at[14], sem_in.at[6], g, keeper).start()

        def combine(q):
            now = lane(q * sub)
            z = lax.rem(q, SLOTS)
            drain(grecv.at[:, now], sem_gm.at[q])

            @pl.when(q >= SLOTS)
            def _():
                drain(gfs.at[z], sem_gf.at[z])

            gfs[z] = (gown[:, lane((q + 1) * sub)].astype(F32) + grecv[:, now].astype(F32)).astype(BF)

            @others
            def _(i):
                remote(gfs.at[z, rows(i), :], gio.at[wc, :, now], sem_gf.at[z], sem_in.at[5], g, first + i).start()

            pltpu.make_async_copy(gfs.at[z, rows(local), :], gio.at[wc, :, now], sem_gf.at[z]).start()

        def send_results(s):
            now = lane(s * sub)
            z = lax.rem(s, SLOTS)

            @others
            def _(i):
                remote(ost.at[z, :, rows(i), :], bro.at[wc, :, :, now], sem_o.at[z], sem_in.at[10], g, first + i).start()

            pltpu.make_async_copy(ost.at[z, :, rows(local), :], bro.at[wc, :, :, now], sem_o.at[z]).start()

            @pl.when(jnp.logical_not(in_half(s)))
            def _():
                remote(gk.at[:, now], kr.at[:, later(s)], sem_send.at[8], sem_kr.at[s], g, mirror).start()

        @pl.loop(0, blocks)
        def _(s):
            at = s * sub
            now = lane(at)
            off = lane(at + LANES)
            z = lax.rem(s, SLOTS)

            @pl.when(s + AHEAD + OWN < blocks)
            def _():
                own(s + AHEAD + OWN)

            @pl.when(s + AHEAD < blocks)
            def _():
                relay(s + AHEAD)

            @pl.when(s >= 1)
            def _():
                send_results(s - 1)

            @pl.when(s >= GIVE + POSTS)
            def _():
                gone(s - GIVE - POSTS)

            @pl.when(s >= GIVE)
            def _():
                give(s - GIVE)

            @pl.when(s >= GIVE + LAG)
            def _():
                combine(s - GIVE - LAG)

            @pl.when(jnp.logical_and(s >= LATE, in_half(s - LATE)))
            def _():
                add_cond(s - LATE)

            @pl.when(jnp.logical_not(in_half(s)))
            def _():
                drain(cnd.at[pl.ds(0, mel), now], sem_km.at[s])

            @pl.when(s >= SLOTS)
            def _():
                drain(ost.at[z], sem_o.at[z])

            drain(xin.at[there, off], sem_xm.at[s])
            drain(cin.at[:, :, now], sem_c.at[s])

            xc = xin[:, off]
            xe = pltpu.roll(xin[:, lane(at, sub + LANES)], DILATION_STEP, 1)[:, LANES:]
            cd = cnd[:, now]
            pre_f = (dot(wall[:, 0:512], xe) + dot(wall[:, 512:1024], xc) + dot(wall[:, 1024:KP], cd))
            pre_g = (dot(wall[:, KP:KP + 512], xe) + dot(wall[:, KP + 512:KP + 1024], xc)
                     + dot(wall[:, KP + 1024:OUT_AT], cd))
            place = at + lax.broadcasted_iota(jnp.int32, (1, sub), 1)
            keep = (place < length).astype(F32)
            th = jnp.tanh(pre_f)
            sg = jax.nn.sigmoid(pre_g)
            hid = (keep * th * sg).astype(BF)
            branch = dot(wtr[OUT_AT:USED, :], hid)
            offset = wall[here, USED:USED + LANES].astype(F32)
            ost[z, 0] = (xin[here, off].astype(F32) + branch[0:HALF] + offset[:, 0:1]).astype(BF)
            ost[z, 1] = (branch[HALF:] + offset[:, 1:2]).astype(BF)
            ct = cin[:, :, now].reshape(2 * HALF, sub)
            for q in range(sub // LANES):
                csum[...] += ct[:, q * LANES:(q + 1) * LANES].astype(F32)
            hg = dot(wall[:, OUT_AT:USED], ct) * keep
            pgf = (hg * sg * (1.0 - th * th)).astype(BF)
            pgg = (hg * th * sg * (1.0 - sg)).astype(BF)
            pg[0:512, sub:] = pgf[:, :LANES]
            pg[512:1024, sub:] = pgg[:, :LANES]
            gacc[:, 0:512] += dot_nt(pgf, xe)
            gacc[:, 512:1024] += dot_nt(pgf, xc)
            gacc[:, 1024:KP] += dot_nt(pgf, cd)
            gacc[:, KP:KP + 512] += dot_nt(pgg, xe)
            gacc[:, KP + 512:KP + 1024] += dot_nt(pgg, xc)
            gacc[:, KP + 1024:OUT_AT] += dot_nt(pgg, cd)
            gacc[:, OUT_AT:USED] += dot_nt(hid, ct)
            gk[:, now] = (dot(wtr[1024:KP, :], pgf) + dot(wtr[KP + 1024:OUT_AT, :], pgg))[0:mel].astype(BF)
            gsend[:, now] = back((1 - h) * HALF).astype(BF)
            gown[:, now] = back(h * HALF).astype(BF)
            pg[0:512, 0:sub] = pgf
            pg[512:1024, 0:sub] = pgg

        send_results(blocks - 1)
        pg[:, sub:] = jnp.zeros((2 * GH, LANES), BF)
        gsend[:, pl.ds(slot, sub)] = back((1 - h) * HALF).astype(BF)
        gown[:, pl.ds(slot, sub)] = back(h * HALF).astype(BF)

        def spread(part, dst, sem):
            @others
            def _(i):
                remote(part.at[rows(i), :], dst, sem, sem_in.at[8], g, first + i).start()

            pltpu.make_async_copy(part.at[rows(local), :], dst, sem_in.at[8]).start()

        spot = lax.broadcasted_iota(jnp.int32, (HALF, LANES), 1)
        total = jnp.sum(csum[...], axis=1, keepdims=True)
        gacc[here, USED:USED + LANES] = jnp.where(spot == 0, total[0:HALF], jnp.where(spot == 1, total[HALF:], 0.0))

        s0 = cin.at[0, :, pl.ds(0, WIDE)]
        for k in range(1, clips):
            to = lax.rem(wc + k, clips)
            s0[...] = gacc[pl.ds(pl.multiple_of(to * band, band), band), :].astype(BF)
            remote(s0, r0.at[k - 1], sem_send.at[9], sem_in.at[7], g, wid(h, to)).start()

        start = blocks - GIVE
        pl.loop(start - POSTS, start - SLOTS)(gone)

        def tail(q):
            gone(q - SLOTS)
            give(q)
            combine(q - LAG)
            more = q + GIVE - LATE

            @pl.when(jnp.logical_and(more < blocks, in_half(more)))
            def _():
                add_cond(more)

        pl.loop(start, start + 2)(tail)
        drain(r0, sem_in.at[7])
        for k in range(1, clips):
            gacc[kept, :] += r0[k - 1].astype(F32)

        @pl.loop(1, d)
        def _(k):
            to = lax.rem(g + k, d)
            src = cin.at[1, :, lane((k - 1) * piece, piece)]
            src[...] = gacc[kept, lane(to * piece, piece)].astype(BF)
            remote(src, r1.at[k - 1], sem_send.at[10], sem_r1.at[k - 1], to, m).start()

        pl.loop(start + 2, start + 7)(tail)

        @pl.loop(1, d)
        def _(k):
            drain(r1.at[k - 1], sem_r1.at[k - 1])
            gacc[kept, mine] += r1[k - 1].astype(F32)

        s2[...] = gacc[kept, mine].astype(BF)

        @pl.when(jnp.logical_not(hub))
        def _():
            remote(s2, r2, sem_send.at[11], sem_in.at[4], g, mirror).start()

        pl.loop(start + 7, start + 13)(tail)

        @pl.when(hub)
        def _():
            drain(r2, sem_in.at[4])

            @pl.when(shared)
            def _():
                s2[...] = (gacc[kept, mine] + r2[...].astype(F32)).astype(BF)
                spread(s2, gw.at[0, :, mine], sem_send.at[11])

            @pl.when(jnp.logical_not(shared))
            def _():
                spread(s2, gw.at[h, :, mine], sem_send.at[11])
                spread(r2, gw.at[1 - h, :, mine], sem_send.at[15])

        pl.loop(start + 13, blocks)(tail)
        share_out()
        pl.loop(blocks - SLOTS, blocks)(gone)
        pl.loop(blocks - LAG, blocks)(combine)

        @pl.loop(0, SLOTS)
        def _(q):
            drain(ost.at[q], sem_o.at[q])
            drain(gfs.at[q], sem_gf.at[q])

        drain(x.at[pl.ds(0, clips - 1)], sem_send.at[3])
        drain(cot.at[pl.ds(0, clips - 1)], sem_send.at[4])
        drain(xin.at[pl.ds(0, HALF - clips * r), pl.ds(0, slot)], sem_send.at[5])
        drain(x, sem_send.at[17])
        drain(wall.at[kept, pl.ds(0, (d - 1) * piece)], sem_send.at[6])
        drain(wall.at[pl.ds(0, GH - band), :], sem_send.at[7])
        drain(gk.at[:, pl.ds(0, slot // 2)], sem_send.at[8])
        drain(cnd.at[pl.ds(0, mel), pl.ds(0, slot // 2)], sem_send.at[12])
        drain(gk.at[:, pl.ds(0, t)], sem_send.at[13])
        drain(gk.at[:, pl.ds(0, slot // 2 - t)], sem_send.at[14])
        drain(r0, sem_send.at[9])
        drain(r1, sem_send.at[10])

    def share_out():
        @pl.when(shared)
        def _():
            drain(gw.at[0, :, mine], sem_in.at[8])
            share(gw.at[0, :, mine])

        @pl.when(jnp.logical_not(shared))
        def _():
            drain(gw.at[:, :, mine], sem_in.at[8])
            share(gw.at[:, :, mine])

    def share(part):
        @pl.loop(1, d)
        def _(k):
            remote(part, part, sem_send.at[16], sem_in.at[9], lax.rem(g + k, d), m).start()

    @pl.when(worker)
    def _():
        work()
        drain(cond.at[pl.ds(0, clips - 1)], sem_send.at[0])
        drain(bro.at[pl.ds(0, clips - 1)], sem_in.at[10])
        drain(gio.at[pl.ds(0, clips - 1)], sem_in.at[5])
        drain(gco.at[pl.ds(0, clips - 1)], sem_in.at[6])

        @pl.when(hub)
        def _():
            drain(s2.at[pl.ds(0, HALF - r), :], sem_send.at[11])

            @pl.when(jnp.logical_not(shared))
            def _():
                drain(r2.at[pl.ds(0, HALF - r), :], sem_send.at[15])

        @pl.when(jnp.logical_not(hub))
        def _():
            drain(s2, sem_send.at[11])

    @pl.when(jnp.logical_not(worker))
    def _():
        far()
        share_out()
        drain(cond, sem_send.at[0])
        drain(gsend.at[pl.ds(0, 2 * r), mine], sem_send.at[1])
        drain(bro, sem_in.at[10])
        drain(gio, sem_in.at[5])
        drain(gco, sem_in.at[6])

    own_piece = 2 * d - OUT_AT // piece

    @pl.when(shared)
    def _():
        whole(gw, own_piece - 1, sem_in.at[9])
        whole(gw, d - 1, sem_send.at[16])

    @pl.when(jnp.logical_not(shared))
    def _():
        whole(gw, own_piece - 2, sem_in.at[9])
        whole(gw, 2 * (d - 1), sem_send.at[16])


def run_layer(n, d, x, cot, cond, lens, conv, proj, bias):
    clips, r, slot = x.shape
    mel = cond.shape[1]
    t = slot // n
    sub = min(256, t)
    blocks = slot // sub
    piece = WIDE // d
    width = RESIDUAL_WIDTH
    band = GH // clips
    any_spec = pl.BlockSpec(memory_space=pltpu.HBM)
    vmem = pl.BlockSpec(memory_space=pltpu.VMEM)
    smem = pl.BlockSpec(memory_space=pltpu.SMEM)
    dma = pltpu.SemaphoreType.DMA
    return pl.pallas_call(
        functools.partial(layer_kernel, n, d, clips, slot, sub, mel),
        out_shape=(
            jax.ShapeDtypeStruct((clips, 2, r, slot), BF),
            jax.ShapeDtypeStruct((clips, r, slot), BF),
            jax.ShapeDtypeStruct((clips, mel, t), BF),
            jax.ShapeDtypeStruct((2, r, WIDE), BF),
        ),
        in_specs=[any_spec, any_spec, any_spec, smem, any_spec, any_spec, vmem],
        out_specs=(any_spec, any_spec, any_spec, vmem),
        scratch_shapes=[
            pltpu.VMEM(conv.shape, F32),
            pltpu.VMEM((8, LANES), F32),
            pltpu.VMEM((width, LANES + slot), BF),
            pltpu.VMEM((2, HALF, slot), BF),
            pltpu.VMEM((LANES, slot), BF),
            pltpu.VMEM((HALF, slot), BF),
            pltpu.VMEM((HALF, slot + sub), BF),
            pltpu.VMEM((HALF, slot + sub), BF),
            pltpu.VMEM((GH, WIDE), BF),
            pltpu.VMEM((USED, GH), BF),
            pltpu.VMEM((2 * GH, sub + LANES), BF),
            pltpu.VMEM((GH, WIDE), F32),
            pltpu.VMEM((2 * HALF, LANES), F32),
            pltpu.VMEM((SLOTS, 2, HALF, sub), BF),
            pltpu.VMEM((SLOTS, HALF, sub), BF),
            pltpu.VMEM((mel, slot), BF),
            pltpu.VMEM((mel, slot // 2), BF),
            pltpu.VMEM((clips - 1, band, WIDE), BF),
            pltpu.VMEM((d - 1, band, piece), BF),
            pltpu.VMEM((band, piece), BF),
            pltpu.VMEM((band, piece), BF),
            dma((SLOTS,)),
            dma((SLOTS,)),
            dma((18,)),
            dma((blocks,)),
            dma((blocks,)),
            dma((blocks,)),
            dma((blocks,)),
            dma((blocks,)),
            dma((blocks,)),
            dma((blocks,)),
            dma((POSTS,)),
            dma((SLOTS,)),
            dma((SLOTS,)),
            dma((11,)),
            dma((d - 1,)),
            dma((2,)),
        ],
        compiler_params=pltpu.CompilerParams(
            collective_id=0, has_side_effects=True, vmem_limit_bytes=60 << 20
        ),
    )(x, cot, cond, lens, conv, proj, bias)


def adamw(master, first_old, second_old, gradient, step_rate, power_one, power_two):
    first_new = BETA_ONE * first_old + (1.0 - BETA_ONE) * gradient
    second_new = BETA_TWO * second_old + (1.0 - BETA_TWO) * gradient * gradient
    first_hat = first_new / (1.0 - power_one)
    second_hat = second_new / (1.0 - power_two)
    renewed = master - step_rate * (
        first_hat / (jnp.sqrt(second_hat) + EPSILON) + WEIGHT_DECAY * master
    )
    return (renewed, first_new, second_new)


def finish_kernel(
    taps, span,
    lo, gio, cot, gco, gw, cw, cm, cv, ow, om, ov, bw, bm, bv,
    lo_out, gi_out, gc_out, cw_out, ow_out, bw_out, cm_out, om_out, bm_out, cv_out, ov_out, bv_out,
    cl_out, ol_out, bl_out,
    lo_v, gio_v, cot_v, gi_v, gco_v, gc_v, gw_v, conv_v, convl_v, proj_v, projl_v,
    sem_lo, sem_gi, sem_cot, sem_small, sem_out,
):
    clips, r, slot = gio.shape
    parts = slot // span
    power_one = jnp.float32(BETA_ONE**STEP)
    power_two = jnp.float32(BETA_TWO**STEP)

    small = [
        pltpu.make_async_copy(src, dst, sem_small.at[i])
        for i, (src, dst) in enumerate(
            [(gw, gw_v), (gco, gco_v)]
            + [(a, conv_v.at[q]) for q, a in enumerate((cw, cm, cv))]
            + [(a, proj_v.at[q]) for q, a in enumerate((ow, om, ov))]
        )
    ]
    blocks = [(c, slice(p * span, (p + 1) * span)) for c in range(clips) for p in range(parts)]
    loads = [
        (
            pltpu.make_async_copy(gio.at[c, :, at], gio_v.at[c, :, at], sem_gi.at[i]),
            pltpu.make_async_copy(cot.at[c, 0, :, at], cot_v.at[c, :, at], sem_cot.at[i]),
            pltpu.make_async_copy(lo.at[c, :, :, at], lo_v.at[c, :, :, at], sem_lo.at[i]),
        )
        for i, (c, at) in enumerate(blocks)
    ]
    for copy in small[:5]:
        copy.start()
    for load in loads[:2]:
        for copy in load:
            copy.start()
    for copy in small[5:]:
        copy.start()
    for load in loads[2:]:
        for copy in load:
            copy.start()

    stores = []

    def store(src, dst):
        copy = pltpu.make_async_copy(src, dst, sem_out.at[len(stores)])
        copy.start()
        stores.append(copy)

    def block(i):
        c, at = blocks[i]
        one, two, three = loads[i]
        three.wait()
        store(lo_v.at[c, :, :, at], lo_out.at[c, :, :, at])
        one.wait()
        two.wait()
        gi_v[c, :, at] = cot_v[c, :, at].astype(F32) + gio_v[c, :, at].astype(F32)
        store(gi_v.at[c, :, at], gi_out.at[c, :, at])

    block(0)
    for copy in small[:5]:
        copy.wait()
    gc_v[...] = gco_v[...].astype(F32)
    store(gc_v, gc_out)
    for q in range(2):
        w, m, v = adamw(conv_v[0, q], conv_v[1, q], conv_v[2, q], gw_v[0, :, q * KP:q * KP + taps].astype(F32),
                        CONV_RATE, power_one, power_two)
        conv_v[0, q], conv_v[1, q], conv_v[2, q] = w, m, v
        convl_v[q] = w.astype(BF)
    for i, dst in enumerate((cw_out, cm_out, cv_out)):
        store(conv_v.at[i], dst)
    store(convl_v, cl_out)
    block(1)
    for copy in small[5:]:
        copy.wait()
    for q in range(4):
        at = slice(q * HALF, (q + 1) * HALF)
        from_at = OUT_AT + q // 2 * HALF
        w, m, v = adamw(proj_v[0, :, at], proj_v[1, :, at], proj_v[2, :, at],
                        gw_v[q % 2, :, from_at:from_at + HALF].astype(F32), OUT_RATE, power_one, power_two)
        proj_v[0, :, at], proj_v[1, :, at], proj_v[2, :, at] = w, m, v
        projl_v[:, at] = w.astype(BF)
    for i, dst in enumerate((ow_out, om_out, ov_out)):
        store(proj_v.at[i], dst)
    store(projl_v, ol_out)
    spot = lax.broadcasted_iota(jnp.int32, (r, LANES), 1)
    last = taps - 1024
    sums = gw_v[0, :, USED:USED + LANES].astype(F32) + gw_v[1, :, USED:USED + LANES].astype(F32)
    columns = (
        gw_v[0, :, 1024:KP].astype(F32)[:, last:last + 1],
        gw_v[0, :, KP + 1024:OUT_AT].astype(F32)[:, last:last + 1],
        sums[:, 0:1],
        sums[:, 1:2],
    )
    table = jnp.zeros((r, LANES), F32)
    for i, column in enumerate(columns):
        table = jnp.where(spot == i, column, table)
    w, m, v = adamw(bw[...], bm[...], bv[...], table.T[0:4], BIAS_RATE, power_one, power_two)
    bw_out[...], bm_out[...], bv_out[...] = w, m, v
    bl_out[...] = w.astype(BF)
    for i in range(2, len(blocks)):
        block(i)
    for copy in stores:
        copy.wait()


def finish(lo, gio, cot, gco, gw, conv, proj, bias):
    clips, r, slot = gio.shape
    taps = conv[0].shape[2]
    span = 2048
    count = clips * (slot // span)
    any_spec = pl.BlockSpec(memory_space=pltpu.HBM)
    vmem = pl.BlockSpec(memory_space=pltpu.VMEM)
    dma = pltpu.SemaphoreType.DMA

    def like(a, dtype=None):
        return jax.ShapeDtypeStruct(a.shape, dtype or a.dtype)

    trio = [like(conv[0]), like(proj[0]), like(bias[0])]
    return pl.pallas_call(
        functools.partial(finish_kernel, taps, span),
        out_shape=[like(lo), like(gio, F32), like(gco, F32)] + trio * 3
        + [like(a, BF) for a in (conv[0], proj[0], bias[0])],
        in_specs=[any_spec] * 11 + [vmem] * 3,
        out_specs=[any_spec] * 3 + [any_spec, any_spec, vmem] * 4,
        scratch_shapes=[
            pltpu.VMEM(lo.shape, BF),
            pltpu.VMEM(gio.shape, BF),
            pltpu.VMEM(gio.shape, BF),
            pltpu.VMEM(gio.shape, F32),
            pltpu.VMEM(gco.shape, BF),
            pltpu.VMEM(gco.shape, F32),
            pltpu.VMEM(gw.shape, BF),
            pltpu.VMEM((3, *conv[0].shape), F32),
            pltpu.VMEM(conv[0].shape, BF),
            pltpu.VMEM((3, *proj[0].shape), F32),
            pltpu.VMEM(proj[0].shape, BF),
            dma((count,)),
            dma((count,)),
            dma((count,)),
            dma((8,)),
            dma((2 * count + 9,)),
        ],
        compiler_params=pltpu.CompilerParams(vmem_limit_bytes=60 << 20),
    )(lo, gio, cot, gco, gw, *conv, *proj, *bias)


def per_device(
    n, d,
    inputs, conditioning, lengths, cotangent, conv_weight, out_weight, biases,
    conv_first, out_first, bias_first, conv_second, out_second, bias_second,
):
    conv = [jnp.transpose(a, (1, 2, 0)) for a in (conv_weight, conv_first, conv_second)]
    proj = [out_weight, out_first, out_second]
    bias = [biases, bias_first, bias_second]
    cond = jnp.transpose(conditioning, (0, 2, 1))
    lo, gio, gco, gw = run_layer(n, d, inputs, cotangent, cond, lengths, conv[0], proj[0], bias[0])
    outs = finish(lo, gio, cotangent, gco, gw, conv, proj, bias)
    layer_out, grad_input, grad_cond = outs[:3]
    news = [jnp.transpose(a, (2, 0, 1)) if i % 3 == 0 else a for i, a in enumerate(outs[3:])]
    return (layer_out, grad_input, jnp.transpose(grad_cond, (0, 2, 1)), *news)


def solution(mesh):
    in_specs = (
        P("dp", "mp", None),
        P("dp", "mp", None),
        P("dp"),
        P("dp", None, "mp", None),
        P(None, None, "mp"),
        P("mp", None),
        P(None, "mp"),
        P(None, None, "mp"),
        P("mp", None),
        P(None, "mp"),
        P(None, None, "mp"),
        P("mp", None),
        P(None, "mp"),
    )
    out_specs = (
        P("dp", None, "mp", None),
        P("dp", "mp", None),
        P("dp", "mp", None),
        P(None, None, "mp"),
        P("mp", None),
        P(None, "mp"),
        P(None, None, "mp"),
        P("mp", None),
        P(None, "mp"),
        P(None, None, "mp"),
        P("mp", None),
        P(None, "mp"),
        P(None, None, "mp"),
        P("mp", None),
        P(None, "mp"),
    )
    return jax.shard_map(
        functools.partial(per_device, mesh.shape["mp"], mesh.shape["dp"]),
        mesh=mesh, in_specs=in_specs, out_specs=out_specs, check_vma=False,
    )
```

```python
import functools

import jax
import jax.numpy as jnp
from jax import lax
from jax.experimental import pallas as pl
from jax.experimental.pallas import tpu as pltpu
from jax.sharding import PartitionSpec as P

RESIDUAL_WIDTH = 512
GH = 512
DILATION_STEP = 32
STEP = 4

BETA_ONE = 0.5
BETA_TWO = 0.5
EPSILON = 1e-08
WEIGHT_DECAY = 0.01
CONV_RATE = 0.03
OUT_RATE = 0.1
BIAS_RATE = 0.3

MESH = pl.DeviceIdType.MESH
LANES = 128
HALF = RESIDUAL_WIDTH // 2
KP = 1152
OUT_AT = 2 * KP
USED = OUT_AT + 2 * HALF
WIDE = 3072
AHEAD = 16
OWN = 6
DIRECT = 6
GIVE = 14
LAG = 8
SLOTS = 4
LATE = 12
POSTS = 8
BF = jnp.bfloat16
F32 = jnp.float32


def dot(a, b):
    return jnp.dot(a, b, preferred_element_type=F32)


def dot_nt(a, b):
    return lax.dot_general(a, b, (((1,), (1,)), ((), ())), preferred_element_type=F32)


def layer_kernel(
    n, d, clips, slot, sub, mel,
    x, cot, cond, lens, conv, proj, bias,
    bro, gio, gco, gw,
    convf, turn, xin, cin, cnd, grecv, lay, wall, wtr, pg, gacc, csum, ost, gfs, gk, kr, r0, r1, s2, r2,
    sem_fx, sem_fc, sem_send, sem_xh, sem_xm, sem_c, sem_k, sem_km, sem_kr, sem_gm, sem_gv, sem_o, sem_gf, sem_in, sem_r1, sem_pre,
):
    g = lax.axis_index("dp")
    m = lax.axis_index("mp")
    r = RESIDUAL_WIDTH // n
    t = slot // n
    per = t // sub
    blocks = slot // sub
    piece = WIDE // d
    half = n // 2
    band = GH // clips
    h = m // half
    first = h * half
    local = m - first
    worker = jnp.logical_and(m >= half - clips, m < half + clips)
    wc = lax.rem(m + 2 * clips * n - (half - clips), clips)
    mirror = half - clips + (1 - h) * clips + wc
    hub = jnp.logical_and(worker, wc == h)
    shared = (g + 1) * piece <= OUT_AT

    def wid(hh, c):
        return half - clips + hh * clips + c

    def lane(i, size=sub):
        return pl.ds(pl.multiple_of(i, LANES), size)

    def rows(j):
        return pl.ds(pl.multiple_of(j * r, r), r)

    def remote(src, dst, ss, rs, gg, j):
        return pltpu.make_async_remote_copy(
            src_ref=src, dst_ref=dst, send_sem=ss, recv_sem=rs,
            device_id=(gg, j), device_id_type=MESH,
        )

    def others(body):
        if half <= 4:
            for k in range(1, half):
                body(lax.rem(local + k, half))
        else:
            pl.loop(1, half)(lambda k: body(lax.rem(local + k, half)))

    def drain(ref, sem):
        pltpu.make_async_copy(ref, ref, sem).wait()

    def whole(ref, count, sem):
        drain(ref.at[0, :, pl.ds(0, count * piece)] if count <= d else ref.at[:, :, pl.ds(0, count // 2 * piece)], sem)

    projf = gacc.at[pl.ds(0, r), pl.ds(0, proj.shape[1])]
    pltpu.make_async_copy(conv, convf, sem_pre.at[0]).start()
    pltpu.make_async_copy(proj, projf, sem_pre.at[1]).start()

    bar = pltpu.get_barrier_semaphore()

    @pl.loop(1, half)
    def _(k):
        pl.semaphore_signal(bar, inc=1, device_id=(g, first + lax.rem(local + k, half)), device_id_type=MESH)

    @pl.loop(1, d)
    def _(k):
        pl.semaphore_signal(bar, inc=1, device_id=(lax.rem(g + k, d), m), device_id_type=MESH)

    @pl.when(worker)
    def _():
        for c in range(clips):
            pl.semaphore_signal(bar, inc=1, device_id=(g, wid(1 - h, c)), device_id_type=MESH)
        pl.semaphore_wait(bar, half + d - 2 + clips)

    @pl.when(jnp.logical_not(worker))
    def _():
        pl.semaphore_wait(bar, half + d - 2)

    mine = lane(g * piece, piece)

    def laid(hh):
        return lay.at[rows(hh), :]

    def laid_piece(hh):
        return lay.at[rows(hh), mine]
    kept = pl.ds(pl.multiple_of(wc * band, band), band)

    def send_cond(s):
        @pl.when(s // per == m)
        def _():
            dst = cnd.at[pl.ds(0, mel), lane(s * sub)]
            for c in range(clips):
                to = wid(h, c)
                part = cond.at[c, :, lane(s * sub - m * t)]

                @pl.when(to == m)
                def _():
                    pltpu.make_async_copy(part, dst, sem_k.at[s]).start()

                @pl.when(to != m)
                def _():
                    remote(part, dst, sem_send.at[0], sem_k.at[s], g, to).start()

    def later(s):
        return lane(lax.rem(s, blocks // 2) * sub)

    def in_half(s):
        return s // (blocks // 2) == h

    def weights():
        taps = convf.shape[2]
        drain(convf, sem_pre.at[0])
        drain(projf, sem_pre.at[1])
        wide = projf[...]
        turn[...] = jnp.zeros_like(turn)
        turn[0:4, 0:r] = bias[...]
        column = turn[...].T
        spot = lax.broadcasted_iota(jnp.int32, (r, LANES), 1)
        for hh in range(2):
            form = laid(hh)
            for q in range(2):
                base = q * KP
                form[:, base:base + 1024] = convf[q, :, 0:1024].astype(BF)
                form[:, base + 1024:base + KP] = jnp.where(
                    spot == taps - 1024, column[0:r, q:q + 1], 0.0).astype(BF)
                form[:, base + 1024:base + taps] = convf[q, :, 1024:taps].astype(BF)
                form[:, OUT_AT + q * HALF:OUT_AT + (q + 1) * HALF] = wide[
                    :, (2 * q + hh) * HALF:(2 * q + hh + 1) * HALF].astype(BF)
            form[:, USED:USED + LANES] = jnp.where(
                spot == 0, column[0:r, 2:3], jnp.where(spot == 1, column[0:r, 3:4], 0.0)).astype(BF)
            form[:, USED + LANES:] = jnp.zeros((r, WIDE - USED - LANES), BF)

        @pl.when(hub)
        def _():
            pltpu.make_async_copy(laid_piece(h), wall.at[rows(m), mine], sem_in.at[0]).start()
            pltpu.make_async_copy(laid_piece(1 - h), s2.at[rows(local), :], sem_in.at[3]).start()

        @pl.when(jnp.logical_not(hub))
        def _():
            remote(laid_piece(h), wall.at[rows(m), mine], sem_send.at[1], sem_in.at[0], g, wid(h, h)).start()
            remote(laid_piece(1 - h), s2.at[rows(local), :], sem_send.at[1], sem_in.at[3], g, wid(h, h)).start()

    def far():
        def send_x(s):
            at = s * sub

            @pl.when(s >= SLOTS)
            def _():
                drain(x.at[:, :, pl.ds(0, sub)], sem_fx.at[lax.rem(s, SLOTS)])

            for c in range(clips):
                remote(x.at[c, :, lane(at)], xin.at[rows(m), lane(at + LANES)],
                       sem_fx.at[lax.rem(s, SLOTS)], sem_xh.at[s], g, wid(h, c)).start()
            send_cond(s)

        def send_cot(s):
            at = s * sub

            @pl.when(s >= SLOTS)
            def _():
                drain(cot.at[:, :, :, pl.ds(0, sub)], sem_fc.at[lax.rem(s, SLOTS)])

            for c in range(clips):
                remote(cot.at[c, :, :, lane(at)], cin.at[:, rows(local), lane(at)],
                       sem_fc.at[lax.rem(s, SLOTS)], sem_c.at[s], g, wid(h, c)).start()

        pl.loop(0, 2)(send_x)
        weights()
        pl.loop(2, AHEAD)(send_x)

        @pl.loop(0, blocks)
        def _(s):
            @pl.when(s + AHEAD < blocks)
            def _():
                send_x(s + AHEAD)

            send_cot(s)

        @pl.loop(0, SLOTS)
        def _(q):
            drain(x.at[:, :, pl.ds(0, sub)], sem_fx.at[q])
            drain(cot.at[:, :, :, pl.ds(0, sub)], sem_fc.at[q])

    def work():
        def own(s):
            at = s * sub
            for k in range(1, clips):
                c = lax.rem(wc + k, clips)
                remote(x.at[c, :, lane(at)], xin.at[rows(m), lane(at + LANES)],
                       sem_send.at[3], sem_xh.at[s], g, wid(h, c)).start()
                remote(cot.at[c, :, :, lane(at)], cin.at[:, rows(local), lane(at)],
                       sem_send.at[4], sem_c.at[s], g, wid(h, c)).start()
            pltpu.make_async_copy(x.at[wc, :, lane(at)], xin.at[rows(m), lane(at + LANES)], sem_xh.at[s]).start()
            pltpu.make_async_copy(cot.at[wc, :, :, lane(at)], cin.at[:, rows(local), lane(at)], sem_c.at[s]).start()
            send_cond(s)

        here = pl.ds(pl.multiple_of(h * HALF, HALF), HALF)
        there = pl.ds(pl.multiple_of((1 - h) * HALF, HALF), HALF)

        def direct(s):
            at = s * sub
            for k in range(clips):
                c = lax.rem(wc + k, clips)
                remote(x.at[c, :, lane(at)], xin.at[rows(m), lane(at + LANES)],
                       sem_send.at[17], sem_xm.at[s], g, wid(1 - h, c)).start()

        far_rows = pl.ds(pl.multiple_of(h * (HALF + clips * r), r), HALF - clips * r)

        def relay(s):
            part = xin.at[far_rows, lane(s * sub + LANES)]
            drain(xin.at[here, lane(s * sub + LANES)], sem_xh.at[s])
            remote(part, part, sem_send.at[5], sem_xm.at[s], g, mirror).start()

            @pl.when(s + DIRECT < blocks)
            def _():
                direct(s + DIRECT)

            @pl.when(in_half(s))
            def _():
                also = cnd.at[pl.ds(0, mel), lane(s * sub)]
                drain(also, sem_k.at[s])
                remote(also, also, sem_send.at[12], sem_km.at[s], g, mirror).start()

        pl.loop(0, DIRECT)(direct)
        weights()
        pl.loop(0, AHEAD + OWN)(own)

        xin[:, 0:LANES] = jnp.zeros((RESIDUAL_WIDTH, LANES), BF)
        pg[...] = jnp.zeros_like(pg)
        cnd[mel:LANES, :] = (
            lax.broadcasted_iota(jnp.int32, (LANES - mel, slot), 0) == 0
        ).astype(F32).astype(BF)
        gacc[...] = jnp.zeros_like(gacc)
        csum[...] = jnp.zeros_like(csum)

        pl.loop(0, 2)(relay)
        drain(wall.at[kept, mine], sem_in.at[0])

        @pl.when(hub)
        def _():
            drain(s2, sem_in.at[3])
            remote(s2, wall.at[kept, mine], sem_send.at[2], sem_in.at[0], g, mirror).start()

        @pl.loop(1, d)
        def _(k):
            remote(wall.at[kept, mine], wall.at[kept, mine], sem_send.at[6], sem_in.at[1],
                   lax.rem(g + k, d), m).start()

        pl.loop(2, 9)(relay)
        drain(wall.at[kept, pl.ds(0, (d - 1) * piece)], sem_in.at[1])
        for k in range(1, clips):
            remote(wall.at[kept, :], wall.at[kept, :], sem_send.at[7], sem_in.at[2], g,
                   wid(h, lax.rem(wc + k, clips))).start()
        pl.loop(9, AHEAD)(relay)
        drain(wall.at[pl.ds(0, GH - band), :], sem_in.at[2])

        @pl.when(hub)
        def _():
            drain(s2, sem_send.at[2])

        @pl.when(jnp.logical_not(hub))
        def _():
            drain(lay.at[:, mine], sem_send.at[1])


        @pl.loop(0, USED // LANES)
        def _(i):
            wtr[pl.ds(pl.multiple_of(i * LANES, LANES), LANES), :] = wall[:, lane(i * LANES, LANES)].T

        length = lens[wc]

        def back(top):
            win = pg[...]
            pn = win[:, :sub]
            pe = pltpu.roll(win, sub + LANES - DILATION_STEP, 1)[:, :sub]

            def tap(base):
                return wtr[pl.ds(pl.multiple_of(base + top, HALF), HALF), :]

            return (dot(tap(512), pn[0:512]) + dot(wtr[pl.ds(pl.multiple_of(KP + 512 + top, LANES), HALF), :], pn[512:1024])
                    + dot(tap(0), pe[0:512]) + dot(wtr[pl.ds(pl.multiple_of(KP + top, LANES), HALF), :], pe[512:1024]))

        def gone(q):
            drain(cin.at[1, :, pl.ds(0, sub)], sem_gv.at[lax.rem(q, POSTS)])

        def give(q):
            remote(cin.at[1, :, lane(q * sub)], grecv.at[:, lane(q * sub)],
                   sem_gv.at[lax.rem(q, POSTS)], sem_gm.at[q], g, mirror).start()

        def add_cond(s):
            now = lane(s * sub)
            keeper = s // per
            spot = gco.at[wc, :, lane(s * sub - keeper * t)]
            drain(kr.at[:, later(s)], sem_kr.at[s])
            gk[:, now] = (gk[:, now].astype(F32) + kr[:, later(s)].astype(F32)).astype(BF)

            @pl.when(keeper == m)
            def _():
                pltpu.make_async_copy(gk.at[:, now], spot, sem_send.at[13]).start()

            @pl.when(keeper != m)
            def _():
                remote(gk.at[:, now], spot, sem_send.at[14], sem_in.at[6], g, keeper).start()

        def combine(q):
            now = lane(q * sub)
            z = lax.rem(q, SLOTS)
            drain(grecv.at[:, now], sem_gm.at[q])

            @pl.when(q >= SLOTS)
            def _():
                drain(gfs.at[z], sem_gf.at[z])

            gfs[z] = (cin[0, :, now].astype(F32) + grecv[:, now].astype(F32)).astype(BF)

            @others
            def _(i):
                remote(gfs.at[z, rows(i), :], gio.at[wc, :, now], sem_gf.at[z], sem_in.at[5], g, first + i).start()

            pltpu.make_async_copy(gfs.at[z, rows(local), :], gio.at[wc, :, now], sem_gf.at[z]).start()

        def send_results(s):
            now = lane(s * sub)
            z = lax.rem(s, SLOTS)

            @others
            def _(i):
                remote(ost.at[z, :, rows(i), :], bro.at[wc, :, :, now], sem_o.at[z], sem_in.at[10], g, first + i).start()

            pltpu.make_async_copy(ost.at[z, :, rows(local), :], bro.at[wc, :, :, now], sem_o.at[z]).start()

            @pl.when(jnp.logical_not(in_half(s)))
            def _():
                remote(gk.at[:, now], kr.at[:, later(s)], sem_send.at[8], sem_kr.at[s], g, mirror).start()

        @pl.loop(0, blocks)
        def _(s):
            at = s * sub
            now = lane(at)
            off = lane(at + LANES)
            z = lax.rem(s, SLOTS)

            @pl.when(s + AHEAD + OWN < blocks)
            def _():
                own(s + AHEAD + OWN)

            @pl.when(s + AHEAD < blocks)
            def _():
                relay(s + AHEAD)

            @pl.when(s >= 1)
            def _():
                send_results(s - 1)

            @pl.when(s >= GIVE + POSTS)
            def _():
                gone(s - GIVE - POSTS)

            @pl.when(s >= GIVE)
            def _():
                give(s - GIVE)

            @pl.when(s >= GIVE + LAG)
            def _():
                combine(s - GIVE - LAG)

            @pl.when(jnp.logical_and(s >= LATE, in_half(s - LATE)))
            def _():
                add_cond(s - LATE)

            @pl.when(jnp.logical_not(in_half(s)))
            def _():
                drain(cnd.at[pl.ds(0, mel), now], sem_km.at[s])

            @pl.when(s >= SLOTS)
            def _():
                drain(ost.at[z], sem_o.at[z])

            drain(xin.at[there, off], sem_xm.at[s])
            drain(cin.at[:, :, now], sem_c.at[s])

            xc = xin[:, off]
            xe = pltpu.roll(xin[:, lane(at, sub + LANES)], DILATION_STEP, 1)[:, LANES:]
            cd = cnd[:, now]
            pre_f = (dot(wall[:, 0:512], xe) + dot(wall[:, 512:1024], xc) + dot(wall[:, 1024:KP], cd))
            pre_g = (dot(wall[:, KP:KP + 512], xe) + dot(wall[:, KP + 512:KP + 1024], xc)
                     + dot(wall[:, KP + 1024:OUT_AT], cd))
            place = at + lax.broadcasted_iota(jnp.int32, (1, sub), 1)
            keep = (place < length).astype(F32)
            th = jnp.tanh(pre_f)
            sg = jax.nn.sigmoid(pre_g)
            hid = (keep * th * sg).astype(BF)
            branch = dot(wtr[OUT_AT:USED, :], hid)
            offset = wall[here, USED:USED + LANES].astype(F32)
            ost[z, 0] = (xin[here, off].astype(F32) + branch[0:HALF] + offset[:, 0:1]).astype(BF)
            ost[z, 1] = (branch[HALF:] + offset[:, 1:2]).astype(BF)
            ct = cin[:, :, now].reshape(2 * HALF, sub)
            for q in range(sub // LANES):
                csum[...] += ct[:, q * LANES:(q + 1) * LANES].astype(F32)
            hg = dot(wall[:, OUT_AT:USED], ct) * keep
            pgf = (hg * sg * (1.0 - th * th)).astype(BF)
            pgg = (hg * th * sg * (1.0 - sg)).astype(BF)
            pg[0:512, sub:] = pgf[:, :LANES]
            pg[512:1024, sub:] = pgg[:, :LANES]
            gacc[:, 0:512] += dot_nt(pgf, xe)
            gacc[:, 512:1024] += dot_nt(pgf, xc)
            gacc[:, 1024:KP] += dot_nt(pgf, cd)
            gacc[:, KP:KP + 512] += dot_nt(pgg, xe)
            gacc[:, KP + 512:KP + 1024] += dot_nt(pgg, xc)
            gacc[:, KP + 1024:OUT_AT] += dot_nt(pgg, cd)
            gacc[:, OUT_AT:USED] += dot_nt(hid, ct)
            gk[:, now] = (dot(wtr[1024:KP, :], pgf) + dot(wtr[KP + 1024:OUT_AT, :], pgg))[0:mel].astype(BF)
            before = lane(jnp.maximum(s - 1, 0) * sub)
            cin[1, :, before] = back((1 - h) * HALF).astype(BF)
            cin[0, :, before] = back(h * HALF).astype(BF)
            pg[0:512, 0:sub] = pgf
            pg[512:1024, 0:sub] = pgg

        send_results(blocks - 1)
        pg[:, sub:] = jnp.zeros((2 * GH, LANES), BF)
        cin[1, :, pl.ds(slot - sub, sub)] = back((1 - h) * HALF).astype(BF)
        cin[0, :, pl.ds(slot - sub, sub)] = back(h * HALF).astype(BF)

        def spread(part, dst, sem):
            @others
            def _(i):
                remote(part.at[rows(i), :], dst, sem, sem_in.at[8], g, first + i).start()

            pltpu.make_async_copy(part.at[rows(local), :], dst, sem_in.at[8]).start()

        spot = lax.broadcasted_iota(jnp.int32, (HALF, LANES), 1)
        total = jnp.sum(csum[...], axis=1, keepdims=True)
        gacc[here, USED:USED + LANES] = jnp.where(spot == 0, total[0:HALF], jnp.where(spot == 1, total[HALF:], 0.0))

        drain(xin.at[pl.ds(0, HALF - clips * r), pl.ds(0, slot)], sem_send.at[5])
        s0 = xin.at[pl.ds(0, band), pl.ds(0, WIDE)]
        for k in range(1, clips):
            to = lax.rem(wc + k, clips)
            s0[...] = gacc[pl.ds(pl.multiple_of(to * band, band), band), :].astype(BF)
            remote(s0, r0.at[k - 1], sem_send.at[9], sem_in.at[7], g, wid(h, to)).start()

        start = blocks - GIVE
        pl.loop(start - POSTS, start - SLOTS)(gone)

        def tail(q):
            gone(q - SLOTS)
            give(q)
            combine(q - LAG)
            more = q + GIVE - LATE

            @pl.when(jnp.logical_and(more < blocks, in_half(more)))
            def _():
                add_cond(more)

        pl.loop(start, start + 2)(tail)
        drain(r0, sem_in.at[7])
        for k in range(1, clips):
            gacc[kept, :] += r0[k - 1].astype(F32)

        @pl.loop(1, d)
        def _(k):
            to = lax.rem(g + k, d)
            src = xin.at[pl.ds(GH - band, band), lane((k - 1) * piece, piece)]
            src[...] = gacc[kept, lane(to * piece, piece)].astype(BF)
            remote(src, r1.at[k - 1], sem_send.at[10], sem_r1.at[k - 1], to, m).start()

        pl.loop(start + 2, start + 7)(tail)

        @pl.loop(1, d)
        def _(k):
            drain(r1.at[k - 1], sem_r1.at[k - 1])
            gacc[kept, mine] += r1[k - 1].astype(F32)

        s2[...] = gacc[kept, mine].astype(BF)

        @pl.when(jnp.logical_not(hub))
        def _():
            remote(s2, r2, sem_send.at[11], sem_in.at[4], g, mirror).start()

        pl.loop(start + 7, start + 13)(tail)

        @pl.when(hub)
        def _():
            drain(r2, sem_in.at[4])

            @pl.when(shared)
            def _():
                s2[...] = (gacc[kept, mine] + r2[...].astype(F32)).astype(BF)
                spread(s2, gw.at[0, :, mine], sem_send.at[11])

            @pl.when(jnp.logical_not(shared))
            def _():
                spread(s2, gw.at[h, :, mine], sem_send.at[11])
                spread(r2, gw.at[1 - h, :, mine], sem_send.at[15])

        pl.loop(start + 13, blocks)(tail)
        share_out()
        pl.loop(blocks - SLOTS, blocks)(gone)
        pl.loop(blocks - LAG, blocks)(combine)

        @pl.loop(0, SLOTS)
        def _(q):
            drain(ost.at[q], sem_o.at[q])
            drain(gfs.at[q], sem_gf.at[q])

        drain(x.at[pl.ds(0, clips - 1)], sem_send.at[3])
        drain(cot.at[pl.ds(0, clips - 1)], sem_send.at[4])
        drain(x, sem_send.at[17])
        drain(wall.at[kept, pl.ds(0, (d - 1) * piece)], sem_send.at[6])
        drain(wall.at[pl.ds(0, GH - band), :], sem_send.at[7])
        drain(gk.at[:, pl.ds(0, slot // 2)], sem_send.at[8])
        drain(cnd.at[pl.ds(0, mel), pl.ds(0, slot // 2)], sem_send.at[12])
        drain(gk.at[:, pl.ds(0, t)], sem_send.at[13])
        drain(gk.at[:, pl.ds(0, slot // 2 - t)], sem_send.at[14])
        drain(r0, sem_send.at[9])
        drain(r1, sem_send.at[10])

    def share_out():
        @pl.when(shared)
        def _():
            drain(gw.at[0, :, mine], sem_in.at[8])
            share(gw.at[0, :, mine])

        @pl.when(jnp.logical_not(shared))
        def _():
            drain(gw.at[:, :, mine], sem_in.at[8])
            share(gw.at[:, :, mine])

    def share(part):
        @pl.loop(1, d)
        def _(k):
            remote(part, part, sem_send.at[16], sem_in.at[9], lax.rem(g + k, d), m).start()

    @pl.when(worker)
    def _():
        work()
        drain(cond.at[pl.ds(0, clips - 1)], sem_send.at[0])
        drain(bro.at[pl.ds(0, clips - 1)], sem_in.at[10])
        drain(gio.at[pl.ds(0, clips - 1)], sem_in.at[5])
        drain(gco.at[pl.ds(0, clips - 1)], sem_in.at[6])

        @pl.when(hub)
        def _():
            drain(s2.at[pl.ds(0, HALF - r), :], sem_send.at[11])

            @pl.when(jnp.logical_not(shared))
            def _():
                drain(r2.at[pl.ds(0, HALF - r), :], sem_send.at[15])

        @pl.when(jnp.logical_not(hub))
        def _():
            drain(s2, sem_send.at[11])

    @pl.when(jnp.logical_not(worker))
    def _():
        far()
        share_out()
        drain(cond, sem_send.at[0])
        drain(lay.at[:, mine], sem_send.at[1])
        drain(bro, sem_in.at[10])
        drain(gio, sem_in.at[5])
        drain(gco, sem_in.at[6])

    own_piece = 2 * d - OUT_AT // piece

    @pl.when(shared)
    def _():
        whole(gw, own_piece - 1, sem_in.at[9])
        whole(gw, d - 1, sem_send.at[16])

    @pl.when(jnp.logical_not(shared))
    def _():
        whole(gw, own_piece - 2, sem_in.at[9])
        whole(gw, 2 * (d - 1), sem_send.at[16])


def run_layer(n, d, x, cot, cond, lens, conv, proj, bias):
    clips, r, slot = x.shape
    mel = cond.shape[1]
    t = slot // n
    sub = min(256, t)
    blocks = slot // sub
    piece = WIDE // d
    width = RESIDUAL_WIDTH
    band = GH // clips
    any_spec = pl.BlockSpec(memory_space=pltpu.HBM)
    vmem = pl.BlockSpec(memory_space=pltpu.VMEM)
    smem = pl.BlockSpec(memory_space=pltpu.SMEM)
    dma = pltpu.SemaphoreType.DMA
    return pl.pallas_call(
        functools.partial(layer_kernel, n, d, clips, slot, sub, mel),
        out_shape=(
            jax.ShapeDtypeStruct((clips, 2, r, slot), BF),
            jax.ShapeDtypeStruct((clips, r, slot), BF),
            jax.ShapeDtypeStruct((clips, mel, t), BF),
            jax.ShapeDtypeStruct((2, r, WIDE), BF),
        ),
        in_specs=[any_spec, any_spec, any_spec, smem, any_spec, any_spec, vmem],
        out_specs=(pl.BlockSpec(memory_space=pl.ANY),) * 3 + (vmem,),
        scratch_shapes=[
            pltpu.VMEM(conv.shape, F32),
            pltpu.VMEM((8, LANES), F32),
            pltpu.VMEM((width, LANES + slot), BF),
            pltpu.VMEM((2, HALF, slot), BF),
            pltpu.VMEM((LANES, slot), BF),
            pltpu.VMEM((HALF, slot), BF),
            pltpu.VMEM((2 * r, WIDE), BF),
            pltpu.VMEM((GH, WIDE), BF),
            pltpu.VMEM((USED, GH), BF),
            pltpu.VMEM((2 * GH, sub + LANES), BF),
            pltpu.VMEM((GH, WIDE), F32),
            pltpu.VMEM((2 * HALF, LANES), F32),
            pltpu.VMEM((SLOTS, 2, HALF, sub), BF),
            pltpu.VMEM((SLOTS, HALF, sub), BF),
            pltpu.VMEM((mel, slot), BF),
            pltpu.VMEM((mel, slot // 2), BF),
            pltpu.VMEM((clips - 1, band, WIDE), BF),
            pltpu.VMEM((d - 1, band, piece), BF),
            pltpu.VMEM((band, piece), BF),
            pltpu.VMEM((band, piece), BF),
            dma((SLOTS,)),
            dma((SLOTS,)),
            dma((18,)),
            dma((blocks,)),
            dma((blocks,)),
            dma((blocks,)),
            dma((blocks,)),
            dma((blocks,)),
            dma((blocks,)),
            dma((blocks,)),
            dma((POSTS,)),
            dma((SLOTS,)),
            dma((SLOTS,)),
            dma((11,)),
            dma((d - 1,)),
            dma((2,)),
        ],
        compiler_params=pltpu.CompilerParams(
            collective_id=0, has_side_effects=True, vmem_limit_bytes=52 << 20
        ),
    )(x, cot, cond, lens, conv, proj, bias)


def adamw(master, first_old, second_old, gradient, step_rate, power_one, power_two):
    first_new = BETA_ONE * first_old + (1.0 - BETA_ONE) * gradient
    second_new = BETA_TWO * second_old + (1.0 - BETA_TWO) * gradient * gradient
    first_hat = first_new / (1.0 - power_one)
    second_hat = second_new / (1.0 - power_two)
    renewed = master - step_rate * (
        first_hat / (jnp.sqrt(second_hat) + EPSILON) + WEIGHT_DECAY * master
    )
    return (renewed, first_new, second_new)


def finish_kernel(
    taps, span,
    lo, gio, cot, gco, gw, cw, cm, cv, ow, om, ov, bw, bm, bv,
    lo_out, gi_out, gc_out, cw_out, ow_out, bw_out, cm_out, om_out, bm_out, cv_out, ov_out, bv_out,
    cl_out, ol_out, bl_out,
    lo_v, gio_v, cot_v, gi_v, gco_v, gc_v, gw_v, conv_v, convl_v, proj_v, projl_v,
    sem_lo, sem_gi, sem_cot, sem_small, sem_out,
):
    clips, r, slot = gio.shape
    parts = slot // span
    power_one = jnp.float32(BETA_ONE**STEP)
    power_two = jnp.float32(BETA_TWO**STEP)

    small = [
        pltpu.make_async_copy(src, dst, sem_small.at[i])
        for i, (src, dst) in enumerate(
            [(gw, gw_v), (gco, gco_v)]
            + [(a, conv_v.at[q]) for q, a in enumerate((cw, cm, cv))]
            + [(a, proj_v.at[q]) for q, a in enumerate((ow, om, ov))]
        )
    ]
    blocks = [(c, slice(p * span, (p + 1) * span)) for c in range(clips) for p in range(parts)]
    loads = [
        (
            pltpu.make_async_copy(gio.at[c, :, at], gio_v.at[c, :, at], sem_gi.at[i]),
            pltpu.make_async_copy(cot.at[c, 0, :, at], cot_v.at[c, :, at], sem_cot.at[i]),
            pltpu.make_async_copy(lo.at[c, :, :, at], lo_v.at[c, :, :, at], sem_lo.at[i]),
        )
        for i, (c, at) in enumerate(blocks)
    ]
    for copy in small[:5]:
        copy.start()
    for load in loads[:2]:
        for copy in load:
            copy.start()
    for copy in small[5:]:
        copy.start()
    for load in loads[2:]:
        for copy in load:
            copy.start()

    stores = []

    def store(src, dst):
        copy = pltpu.make_async_copy(src, dst, sem_out.at[len(stores)])
        copy.start()
        stores.append(copy)

    def block(i):
        c, at = blocks[i]
        one, two, three = loads[i]
        three.wait()
        store(lo_v.at[c, :, :, at], lo_out.at[c, :, :, at])
        one.wait()
        two.wait()
        gi_v[c, :, at] = cot_v[c, :, at].astype(F32) + gio_v[c, :, at].astype(F32)
        store(gi_v.at[c, :, at], gi_out.at[c, :, at])

    block(0)
    for copy in small[:5]:
        copy.wait()
    gc_v[...] = gco_v[...].astype(F32)
    store(gc_v, gc_out)
    for q in range(2):
        w, m, v = adamw(conv_v[0, q], conv_v[1, q], conv_v[2, q], gw_v[0, :, q * KP:q * KP + taps].astype(F32),
                        CONV_RATE, power_one, power_two)
        conv_v[0, q], conv_v[1, q], conv_v[2, q] = w, m, v
        convl_v[q] = w.astype(BF)
    for i, dst in enumerate((cw_out, cm_out, cv_out)):
        store(conv_v.at[i], dst)
    store(convl_v, cl_out)
    block(1)
    for copy in small[5:]:
        copy.wait()
    for q in range(4):
        at = slice(q * HALF, (q + 1) * HALF)
        from_at = OUT_AT + q // 2 * HALF
        w, m, v = adamw(proj_v[0, :, at], proj_v[1, :, at], proj_v[2, :, at],
                        gw_v[q % 2, :, from_at:from_at + HALF].astype(F32), OUT_RATE, power_one, power_two)
        proj_v[0, :, at], proj_v[1, :, at], proj_v[2, :, at] = w, m, v
        projl_v[:, at] = w.astype(BF)
    for i, dst in enumerate((ow_out, om_out, ov_out)):
        store(proj_v.at[i], dst)
    store(projl_v, ol_out)
    spot = lax.broadcasted_iota(jnp.int32, (r, LANES), 1)
    last = taps - 1024
    sums = gw_v[0, :, USED:USED + LANES].astype(F32) + gw_v[1, :, USED:USED + LANES].astype(F32)
    columns = (
        gw_v[0, :, 1024:KP].astype(F32)[:, last:last + 1],
        gw_v[0, :, KP + 1024:OUT_AT].astype(F32)[:, last:last + 1],
        sums[:, 0:1],
        sums[:, 1:2],
    )
    table = jnp.zeros((r, LANES), F32)
    for i, column in enumerate(columns):
        table = jnp.where(spot == i, column, table)
    w, m, v = adamw(bw[...], bm[...], bv[...], table.T[0:4], BIAS_RATE, power_one, power_two)
    bw_out[...], bm_out[...], bv_out[...] = w, m, v
    bl_out[...] = w.astype(BF)
    for i in range(2, len(blocks)):
        block(i)
    for copy in stores:
        copy.wait()


def finish(lo, gio, cot, gco, gw, conv, proj, bias):
    clips, r, slot = gio.shape
    taps = conv[0].shape[2]
    span = 2048
    count = clips * (slot // span)
    any_spec = pl.BlockSpec(memory_space=pltpu.HBM)
    vmem = pl.BlockSpec(memory_space=pltpu.VMEM)
    dma = pltpu.SemaphoreType.DMA

    def like(a, dtype=None):
        return jax.ShapeDtypeStruct(a.shape, dtype or a.dtype)

    trio = [like(conv[0]), like(proj[0]), like(bias[0])]
    return pl.pallas_call(
        functools.partial(finish_kernel, taps, span),
        out_shape=[like(lo), like(gio, F32), like(gco, F32)] + trio * 3
        + [like(a, BF) for a in (conv[0], proj[0], bias[0])],
        in_specs=[any_spec] * 11 + [vmem] * 3,
        out_specs=[any_spec] * 3 + [any_spec, any_spec, vmem] * 4,
        scratch_shapes=[
            pltpu.VMEM(lo.shape, BF),
            pltpu.VMEM(gio.shape, BF),
            pltpu.VMEM(gio.shape, BF),
            pltpu.VMEM(gio.shape, F32),
            pltpu.VMEM(gco.shape, BF),
            pltpu.VMEM(gco.shape, F32),
            pltpu.VMEM(gw.shape, BF),
            pltpu.VMEM((3, *conv[0].shape), F32),
            pltpu.VMEM(conv[0].shape, BF),
            pltpu.VMEM((3, *proj[0].shape), F32),
            pltpu.VMEM(proj[0].shape, BF),
            dma((count,)),
            dma((count,)),
            dma((count,)),
            dma((8,)),
            dma((2 * count + 9,)),
        ],
        compiler_params=pltpu.CompilerParams(vmem_limit_bytes=24 << 20),
    )(lo, gio, cot, gco, gw, *conv, *proj, *bias)


def per_device(
    n, d,
    inputs, conditioning, lengths, cotangent, conv_weight, out_weight, biases,
    conv_first, out_first, bias_first, conv_second, out_second, bias_second,
):
    conv = [jnp.transpose(a, (1, 2, 0)) for a in (conv_weight, conv_first, conv_second)]
    proj = [out_weight, out_first, out_second]
    bias = [biases, bias_first, bias_second]
    cond = jnp.transpose(conditioning, (0, 2, 1))
    def pinned(a):
        return pltpu.with_memory_space_constraint(a, pltpu.HBM)

    lo, gio, gco, gw = run_layer(
        n, d, pinned(inputs), pinned(cotangent), pinned(cond), pinned(lengths), pinned(conv[0]), pinned(proj[0]), pinned(bias[0])
    )
    lo, gio = pinned(lo), pinned(gio)
    outs = finish(lo, gio, cotangent, gco, gw, conv, proj, bias)
    layer_out, grad_input, grad_cond = outs[:3]
    news = [jnp.transpose(a, (2, 0, 1)) if i % 3 == 0 else a for i, a in enumerate(outs[3:])]
    return (layer_out, grad_input, jnp.transpose(grad_cond, (0, 2, 1)), *news)


def solution(mesh):
    in_specs = (
        P("dp", "mp", None),
        P("dp", "mp", None),
        P("dp"),
        P("dp", None, "mp", None),
        P(None, None, "mp"),
        P("mp", None),
        P(None, "mp"),
        P(None, None, "mp"),
        P("mp", None),
        P(None, "mp"),
        P(None, None, "mp"),
        P("mp", None),
        P(None, "mp"),
    )
    out_specs = (
        P("dp", None, "mp", None),
        P("dp", "mp", None),
        P("dp", "mp", None),
        P(None, None, "mp"),
        P("mp", None),
        P(None, "mp"),
        P(None, None, "mp"),
        P("mp", None),
        P(None, "mp"),
        P(None, None, "mp"),
        P("mp", None),
        P(None, "mp"),
        P(None, None, "mp"),
        P("mp", None),
        P(None, "mp"),
    )
    return jax.shard_map(
        functools.partial(per_device, mesh.shape["mp"], mesh.shape["dp"]),
        mesh=mesh, in_specs=in_specs, out_specs=out_specs, check_vma=False,
    )
```

```python
import functools

import jax
import jax.numpy as jnp
from jax import lax
from jax.experimental import pallas as pl
from jax.experimental.pallas import tpu as pltpu
from jax.sharding import PartitionSpec as P

RESIDUAL_WIDTH = 512
GH = 512
DILATION_STEP = 32
STEP = 4

BETA_ONE = 0.5
BETA_TWO = 0.5
EPSILON = 1e-08
WEIGHT_DECAY = 0.01
CONV_RATE = 0.03
OUT_RATE = 0.1
BIAS_RATE = 0.3

MESH = pl.DeviceIdType.MESH
LANES = 128
HALF = RESIDUAL_WIDTH // 2
KP = 1152
OUT_AT = 2 * KP
USED = OUT_AT + 2 * HALF
WIDE = 3072
AHEAD = 16
OWN = 6
DIRECT = 6
GIVE = 14
LAG = 6
SLOTS = 4
LATE = 12
POSTS = 8
BF = jnp.bfloat16
F32 = jnp.float32


def dot(a, b):
    return jnp.dot(a, b, preferred_element_type=F32)


def dot_nt(a, b):
    return lax.dot_general(a, b, (((1,), (1,)), ((), ())), preferred_element_type=F32)


def layer_kernel(
    n, d, clips, slot, sub, mel,
    x, cot, cond, lens, conv, proj, bias,
    bro, gio, gco, gw,
    convf, turn, xin, cin, cnd, grecv, lay, wall, wtr, pg, gacc, csum, ost, gfs, gk, kr, r0, r1, s2, r2,
    sem_fx, sem_fc, sem_send, sem_xh, sem_xm, sem_c, sem_k, sem_km, sem_kr, sem_gm, sem_gv, sem_o, sem_gf, sem_in, sem_r1, sem_pre,
):
    g = lax.axis_index("dp")
    m = lax.axis_index("mp")
    r = RESIDUAL_WIDTH // n
    t = slot // n
    per = t // sub
    blocks = slot // sub
    piece = WIDE // d
    half = n // 2
    band = GH // clips
    h = m // half
    first = h * half
    local = m - first
    worker = jnp.logical_and(m >= half - clips, m < half + clips)
    wc = lax.rem(m + 2 * clips * n - (half - clips), clips)
    mirror = half - clips + (1 - h) * clips + wc
    hub = jnp.logical_and(worker, wc == h)
    shared = (g + 1) * piece <= OUT_AT

    def wid(hh, c):
        return half - clips + hh * clips + c

    def lane(i, size=sub):
        return pl.ds(pl.multiple_of(i, LANES), size)

    def rows(j):
        return pl.ds(pl.multiple_of(j * r, r), r)

    def remote(src, dst, ss, rs, gg, j):
        return pltpu.make_async_remote_copy(
            src_ref=src, dst_ref=dst, send_sem=ss, recv_sem=rs,
            device_id=(gg, j), device_id_type=MESH,
        )

    def others(body):
        if half <= 4:
            for k in range(1, half):
                body(lax.rem(local + k, half))
        else:
            pl.loop(1, half)(lambda k: body(lax.rem(local + k, half)))

    def drain(ref, sem):
        pltpu.make_async_copy(ref, ref, sem).wait()

    def whole(ref, count, sem):
        drain(ref.at[0, :, pl.ds(0, count * piece)] if count <= d else ref.at[:, :, pl.ds(0, count // 2 * piece)], sem)

    projf = gacc.at[pl.ds(0, r), pl.ds(0, proj.shape[1])]
    pltpu.make_async_copy(conv, convf, sem_pre.at[0]).start()
    pltpu.make_async_copy(proj, projf, sem_pre.at[1]).start()

    bar = pltpu.get_barrier_semaphore()

    @pl.loop(1, half)
    def _(k):
        pl.semaphore_signal(bar, inc=1, device_id=(g, first + lax.rem(local + k, half)), device_id_type=MESH)

    @pl.loop(1, d)
    def _(k):
        pl.semaphore_signal(bar, inc=1, device_id=(lax.rem(g + k, d), m), device_id_type=MESH)

    @pl.when(worker)
    def _():
        for c in range(clips):
            pl.semaphore_signal(bar, inc=1, device_id=(g, wid(1 - h, c)), device_id_type=MESH)
        pl.semaphore_wait(bar, half + d - 2 + clips)

    @pl.when(jnp.logical_not(worker))
    def _():
        pl.semaphore_wait(bar, half + d - 2)

    mine = lane(g * piece, piece)

    def laid(hh):
        return lay.at[rows(hh), :]

    def laid_piece(hh):
        return lay.at[rows(hh), mine]
    kept = pl.ds(pl.multiple_of(wc * band, band), band)

    def send_cond(s):
        @pl.when(s // per == m)
        def _():
            dst = cnd.at[pl.ds(0, mel), lane(s * sub)]
            for c in range(clips):
                to = wid(h, c)
                part = cond.at[c, :, lane(s * sub - m * t)]

                @pl.when(to == m)
                def _():
                    pltpu.make_async_copy(part, dst, sem_k.at[s]).start()

                @pl.when(to != m)
                def _():
                    remote(part, dst, sem_send.at[0], sem_k.at[s], g, to).start()

    def later(s):
        return lane(lax.rem(s, blocks // 2) * sub)

    def in_half(s):
        return s // (blocks // 2) == h

    def weights():
        taps = convf.shape[2]
        drain(convf, sem_pre.at[0])
        drain(projf, sem_pre.at[1])
        wide = projf[...]
        turn[...] = jnp.zeros_like(turn)
        turn[0:4, 0:r] = bias[...]
        column = turn[...].T
        spot = lax.broadcasted_iota(jnp.int32, (r, LANES), 1)
        for hh in range(2):
            form = laid(hh)
            for q in range(2):
                base = q * KP
                form[:, base:base + 1024] = convf[q, :, 0:1024].astype(BF)
                form[:, base + 1024:base + KP] = jnp.where(
                    spot == taps - 1024, column[0:r, q:q + 1], 0.0).astype(BF)
                form[:, base + 1024:base + taps] = convf[q, :, 1024:taps].astype(BF)
                form[:, OUT_AT + q * HALF:OUT_AT + (q + 1) * HALF] = wide[
                    :, (2 * q + hh) * HALF:(2 * q + hh + 1) * HALF].astype(BF)
            form[:, USED:USED + LANES] = jnp.where(
                spot == 0, column[0:r, 2:3], jnp.where(spot == 1, column[0:r, 3:4], 0.0)).astype(BF)
            form[:, USED + LANES:] = jnp.zeros((r, WIDE - USED - LANES), BF)

        @pl.when(hub)
        def _():
            pltpu.make_async_copy(laid_piece(h), wall.at[rows(m), mine], sem_in.at[0]).start()
            pltpu.make_async_copy(laid_piece(1 - h), s2.at[rows(local), :], sem_in.at[3]).start()

        @pl.when(jnp.logical_not(hub))
        def _():
            remote(laid_piece(h), wall.at[rows(m), mine], sem_send.at[1], sem_in.at[0], g, wid(h, h)).start()
            remote(laid_piece(1 - h), s2.at[rows(local), :], sem_send.at[1], sem_in.at[3], g, wid(h, h)).start()

    def far():
        def send_x(s):
            at = s * sub

            @pl.when(s >= SLOTS)
            def _():
                drain(x.at[:, :, pl.ds(0, sub)], sem_fx.at[lax.rem(s, SLOTS)])

            for c in range(clips):
                remote(x.at[c, :, lane(at)], xin.at[rows(m), lane(at + LANES)],
                       sem_fx.at[lax.rem(s, SLOTS)], sem_xh.at[s], g, wid(h, c)).start()
            send_cond(s)

        def send_cot(s):
            at = s * sub

            @pl.when(s >= SLOTS)
            def _():
                drain(cot.at[:, :, :, pl.ds(0, sub)], sem_fc.at[lax.rem(s, SLOTS)])

            for c in range(clips):
                remote(cot.at[c, :, :, lane(at)], cin.at[:, rows(local), lane(at)],
                       sem_fc.at[lax.rem(s, SLOTS)], sem_c.at[s], g, wid(h, c)).start()

        pl.loop(0, 1)(send_x)
        weights()
        pl.loop(1, AHEAD)(send_x)

        @pl.loop(0, blocks)
        def _(s):
            @pl.when(s + AHEAD < blocks)
            def _():
                send_x(s + AHEAD)

            send_cot(s)

        @pl.loop(0, SLOTS)
        def _(q):
            drain(x.at[:, :, pl.ds(0, sub)], sem_fx.at[q])
            drain(cot.at[:, :, :, pl.ds(0, sub)], sem_fc.at[q])

    def work():
        def own(s):
            at = s * sub
            for k in range(1, clips):
                c = lax.rem(wc + k, clips)
                remote(x.at[c, :, lane(at)], xin.at[rows(m), lane(at + LANES)],
                       sem_send.at[3], sem_xh.at[s], g, wid(h, c)).start()
                remote(cot.at[c, :, :, lane(at)], cin.at[:, rows(local), lane(at)],
                       sem_send.at[4], sem_c.at[s], g, wid(h, c)).start()
            pltpu.make_async_copy(x.at[wc, :, lane(at)], xin.at[rows(m), lane(at + LANES)], sem_xh.at[s]).start()
            pltpu.make_async_copy(cot.at[wc, :, :, lane(at)], cin.at[:, rows(local), lane(at)], sem_c.at[s]).start()
            send_cond(s)

        here = pl.ds(pl.multiple_of(h * HALF, HALF), HALF)
        there = pl.ds(pl.multiple_of((1 - h) * HALF, HALF), HALF)

        def direct(s):
            at = s * sub
            for k in range(clips):
                c = lax.rem(wc + k, clips)
                remote(x.at[c, :, lane(at)], xin.at[rows(m), lane(at + LANES)],
                       sem_send.at[17], sem_xm.at[s], g, wid(1 - h, c)).start()

        far_rows = pl.ds(pl.multiple_of(h * (HALF + clips * r), r), HALF - clips * r)

        def relay(s):
            part = xin.at[far_rows, lane(s * sub + LANES)]
            drain(xin.at[here, lane(s * sub + LANES)], sem_xh.at[s])
            remote(part, part, sem_send.at[5], sem_xm.at[s], g, mirror).start()

            @pl.when(s + DIRECT < blocks)
            def _():
                direct(s + DIRECT)

            @pl.when(in_half(s))
            def _():
                also = cnd.at[pl.ds(0, mel), lane(s * sub)]
                drain(also, sem_k.at[s])
                remote(also, also, sem_send.at[12], sem_km.at[s], g, mirror).start()

        pl.loop(0, DIRECT)(direct)
        weights()
        pl.loop(0, AHEAD + OWN)(own)

        xin[:, 0:LANES] = jnp.zeros((RESIDUAL_WIDTH, LANES), BF)
        pg[...] = jnp.zeros_like(pg)
        cnd[mel:LANES, :] = (
            lax.broadcasted_iota(jnp.int32, (LANES - mel, slot), 0) == 0
        ).astype(F32).astype(BF)
        gacc[...] = jnp.zeros_like(gacc)
        csum[...] = jnp.zeros_like(csum)

        pl.loop(0, 2)(relay)
        drain(wall.at[kept, mine], sem_in.at[0])

        @pl.when(hub)
        def _():
            drain(s2, sem_in.at[3])
            remote(s2, wall.at[kept, mine], sem_send.at[2], sem_in.at[0], g, mirror).start()

        @pl.loop(1, d)
        def _(k):
            remote(wall.at[kept, mine], wall.at[kept, mine], sem_send.at[6], sem_in.at[1],
                   lax.rem(g + k, d), m).start()

        pl.loop(2, 9)(relay)
        drain(wall.at[kept, pl.ds(0, (d - 1) * piece)], sem_in.at[1])
        for k in range(1, clips):
            remote(wall.at[kept, :], wall.at[kept, :], sem_send.at[7], sem_in.at[2], g,
                   wid(h, lax.rem(wc + k, clips))).start()
        pl.loop(9, AHEAD)(relay)
        drain(wall.at[pl.ds(0, GH - band), :], sem_in.at[2])

        @pl.when(hub)
        def _():
            drain(s2, sem_send.at[2])

        @pl.when(jnp.logical_not(hub))
        def _():
            drain(lay.at[:, mine], sem_send.at[1])


        @pl.loop(0, USED // LANES)
        def _(i):
            wtr[pl.ds(pl.multiple_of(i * LANES, LANES), LANES), :] = wall[:, lane(i * LANES, LANES)].T

        length = lens[wc]

        def back(top):
            win = pg[...]
            pn = win[:, :sub]
            pe = pltpu.roll(win, sub + LANES - DILATION_STEP, 1)[:, :sub]

            def tap(base):
                return wtr[pl.ds(pl.multiple_of(base + top, HALF), HALF), :]

            return (dot(tap(512), pn[0:512]) + dot(wtr[pl.ds(pl.multiple_of(KP + 512 + top, LANES), HALF), :], pn[512:1024])
                    + dot(tap(0), pe[0:512]) + dot(wtr[pl.ds(pl.multiple_of(KP + top, LANES), HALF), :], pe[512:1024]))

        def gone(q):
            drain(cin.at[1, :, pl.ds(0, sub)], sem_gv.at[lax.rem(q, POSTS)])

        def give(q):
            remote(cin.at[1, :, lane(q * sub)], grecv.at[:, lane(q * sub)],
                   sem_gv.at[lax.rem(q, POSTS)], sem_gm.at[q], g, mirror).start()

        def add_cond(s):
            now = lane(s * sub)
            keeper = s // per
            spot = gco.at[wc, :, lane(s * sub - keeper * t)]
            drain(kr.at[:, later(s)], sem_kr.at[s])
            gk[:, now] = (gk[:, now].astype(F32) + kr[:, later(s)].astype(F32)).astype(BF)

            @pl.when(keeper == m)
            def _():
                pltpu.make_async_copy(gk.at[:, now], spot, sem_send.at[13]).start()

            @pl.when(keeper != m)
            def _():
                remote(gk.at[:, now], spot, sem_send.at[14], sem_in.at[6], g, keeper).start()

        def combine(q):
            now = lane(q * sub)
            z = lax.rem(q, SLOTS)
            drain(grecv.at[:, now], sem_gm.at[q])

            @pl.when(q >= SLOTS)
            def _():
                drain(gfs.at[z], sem_gf.at[z])

            gfs[z] = (cin[0, :, now].astype(F32) + grecv[:, now].astype(F32)).astype(BF)

            @others
            def _(i):
                remote(gfs.at[z, rows(i), :], gio.at[wc, :, now], sem_gf.at[z], sem_in.at[5], g, first + i).start()

            pltpu.make_async_copy(gfs.at[z, rows(local), :], gio.at[wc, :, now], sem_gf.at[z]).start()

        def send_results(s):
            now = lane(s * sub)
            z = lax.rem(s, SLOTS)

            @others
            def _(i):
                remote(ost.at[z, :, rows(i), :], bro.at[wc, :, :, now], sem_o.at[z], sem_in.at[10], g, first + i).start()

            pltpu.make_async_copy(ost.at[z, :, rows(local), :], bro.at[wc, :, :, now], sem_o.at[z]).start()

            @pl.when(jnp.logical_not(in_half(s)))
            def _():
                remote(gk.at[:, now], kr.at[:, later(s)], sem_send.at[8], sem_kr.at[s], g, mirror).start()

        @pl.loop(0, blocks)
        def _(s):
            at = s * sub
            now = lane(at)
            off = lane(at + LANES)
            z = lax.rem(s, SLOTS)

            @pl.when(s + AHEAD + OWN < blocks)
            def _():
                own(s + AHEAD + OWN)

            @pl.when(s + AHEAD < blocks)
            def _():
                relay(s + AHEAD)

            @pl.when(s >= 1)
            def _():
                send_results(s - 1)

            @pl.when(s >= GIVE + POSTS)
            def _():
                gone(s - GIVE - POSTS)

            @pl.when(s >= GIVE)
            def _():
                give(s - GIVE)

            @pl.when(s >= GIVE + LAG)
            def _():
                combine(s - GIVE - LAG)

            @pl.when(jnp.logical_and(s >= LATE, in_half(s - LATE)))
            def _():
                add_cond(s - LATE)

            @pl.when(jnp.logical_not(in_half(s)))
            def _():
                drain(cnd.at[pl.ds(0, mel), now], sem_km.at[s])

            @pl.when(s >= SLOTS)
            def _():
                drain(ost.at[z], sem_o.at[z])

            drain(xin.at[there, off], sem_xm.at[s])
            drain(cin.at[:, :, now], sem_c.at[s])

            xc = xin[:, off]
            xe = pltpu.roll(xin[:, lane(at, sub + LANES)], DILATION_STEP, 1)[:, LANES:]
            cd = cnd[:, now]
            pre_f = (dot(wall[:, 0:512], xe) + dot(wall[:, 512:1024], xc) + dot(wall[:, 1024:KP], cd))
            pre_g = (dot(wall[:, KP:KP + 512], xe) + dot(wall[:, KP + 512:KP + 1024], xc)
                     + dot(wall[:, KP + 1024:OUT_AT], cd))
            place = at + lax.broadcasted_iota(jnp.int32, (1, sub), 1)
            keep = (place < length).astype(F32)
            th = jnp.tanh(pre_f)
            sg = jax.nn.sigmoid(pre_g)
            hid = (keep * th * sg).astype(BF)
            branch = dot(wtr[OUT_AT:USED, :], hid)
            offset = wall[here, USED:USED + LANES].astype(F32)
            ost[z, 0] = (xin[here, off].astype(F32) + branch[0:HALF] + offset[:, 0:1]).astype(BF)
            ost[z, 1] = (branch[HALF:] + offset[:, 1:2]).astype(BF)
            ct = cin[:, :, now].reshape(2 * HALF, sub)
            for q in range(sub // LANES):
                csum[...] += ct[:, q * LANES:(q + 1) * LANES].astype(F32)
            hg = dot(wall[:, OUT_AT:USED], ct) * keep
            pgf = (hg * sg * (1.0 - th * th)).astype(BF)
            pgg = (hg * th * sg * (1.0 - sg)).astype(BF)
            pg[0:512, sub:] = pgf[:, :LANES]
            pg[512:1024, sub:] = pgg[:, :LANES]
            gacc[:, 0:512] += dot_nt(pgf, xe)
            gacc[:, 512:1024] += dot_nt(pgf, xc)
            gacc[:, 1024:KP] += dot_nt(pgf, cd)
            gacc[:, KP:KP + 512] += dot_nt(pgg, xe)
            gacc[:, KP + 512:KP + 1024] += dot_nt(pgg, xc)
            gacc[:, KP + 1024:OUT_AT] += dot_nt(pgg, cd)
            gacc[:, OUT_AT:USED] += dot_nt(hid, ct)
            gk[:, now] = (dot(wtr[1024:KP, :], pgf) + dot(wtr[KP + 1024:OUT_AT, :], pgg))[0:mel].astype(BF)
            before = lane(jnp.maximum(s - 1, 0) * sub)
            cin[1, :, before] = back((1 - h) * HALF).astype(BF)
            cin[0, :, before] = back(h * HALF).astype(BF)
            pg[0:512, 0:sub] = pgf
            pg[512:1024, 0:sub] = pgg

        send_results(blocks - 1)
        pg[:, sub:] = jnp.zeros((2 * GH, LANES), BF)
        cin[1, :, pl.ds(slot - sub, sub)] = back((1 - h) * HALF).astype(BF)
        cin[0, :, pl.ds(slot - sub, sub)] = back(h * HALF).astype(BF)

        def spread(part, dst, sem):
            @others
            def _(i):
                remote(part.at[rows(i), :], dst, sem, sem_in.at[8], g, first + i).start()

            pltpu.make_async_copy(part.at[rows(local), :], dst, sem_in.at[8]).start()

        spot = lax.broadcasted_iota(jnp.int32, (HALF, LANES), 1)
        total = jnp.sum(csum[...], axis=1, keepdims=True)
        gacc[here, USED:USED + LANES] = jnp.where(spot == 0, total[0:HALF], jnp.where(spot == 1, total[HALF:], 0.0))

        drain(xin.at[pl.ds(0, HALF - clips * r), pl.ds(0, slot)], sem_send.at[5])
        s0 = xin.at[pl.ds(0, band), pl.ds(0, WIDE)]
        for k in range(1, clips):
            to = lax.rem(wc + k, clips)
            s0[...] = gacc[pl.ds(pl.multiple_of(to * band, band), band), :].astype(BF)
            remote(s0, r0.at[k - 1], sem_send.at[9], sem_in.at[7], g, wid(h, to)).start()

        start = blocks - GIVE
        pl.loop(start - POSTS, start - SLOTS)(gone)

        def tail(q):
            gone(q - SLOTS)
            give(q)
            combine(q - LAG)
            more = q + GIVE - LATE

            @pl.when(jnp.logical_and(more < blocks, in_half(more)))
            def _():
                add_cond(more)

        pl.loop(start, start + 2)(tail)
        drain(r0, sem_in.at[7])
        for k in range(1, clips):
            gacc[kept, :] += r0[k - 1].astype(F32)

        @pl.loop(1, d)
        def _(k):
            to = lax.rem(g + k, d)
            src = xin.at[pl.ds(GH - band, band), lane((k - 1) * piece, piece)]
            src[...] = gacc[kept, lane(to * piece, piece)].astype(BF)
            remote(src, r1.at[k - 1], sem_send.at[10], sem_r1.at[k - 1], to, m).start()

        pl.loop(start + 2, start + 7)(tail)

        @pl.loop(1, d)
        def _(k):
            drain(r1.at[k - 1], sem_r1.at[k - 1])
            gacc[kept, mine] += r1[k - 1].astype(F32)

        s2[...] = gacc[kept, mine].astype(BF)

        @pl.when(jnp.logical_not(hub))
        def _():
            remote(s2, r2, sem_send.at[11], sem_in.at[4], g, mirror).start()

        pl.loop(start + 7, start + 13)(tail)

        @pl.when(hub)
        def _():
            drain(r2, sem_in.at[4])

            @pl.when(shared)
            def _():
                s2[...] = (gacc[kept, mine] + r2[...].astype(F32)).astype(BF)
                spread(s2, gw.at[0, :, mine], sem_send.at[11])

            @pl.when(jnp.logical_not(shared))
            def _():
                spread(s2, gw.at[h, :, mine], sem_send.at[11])
                spread(r2, gw.at[1 - h, :, mine], sem_send.at[15])

        pl.loop(start + 13, blocks)(tail)
        share_out()
        pl.loop(blocks - SLOTS, blocks)(gone)
        pl.loop(blocks - LAG, blocks)(combine)

        @pl.loop(0, SLOTS)
        def _(q):
            drain(ost.at[q], sem_o.at[q])
            drain(gfs.at[q], sem_gf.at[q])

        drain(x.at[pl.ds(0, clips - 1)], sem_send.at[3])
        drain(cot.at[pl.ds(0, clips - 1)], sem_send.at[4])
        drain(x, sem_send.at[17])
        drain(wall.at[kept, pl.ds(0, (d - 1) * piece)], sem_send.at[6])
        drain(wall.at[pl.ds(0, GH - band), :], sem_send.at[7])
        drain(gk.at[:, pl.ds(0, slot // 2)], sem_send.at[8])
        drain(cnd.at[pl.ds(0, mel), pl.ds(0, slot // 2)], sem_send.at[12])
        drain(gk.at[:, pl.ds(0, t)], sem_send.at[13])
        drain(gk.at[:, pl.ds(0, slot // 2 - t)], sem_send.at[14])
        drain(r0, sem_send.at[9])
        drain(r1, sem_send.at[10])

    def share_out():
        @pl.when(shared)
        def _():
            drain(gw.at[0, :, mine], sem_in.at[8])
            share(gw.at[0, :, mine])

        @pl.when(jnp.logical_not(shared))
        def _():
            drain(gw.at[:, :, mine], sem_in.at[8])
            share(gw.at[:, :, mine])

    def share(part):
        @pl.loop(1, d)
        def _(k):
            remote(part, part, sem_send.at[16], sem_in.at[9], lax.rem(g + k, d), m).start()

    @pl.when(worker)
    def _():
        work()
        drain(cond.at[pl.ds(0, clips - 1)], sem_send.at[0])
        drain(bro.at[pl.ds(0, clips - 1)], sem_in.at[10])
        drain(gio.at[pl.ds(0, clips - 1)], sem_in.at[5])
        drain(gco.at[pl.ds(0, clips - 1)], sem_in.at[6])

        @pl.when(hub)
        def _():
            drain(s2.at[pl.ds(0, HALF - r), :], sem_send.at[11])

            @pl.when(jnp.logical_not(shared))
            def _():
                drain(r2.at[pl.ds(0, HALF - r), :], sem_send.at[15])

        @pl.when(jnp.logical_not(hub))
        def _():
            drain(s2, sem_send.at[11])

    @pl.when(jnp.logical_not(worker))
    def _():
        far()
        share_out()
        drain(cond, sem_send.at[0])
        drain(lay.at[:, mine], sem_send.at[1])
        drain(bro, sem_in.at[10])
        drain(gio, sem_in.at[5])
        drain(gco, sem_in.at[6])

    own_piece = 2 * d - OUT_AT // piece

    @pl.when(shared)
    def _():
        whole(gw, own_piece - 1, sem_in.at[9])
        whole(gw, d - 1, sem_send.at[16])

    @pl.when(jnp.logical_not(shared))
    def _():
        whole(gw, own_piece - 2, sem_in.at[9])
        whole(gw, 2 * (d - 1), sem_send.at[16])


def run_layer(n, d, x, cot, cond, lens, conv, proj, bias):
    clips, r, slot = x.shape
    mel = cond.shape[1]
    t = slot // n
    sub = min(256, t)
    blocks = slot // sub
    piece = WIDE // d
    width = RESIDUAL_WIDTH
    band = GH // clips
    any_spec = pl.BlockSpec(memory_space=pltpu.HBM)
    vmem = pl.BlockSpec(memory_space=pltpu.VMEM)
    smem = pl.BlockSpec(memory_space=pltpu.SMEM)
    dma = pltpu.SemaphoreType.DMA
    return pl.pallas_call(
        functools.partial(layer_kernel, n, d, clips, slot, sub, mel),
        out_shape=(
            jax.ShapeDtypeStruct((clips, 2, r, slot), BF),
            jax.ShapeDtypeStruct((clips, r, slot), BF),
            jax.ShapeDtypeStruct((clips, mel, t), BF),
            jax.ShapeDtypeStruct((2, r, WIDE), BF),
        ),
        in_specs=[any_spec, any_spec, any_spec, smem, any_spec, any_spec, vmem],
        out_specs=(pl.BlockSpec(memory_space=pl.ANY),) * 3 + (vmem,),
        scratch_shapes=[
            pltpu.VMEM(conv.shape, F32),
            pltpu.VMEM((8, LANES), F32),
            pltpu.VMEM((width, LANES + slot), BF),
            pltpu.VMEM((2, HALF, slot), BF),
            pltpu.VMEM((LANES, slot), BF),
            pltpu.VMEM((HALF, slot), BF),
            pltpu.VMEM((2 * r, WIDE), BF),
            pltpu.VMEM((GH, WIDE), BF),
            pltpu.VMEM((USED, GH), BF),
            pltpu.VMEM((2 * GH, sub + LANES), BF),
            pltpu.VMEM((GH, WIDE), F32),
            pltpu.VMEM((2 * HALF, LANES), F32),
            pltpu.VMEM((SLOTS, 2, HALF, sub), BF),
            pltpu.VMEM((SLOTS, HALF, sub), BF),
            pltpu.VMEM((mel, slot), BF),
            pltpu.VMEM((mel, slot // 2), BF),
            pltpu.VMEM((clips - 1, band, WIDE), BF),
            pltpu.VMEM((d - 1, band, piece), BF),
            pltpu.VMEM((band, piece), BF),
            pltpu.VMEM((band, piece), BF),
            dma((SLOTS,)),
            dma((SLOTS,)),
            dma((18,)),
            dma((blocks,)),
            dma((blocks,)),
            dma((blocks,)),
            dma((blocks,)),
            dma((blocks,)),
            dma((blocks,)),
            dma((blocks,)),
            dma((POSTS,)),
            dma((SLOTS,)),
            dma((SLOTS,)),
            dma((11,)),
            dma((d - 1,)),
            dma((2,)),
        ],
        compiler_params=pltpu.CompilerParams(
            collective_id=0, has_side_effects=True, vmem_limit_bytes=52 << 20
        ),
    )(x, cot, cond, lens, conv, proj, bias)


def adamw(master, first_old, second_old, gradient, step_rate, power_one, power_two):
    first_new = BETA_ONE * first_old + (1.0 - BETA_ONE) * gradient
    second_new = BETA_TWO * second_old + (1.0 - BETA_TWO) * gradient * gradient
    first_hat = first_new / (1.0 - power_one)
    second_hat = second_new / (1.0 - power_two)
    renewed = master - step_rate * (
        first_hat / (jnp.sqrt(second_hat) + EPSILON) + WEIGHT_DECAY * master
    )
    return (renewed, first_new, second_new)


def finish_kernel(
    taps, span,
    lo, gio, cot, gco, gw, cw, cm, cv, ow, om, ov, bw, bm, bv,
    lo_out, gi_out, gc_out, cw_out, ow_out, bw_out, cm_out, om_out, bm_out, cv_out, ov_out, bv_out,
    cl_out, ol_out, bl_out,
    lo_v, gio_v, cot_v, gi_v, gco_v, gc_v, gw_v, conv_v, convl_v, proj_v, projl_v,
    sem_lo, sem_gi, sem_cot, sem_small, sem_out,
):
    clips, r, slot = gio.shape
    parts = slot // span
    power_one = jnp.float32(BETA_ONE**STEP)
    power_two = jnp.float32(BETA_TWO**STEP)

    small = [
        pltpu.make_async_copy(src, dst, sem_small.at[i])
        for i, (src, dst) in enumerate(
            [(gw, gw_v), (gco, gco_v)]
            + [(a, conv_v.at[q]) for q, a in enumerate((cw, cm, cv))]
            + [(a, proj_v.at[q]) for q, a in enumerate((ow, om, ov))]
        )
    ]
    blocks = [(c, slice(p * span, (p + 1) * span)) for c in range(clips) for p in range(parts)]
    loads = [
        (
            pltpu.make_async_copy(gio.at[c, :, at], gio_v.at[c, :, at], sem_gi.at[i]),
            pltpu.make_async_copy(cot.at[c, 0, :, at], cot_v.at[c, :, at], sem_cot.at[i]),
            pltpu.make_async_copy(lo.at[c, :, :, at], lo_v.at[c, :, :, at], sem_lo.at[i]),
        )
        for i, (c, at) in enumerate(blocks)
    ]
    for copy in small[:5]:
        copy.start()
    for load in loads[:2]:
        for copy in load:
            copy.start()
    for copy in small[5:]:
        copy.start()
    for load in loads[2:]:
        for copy in load:
            copy.start()

    stores = []

    def store(src, dst):
        copy = pltpu.make_async_copy(src, dst, sem_out.at[len(stores)])
        copy.start()
        stores.append(copy)

    def block(i):
        c, at = blocks[i]
        one, two, three = loads[i]
        three.wait()
        store(lo_v.at[c, :, :, at], lo_out.at[c, :, :, at])
        one.wait()
        two.wait()
        gi_v[c, :, at] = cot_v[c, :, at].astype(F32) + gio_v[c, :, at].astype(F32)
        store(gi_v.at[c, :, at], gi_out.at[c, :, at])

    block(0)
    for copy in small[:5]:
        copy.wait()
    gc_v[...] = gco_v[...].astype(F32)
    store(gc_v, gc_out)
    for q in range(2):
        w, m, v = adamw(conv_v[0, q], conv_v[1, q], conv_v[2, q], gw_v[0, :, q * KP:q * KP + taps].astype(F32),
                        CONV_RATE, power_one, power_two)
        conv_v[0, q], conv_v[1, q], conv_v[2, q] = w, m, v
        convl_v[q] = w.astype(BF)
    for i, dst in enumerate((cw_out, cm_out, cv_out)):
        store(conv_v.at[i], dst)
    store(convl_v, cl_out)
    block(1)
    for copy in small[5:]:
        copy.wait()
    for q in range(4):
        at = slice(q * HALF, (q + 1) * HALF)
        from_at = OUT_AT + q // 2 * HALF
        w, m, v = adamw(proj_v[0, :, at], proj_v[1, :, at], proj_v[2, :, at],
                        gw_v[q % 2, :, from_at:from_at + HALF].astype(F32), OUT_RATE, power_one, power_two)
        proj_v[0, :, at], proj_v[1, :, at], proj_v[2, :, at] = w, m, v
        projl_v[:, at] = w.astype(BF)
    for i, dst in enumerate((ow_out, om_out, ov_out)):
        store(proj_v.at[i], dst)
    store(projl_v, ol_out)
    spot = lax.broadcasted_iota(jnp.int32, (r, LANES), 1)
    last = taps - 1024
    sums = gw_v[0, :, USED:USED + LANES].astype(F32) + gw_v[1, :, USED:USED + LANES].astype(F32)
    columns = (
        gw_v[0, :, 1024:KP].astype(F32)[:, last:last + 1],
        gw_v[0, :, KP + 1024:OUT_AT].astype(F32)[:, last:last + 1],
        sums[:, 0:1],
        sums[:, 1:2],
    )
    table = jnp.zeros((r, LANES), F32)
    for i, column in enumerate(columns):
        table = jnp.where(spot == i, column, table)
    w, m, v = adamw(bw[...], bm[...], bv[...], table.T[0:4], BIAS_RATE, power_one, power_two)
    bw_out[...], bm_out[...], bv_out[...] = w, m, v
    bl_out[...] = w.astype(BF)
    for i in range(2, len(blocks)):
        block(i)
    for copy in stores:
        copy.wait()


def finish(lo, gio, cot, gco, gw, conv, proj, bias):
    clips, r, slot = gio.shape
    taps = conv[0].shape[2]
    span = 2048
    count = clips * (slot // span)
    any_spec = pl.BlockSpec(memory_space=pltpu.HBM)
    vmem = pl.BlockSpec(memory_space=pltpu.VMEM)
    dma = pltpu.SemaphoreType.DMA

    def like(a, dtype=None):
        return jax.ShapeDtypeStruct(a.shape, dtype or a.dtype)

    trio = [like(conv[0]), like(proj[0]), like(bias[0])]
    return pl.pallas_call(
        functools.partial(finish_kernel, taps, span),
        out_shape=[like(lo), like(gio, F32), like(gco, F32)] + trio * 3
        + [like(a, BF) for a in (conv[0], proj[0], bias[0])],
        in_specs=[any_spec] * 11 + [vmem] * 3,
        out_specs=[any_spec] * 3 + [any_spec, any_spec, vmem] * 4,
        scratch_shapes=[
            pltpu.VMEM(lo.shape, BF),
            pltpu.VMEM(gio.shape, BF),
            pltpu.VMEM(gio.shape, BF),
            pltpu.VMEM(gio.shape, F32),
            pltpu.VMEM(gco.shape, BF),
            pltpu.VMEM(gco.shape, F32),
            pltpu.VMEM(gw.shape, BF),
            pltpu.VMEM((3, *conv[0].shape), F32),
            pltpu.VMEM(conv[0].shape, BF),
            pltpu.VMEM((3, *proj[0].shape), F32),
            pltpu.VMEM(proj[0].shape, BF),
            dma((count,)),
            dma((count,)),
            dma((count,)),
            dma((8,)),
            dma((2 * count + 9,)),
        ],
        compiler_params=pltpu.CompilerParams(vmem_limit_bytes=24 << 20),
    )(lo, gio, cot, gco, gw, *conv, *proj, *bias)


def per_device(
    n, d,
    inputs, conditioning, lengths, cotangent, conv_weight, out_weight, biases,
    conv_first, out_first, bias_first, conv_second, out_second, bias_second,
):
    conv = [jnp.transpose(a, (1, 2, 0)) for a in (conv_weight, conv_first, conv_second)]
    proj = [out_weight, out_first, out_second]
    bias = [biases, bias_first, bias_second]
    cond = jnp.transpose(conditioning, (0, 2, 1))
    def pinned(a):
        return pltpu.with_memory_space_constraint(a, pltpu.HBM)

    lo, gio, gco, gw = run_layer(
        n, d, pinned(inputs), pinned(cotangent), pinned(cond), pinned(lengths), pinned(conv[0]), pinned(proj[0]), pinned(bias[0])
    )
    lo, gio = pinned(lo), pinned(gio)
    outs = finish(lo, gio, cotangent, gco, gw, conv, proj, bias)
    layer_out, grad_input, grad_cond = outs[:3]
    news = [jnp.transpose(a, (2, 0, 1)) if i % 3 == 0 else a for i, a in enumerate(outs[3:])]
    return (layer_out, grad_input, jnp.transpose(grad_cond, (0, 2, 1)), *news)


def solution(mesh):
    in_specs = (
        P("dp", "mp", None),
        P("dp", "mp", None),
        P("dp"),
        P("dp", None, "mp", None),
        P(None, None, "mp"),
        P("mp", None),
        P(None, "mp"),
        P(None, None, "mp"),
        P("mp", None),
        P(None, "mp"),
        P(None, None, "mp"),
        P("mp", None),
        P(None, "mp"),
    )
    out_specs = (
        P("dp", None, "mp", None),
        P("dp", "mp", None),
        P("dp", "mp", None),
        P(None, None, "mp"),
        P("mp", None),
        P(None, "mp"),
        P(None, None, "mp"),
        P("mp", None),
        P(None, "mp"),
        P(None, None, "mp"),
        P("mp", None),
        P(None, "mp"),
        P(None, None, "mp"),
        P("mp", None),
        P(None, "mp"),
    )
    return jax.shard_map(
        functools.partial(per_device, mesh.shape["mp"], mesh.shape["dp"]),
        mesh=mesh, in_specs=in_specs, out_specs=out_specs, check_vma=False,
    )
```

```python
import functools

import jax
import jax.numpy as jnp
from jax import lax
from jax.experimental import pallas as pl
from jax.experimental.pallas import tpu as pltpu
from jax.sharding import PartitionSpec as P

RESIDUAL_WIDTH = 512
GH = 512
DILATION_STEP = 32
STEP = 4

BETA_ONE = 0.5
BETA_TWO = 0.5
EPSILON = 1e-08
WEIGHT_DECAY = 0.01
CONV_RATE = 0.03
OUT_RATE = 0.1
BIAS_RATE = 0.3

MESH = pl.DeviceIdType.MESH
LANES = 128
HALF = RESIDUAL_WIDTH // 2
KP = 1152
OUT_AT = 2 * KP
USED = OUT_AT + 2 * HALF
WIDE = 3072
AHEAD = 16
OWN = 6
DIRECT = 6
GIVE = 14
LAG = 6
SLOTS = 4
LATE = 12
POSTS = 8
BF = jnp.bfloat16
F32 = jnp.float32


def dot(a, b):
    return jnp.dot(a, b, preferred_element_type=F32)


def dot_nt(a, b):
    return lax.dot_general(a, b, (((1,), (1,)), ((), ())), preferred_element_type=F32)


def layer_kernel(
    n, d, clips, slot, sub, mel,
    x, cot, cond, lens, conv, proj, bias,
    bro, gio, gco, gw,
    convf, turn, xin, cin, cnd, grecv, lay, wall, wtr, pg, gacc, csum, ost, gfs, gk, kr, r0, r1, s2, r2,
    sem_fx, sem_fc, sem_send, sem_xh, sem_xm, sem_c, sem_k, sem_km, sem_kr, sem_gm, sem_gv, sem_o, sem_gf, sem_in, sem_r1, sem_pre,
):
    g = lax.axis_index("dp")
    m = lax.axis_index("mp")
    r = RESIDUAL_WIDTH // n
    t = slot // n
    per = t // sub
    blocks = slot // sub
    piece = WIDE // d
    half = n // 2
    band = GH // clips
    h = m // half
    first = h * half
    local = m - first
    worker = jnp.logical_and(m >= half - clips, m < half + clips)
    wc = lax.rem(m + 2 * clips * n - (half - clips), clips)
    mirror = half - clips + (1 - h) * clips + wc
    hub = jnp.logical_and(worker, wc == h)
    shared = (g + 1) * piece <= OUT_AT

    def wid(hh, c):
        return half - clips + hh * clips + c

    def lane(i, size=sub):
        return pl.ds(pl.multiple_of(i, LANES), size)

    def rows(j):
        return pl.ds(pl.multiple_of(j * r, r), r)

    def remote(src, dst, ss, rs, gg, j):
        return pltpu.make_async_remote_copy(
            src_ref=src, dst_ref=dst, send_sem=ss, recv_sem=rs,
            device_id=(gg, j), device_id_type=MESH,
        )

    def others(body):
        if half <= 4:
            for k in range(1, half):
                body(lax.rem(local + k, half))
        else:
            pl.loop(1, half)(lambda k: body(lax.rem(local + k, half)))

    def drain(ref, sem):
        pltpu.make_async_copy(ref, ref, sem).wait()

    def whole(ref, count, sem):
        drain(ref.at[0, :, pl.ds(0, count * piece)] if count <= d else ref.at[:, :, pl.ds(0, count // 2 * piece)], sem)

    projf = gacc.at[pl.ds(0, r), pl.ds(0, proj.shape[1])]
    pltpu.make_async_copy(conv, convf, sem_pre.at[0]).start()
    pltpu.make_async_copy(proj, projf, sem_pre.at[1]).start()

    bar = pltpu.get_barrier_semaphore()

    @pl.loop(1, half)
    def _(k):
        pl.semaphore_signal(bar, inc=1, device_id=(g, first + lax.rem(local + k, half)), device_id_type=MESH)

    @pl.loop(1, d)
    def _(k):
        pl.semaphore_signal(bar, inc=1, device_id=(lax.rem(g + k, d), m), device_id_type=MESH)

    @pl.when(worker)
    def _():
        for c in range(clips):
            pl.semaphore_signal(bar, inc=1, device_id=(g, wid(1 - h, c)), device_id_type=MESH)
        pl.semaphore_wait(bar, half + d - 2 + clips)

    @pl.when(jnp.logical_not(worker))
    def _():
        pl.semaphore_wait(bar, half + d - 2)

    mine = lane(g * piece, piece)

    def laid(hh):
        return lay.at[rows(hh), :]

    def laid_piece(hh):
        return lay.at[rows(hh), mine]
    kept = pl.ds(pl.multiple_of(wc * band, band), band)

    def send_cond(s):
        @pl.when(s // per == m)
        def _():
            dst = cnd.at[pl.ds(0, mel), lane(s * sub)]
            for c in range(clips):
                to = wid(h, c)
                part = cond.at[c, :, lane(s * sub - m * t)]

                @pl.when(to == m)
                def _():
                    pltpu.make_async_copy(part, dst, sem_k.at[s]).start()

                @pl.when(to != m)
                def _():
                    remote(part, dst, sem_send.at[0], sem_k.at[s], g, to).start()

    def later(s):
        return lane(lax.rem(s, blocks // 2) * sub)

    def in_half(s):
        return s // (blocks // 2) == h

    def weights():
        taps = convf.shape[2]
        drain(convf, sem_pre.at[0])
        drain(projf, sem_pre.at[1])
        wide = projf[...]
        turn[...] = jnp.zeros_like(turn)
        turn[0:4, 0:r] = bias[...]
        column = turn[...].T
        spot = lax.broadcasted_iota(jnp.int32, (r, LANES), 1)
        for hh in range(2):
            form = laid(hh)
            for q in range(2):
                base = q * KP
                form[:, base:base + 1024] = convf[q, :, 0:1024].astype(BF)
                form[:, base + 1024:base + KP] = jnp.where(
                    spot == taps - 1024, column[0:r, q:q + 1], 0.0).astype(BF)
                form[:, base + 1024:base + taps] = convf[q, :, 1024:taps].astype(BF)
                form[:, OUT_AT + q * HALF:OUT_AT + (q + 1) * HALF] = wide[
                    :, (2 * q + hh) * HALF:(2 * q + hh + 1) * HALF].astype(BF)
            form[:, USED:USED + LANES] = jnp.where(
                spot == 0, column[0:r, 2:3], jnp.where(spot == 1, column[0:r, 3:4], 0.0)).astype(BF)
            form[:, USED + LANES:] = jnp.zeros((r, WIDE - USED - LANES), BF)

        @pl.when(hub)
        def _():
            pltpu.make_async_copy(laid_piece(h), wall.at[rows(m), mine], sem_in.at[0]).start()
            pltpu.make_async_copy(laid_piece(1 - h), s2.at[rows(local), :], sem_in.at[3]).start()

        @pl.when(jnp.logical_not(hub))
        def _():
            remote(laid_piece(1 - h), s2.at[rows(local), :], sem_send.at[1], sem_in.at[3], g, wid(h, h)).start()
            remote(laid_piece(h), wall.at[rows(m), mine], sem_send.at[1], sem_in.at[0], g, wid(h, h)).start()

    def far():
        def send_x(s):
            at = s * sub

            @pl.when(s >= SLOTS)
            def _():
                drain(x.at[:, :, pl.ds(0, sub)], sem_fx.at[lax.rem(s, SLOTS)])

            for c in range(clips):
                remote(x.at[c, :, lane(at)], xin.at[rows(m), lane(at + LANES)],
                       sem_fx.at[lax.rem(s, SLOTS)], sem_xh.at[s], g, wid(h, c)).start()
            send_cond(s)

        def send_cot(s):
            at = s * sub

            @pl.when(s >= SLOTS)
            def _():
                drain(cot.at[:, :, :, pl.ds(0, sub)], sem_fc.at[lax.rem(s, SLOTS)])

            for c in range(clips):
                remote(cot.at[c, :, :, lane(at)], cin.at[:, rows(local), lane(at)],
                       sem_fc.at[lax.rem(s, SLOTS)], sem_c.at[s], g, wid(h, c)).start()

        pl.loop(0, 1)(send_x)
        weights()
        pl.loop(1, AHEAD)(send_x)

        @pl.loop(0, blocks)
        def _(s):
            @pl.when(s + AHEAD < blocks)
            def _():
                send_x(s + AHEAD)

            send_cot(s)

        @pl.loop(0, SLOTS)
        def _(q):
            drain(x.at[:, :, pl.ds(0, sub)], sem_fx.at[q])
            drain(cot.at[:, :, :, pl.ds(0, sub)], sem_fc.at[q])

    def work():
        def own(s):
            at = s * sub
            for k in range(1, clips):
                c = lax.rem(wc + k, clips)
                remote(x.at[c, :, lane(at)], xin.at[rows(m), lane(at + LANES)],
                       sem_send.at[3], sem_xh.at[s], g, wid(h, c)).start()
                remote(cot.at[c, :, :, lane(at)], cin.at[:, rows(local), lane(at)],
                       sem_send.at[4], sem_c.at[s], g, wid(h, c)).start()
            pltpu.make_async_copy(x.at[wc, :, lane(at)], xin.at[rows(m), lane(at + LANES)], sem_xh.at[s]).start()
            pltpu.make_async_copy(cot.at[wc, :, :, lane(at)], cin.at[:, rows(local), lane(at)], sem_c.at[s]).start()
            send_cond(s)

        here = pl.ds(pl.multiple_of(h * HALF, HALF), HALF)
        there = pl.ds(pl.multiple_of((1 - h) * HALF, HALF), HALF)

        def direct(s):
            at = s * sub
            for k in range(clips):
                c = lax.rem(wc + k, clips)
                remote(x.at[c, :, lane(at)], xin.at[rows(m), lane(at + LANES)],
                       sem_send.at[17], sem_xm.at[s], g, wid(1 - h, c)).start()

        far_rows = pl.ds(pl.multiple_of(h * (HALF + clips * r), r), HALF - clips * r)

        def relay(s):
            part = xin.at[far_rows, lane(s * sub + LANES)]
            drain(xin.at[here, lane(s * sub + LANES)], sem_xh.at[s])
            remote(part, part, sem_send.at[5], sem_xm.at[s], g, mirror).start()

            @pl.when(s + DIRECT < blocks)
            def _():
                direct(s + DIRECT)

            @pl.when(in_half(s))
            def _():
                also = cnd.at[pl.ds(0, mel), lane(s * sub)]
                drain(also, sem_k.at[s])
                remote(also, also, sem_send.at[12], sem_km.at[s], g, mirror).start()

        pl.loop(0, DIRECT)(direct)
        weights()
        pl.loop(0, AHEAD + OWN)(own)

        xin[:, 0:LANES] = jnp.zeros((RESIDUAL_WIDTH, LANES), BF)
        pg[...] = jnp.zeros_like(pg)
        cnd[mel:LANES, :] = (
            lax.broadcasted_iota(jnp.int32, (LANES - mel, slot), 0) == 0
        ).astype(F32).astype(BF)
        gacc[...] = jnp.zeros_like(gacc)
        csum[...] = jnp.zeros_like(csum)

        pl.loop(0, 2)(relay)

        @pl.when(hub)
        def _():
            drain(s2, sem_in.at[3])
            remote(s2, wall.at[kept, mine], sem_send.at[2], sem_in.at[0], g, mirror).start()

        drain(wall.at[kept, mine], sem_in.at[0])

        @pl.loop(1, d)
        def _(k):
            remote(wall.at[kept, mine], wall.at[kept, mine], sem_send.at[6], sem_in.at[1],
                   lax.rem(g + k, d), m).start()

        pl.loop(2, 9)(relay)
        drain(wall.at[kept, pl.ds(0, (d - 1) * piece)], sem_in.at[1])
        for k in range(1, clips):
            remote(wall.at[kept, :], wall.at[kept, :], sem_send.at[7], sem_in.at[2], g,
                   wid(h, lax.rem(wc + k, clips))).start()
        pl.loop(9, AHEAD)(relay)
        drain(wall.at[pl.ds(0, GH - band), :], sem_in.at[2])

        @pl.when(hub)
        def _():
            drain(s2, sem_send.at[2])

        @pl.when(jnp.logical_not(hub))
        def _():
            drain(lay.at[:, mine], sem_send.at[1])


        @pl.loop(0, USED // LANES)
        def _(i):
            wtr[pl.ds(pl.multiple_of(i * LANES, LANES), LANES), :] = wall[:, lane(i * LANES, LANES)].T

        length = lens[wc]

        def back(top):
            win = pg[...]
            pn = win[:, :sub]
            pe = pltpu.roll(win, sub + LANES - DILATION_STEP, 1)[:, :sub]

            def tap(base):
                return wtr[pl.ds(pl.multiple_of(base + top, HALF), HALF), :]

            return (dot(tap(512), pn[0:512]) + dot(wtr[pl.ds(pl.multiple_of(KP + 512 + top, LANES), HALF), :], pn[512:1024])
                    + dot(tap(0), pe[0:512]) + dot(wtr[pl.ds(pl.multiple_of(KP + top, LANES), HALF), :], pe[512:1024]))

        def gone(q):
            drain(cin.at[1, :, pl.ds(0, sub)], sem_gv.at[lax.rem(q, POSTS)])

        def give(q):
            remote(cin.at[1, :, lane(q * sub)], grecv.at[:, lane(q * sub)],
                   sem_gv.at[lax.rem(q, POSTS)], sem_gm.at[q], g, mirror).start()

        def add_cond(s):
            now = lane(s * sub)
            keeper = s // per
            spot = gco.at[wc, :, lane(s * sub - keeper * t)]
            drain(kr.at[:, later(s)], sem_kr.at[s])
            gk[:, now] = (gk[:, now].astype(F32) + kr[:, later(s)].astype(F32)).astype(BF)

            @pl.when(keeper == m)
            def _():
                pltpu.make_async_copy(gk.at[:, now], spot, sem_send.at[13]).start()

            @pl.when(keeper != m)
            def _():
                remote(gk.at[:, now], spot, sem_send.at[14], sem_in.at[6], g, keeper).start()

        def combine(q):
            now = lane(q * sub)
            z = lax.rem(q, SLOTS)
            drain(grecv.at[:, now], sem_gm.at[q])

            @pl.when(q >= SLOTS)
            def _():
                drain(gfs.at[z], sem_gf.at[z])

            gfs[z] = (cin[0, :, now].astype(F32) + grecv[:, now].astype(F32)).astype(BF)

            @others
            def _(i):
                remote(gfs.at[z, rows(i), :], gio.at[wc, :, now], sem_gf.at[z], sem_in.at[5], g, first + i).start()

            pltpu.make_async_copy(gfs.at[z, rows(local), :], gio.at[wc, :, now], sem_gf.at[z]).start()

        def send_results(s):
            now = lane(s * sub)
            z = lax.rem(s, SLOTS)

            @others
            def _(i):
                remote(ost.at[z, :, rows(i), :], bro.at[wc, :, :, now], sem_o.at[z], sem_in.at[10], g, first + i).start()

            pltpu.make_async_copy(ost.at[z, :, rows(local), :], bro.at[wc, :, :, now], sem_o.at[z]).start()

            @pl.when(jnp.logical_not(in_half(s)))
            def _():
                remote(gk.at[:, now], kr.at[:, later(s)], sem_send.at[8], sem_kr.at[s], g, mirror).start()

        @pl.loop(0, blocks)
        def _(s):
            at = s * sub
            now = lane(at)
            off = lane(at + LANES)
            z = lax.rem(s, SLOTS)

            @pl.when(s + AHEAD + OWN < blocks)
            def _():
                own(s + AHEAD + OWN)

            @pl.when(s + AHEAD < blocks)
            def _():
                relay(s + AHEAD)

            @pl.when(s >= 1)
            def _():
                send_results(s - 1)

            @pl.when(s >= GIVE + POSTS)
            def _():
                gone(s - GIVE - POSTS)

            @pl.when(s >= GIVE)
            def _():
                give(s - GIVE)

            @pl.when(s >= GIVE + LAG)
            def _():
                combine(s - GIVE - LAG)

            @pl.when(jnp.logical_and(s >= LATE, in_half(s - LATE)))
            def _():
                add_cond(s - LATE)

            @pl.when(jnp.logical_not(in_half(s)))
            def _():
                drain(cnd.at[pl.ds(0, mel), now], sem_km.at[s])

            @pl.when(s >= SLOTS)
            def _():
                drain(ost.at[z], sem_o.at[z])

            drain(xin.at[there, off], sem_xm.at[s])
            drain(cin.at[:, :, now], sem_c.at[s])

            xc = xin[:, off]
            xe = pltpu.roll(xin[:, lane(at, sub + LANES)], DILATION_STEP, 1)[:, LANES:]
            cd = cnd[:, now]
            pre_f = (dot(wall[:, 0:512], xe) + dot(wall[:, 512:1024], xc) + dot(wall[:, 1024:KP], cd))
            pre_g = (dot(wall[:, KP:KP + 512], xe) + dot(wall[:, KP + 512:KP + 1024], xc)
                     + dot(wall[:, KP + 1024:OUT_AT], cd))
            place = at + lax.broadcasted_iota(jnp.int32, (1, sub), 1)
            keep = (place < length).astype(F32)
            th = jnp.tanh(pre_f)
            sg = jax.nn.sigmoid(pre_g)
            hid = (keep * th * sg).astype(BF)
            branch = dot(wtr[OUT_AT:USED, :], hid)
            offset = wall[here, USED:USED + LANES].astype(F32)
            ost[z, 0] = (xin[here, off].astype(F32) + branch[0:HALF] + offset[:, 0:1]).astype(BF)
            ost[z, 1] = (branch[HALF:] + offset[:, 1:2]).astype(BF)
            ct = cin[:, :, now].reshape(2 * HALF, sub)
            for q in range(sub // LANES):
                csum[...] += ct[:, q * LANES:(q + 1) * LANES].astype(F32)
            hg = dot(wall[:, OUT_AT:USED], ct) * keep
            pgf = (hg * sg * (1.0 - th * th)).astype(BF)
            pgg = (hg * th * sg * (1.0 - sg)).astype(BF)
            pg[0:512, sub:] = pgf[:, :LANES]
            pg[512:1024, sub:] = pgg[:, :LANES]
            gacc[:, 0:512] += dot_nt(pgf, xe)
            gacc[:, 512:1024] += dot_nt(pgf, xc)
            gacc[:, 1024:KP] += dot_nt(pgf, cd)
            gacc[:, KP:KP + 512] += dot_nt(pgg, xe)
            gacc[:, KP + 512:KP + 1024] += dot_nt(pgg, xc)
            gacc[:, KP + 1024:OUT_AT] += dot_nt(pgg, cd)
            gacc[:, OUT_AT:USED] += dot_nt(hid, ct)
            gk[:, now] = (dot(wtr[1024:KP, :], pgf) + dot(wtr[KP + 1024:OUT_AT, :], pgg))[0:mel].astype(BF)
            before = lane(jnp.maximum(s - 1, 0) * sub)
            cin[1, :, before] = back((1 - h) * HALF).astype(BF)
            cin[0, :, before] = back(h * HALF).astype(BF)
            pg[0:512, 0:sub] = pgf
            pg[512:1024, 0:sub] = pgg

        send_results(blocks - 1)
        pg[:, sub:] = jnp.zeros((2 * GH, LANES), BF)
        cin[1, :, pl.ds(slot - sub, sub)] = back((1 - h) * HALF).astype(BF)
        cin[0, :, pl.ds(slot - sub, sub)] = back(h * HALF).astype(BF)

        def spread(part, dst, sem):
            @others
            def _(i):
                remote(part.at[rows(i), :], dst, sem, sem_in.at[8], g, first + i).start()

            pltpu.make_async_copy(part.at[rows(local), :], dst, sem_in.at[8]).start()

        spot = lax.broadcasted_iota(jnp.int32, (HALF, LANES), 1)
        total = jnp.sum(csum[...], axis=1, keepdims=True)
        gacc[here, USED:USED + LANES] = jnp.where(spot == 0, total[0:HALF], jnp.where(spot == 1, total[HALF:], 0.0))

        drain(xin.at[pl.ds(0, HALF - clips * r), pl.ds(0, slot)], sem_send.at[5])
        s0 = xin.at[pl.ds(0, band), pl.ds(0, WIDE)]
        for k in range(1, clips):
            to = lax.rem(wc + k, clips)
            s0[...] = gacc[pl.ds(pl.multiple_of(to * band, band), band), :].astype(BF)
            remote(s0, r0.at[k - 1], sem_send.at[9], sem_in.at[7], g, wid(h, to)).start()

        start = blocks - GIVE
        pl.loop(start - POSTS, start - SLOTS)(gone)

        def tail(q):
            gone(q - SLOTS)
            give(q)
            combine(q - LAG)
            more = q + GIVE - LATE

            @pl.when(jnp.logical_and(more < blocks, in_half(more)))
            def _():
                add_cond(more)

        pl.loop(start, start + 2)(tail)
        drain(r0, sem_in.at[7])
        for k in range(1, clips):
            gacc[kept, :] += r0[k - 1].astype(F32)

        @pl.loop(1, d)
        def _(k):
            to = lax.rem(g + k, d)
            src = xin.at[pl.ds(GH - band, band), lane((k - 1) * piece, piece)]
            src[...] = gacc[kept, lane(to * piece, piece)].astype(BF)
            remote(src, r1.at[k - 1], sem_send.at[10], sem_r1.at[k - 1], to, m).start()

        pl.loop(start + 2, start + 7)(tail)

        @pl.loop(1, d)
        def _(k):
            drain(r1.at[k - 1], sem_r1.at[k - 1])
            gacc[kept, mine] += r1[k - 1].astype(F32)

        s2[...] = gacc[kept, mine].astype(BF)

        @pl.when(jnp.logical_not(hub))
        def _():
            remote(s2, r2, sem_send.at[11], sem_in.at[4], g, mirror).start()

        pl.loop(start + 7, start + 13)(tail)

        @pl.when(hub)
        def _():
            drain(r2, sem_in.at[4])

            @pl.when(shared)
            def _():
                s2[...] = (gacc[kept, mine] + r2[...].astype(F32)).astype(BF)
                spread(s2, gw.at[0, :, mine], sem_send.at[11])

            @pl.when(jnp.logical_not(shared))
            def _():
                spread(s2, gw.at[h, :, mine], sem_send.at[11])
                spread(r2, gw.at[1 - h, :, mine], sem_send.at[15])

        pl.loop(start + 13, blocks)(tail)
        share_out()
        pl.loop(blocks - SLOTS, blocks)(gone)
        pl.loop(blocks - LAG, blocks)(combine)

        @pl.loop(0, SLOTS)
        def _(q):
            drain(ost.at[q], sem_o.at[q])
            drain(gfs.at[q], sem_gf.at[q])

        drain(x.at[pl.ds(0, clips - 1)], sem_send.at[3])
        drain(cot.at[pl.ds(0, clips - 1)], sem_send.at[4])
        drain(x, sem_send.at[17])
        drain(wall.at[kept, pl.ds(0, (d - 1) * piece)], sem_send.at[6])
        drain(wall.at[pl.ds(0, GH - band), :], sem_send.at[7])
        drain(gk.at[:, pl.ds(0, slot // 2)], sem_send.at[8])
        drain(cnd.at[pl.ds(0, mel), pl.ds(0, slot // 2)], sem_send.at[12])
        drain(gk.at[:, pl.ds(0, t)], sem_send.at[13])
        drain(gk.at[:, pl.ds(0, slot // 2 - t)], sem_send.at[14])
        drain(r0, sem_send.at[9])
        drain(r1, sem_send.at[10])

    def share_out():
        @pl.when(shared)
        def _():
            drain(gw.at[0, :, mine], sem_in.at[8])
            share(gw.at[0, :, mine])

        @pl.when(jnp.logical_not(shared))
        def _():
            drain(gw.at[:, :, mine], sem_in.at[8])
            share(gw.at[:, :, mine])

    def share(part):
        @pl.loop(1, d)
        def _(k):
            remote(part, part, sem_send.at[16], sem_in.at[9], lax.rem(g + k, d), m).start()

    @pl.when(worker)
    def _():
        work()
        drain(cond.at[pl.ds(0, clips - 1)], sem_send.at[0])
        drain(bro.at[pl.ds(0, clips - 1)], sem_in.at[10])
        drain(gio.at[pl.ds(0, clips - 1)], sem_in.at[5])
        drain(gco.at[pl.ds(0, clips - 1)], sem_in.at[6])

        @pl.when(hub)
        def _():
            drain(s2.at[pl.ds(0, HALF - r), :], sem_send.at[11])

            @pl.when(jnp.logical_not(shared))
            def _():
                drain(r2.at[pl.ds(0, HALF - r), :], sem_send.at[15])

        @pl.when(jnp.logical_not(hub))
        def _():
            drain(s2, sem_send.at[11])

    @pl.when(jnp.logical_not(worker))
    def _():
        far()
        share_out()
        drain(cond, sem_send.at[0])
        drain(lay.at[:, mine], sem_send.at[1])
        drain(bro, sem_in.at[10])
        drain(gio, sem_in.at[5])
        drain(gco, sem_in.at[6])

    own_piece = 2 * d - OUT_AT // piece

    @pl.when(shared)
    def _():
        whole(gw, own_piece - 1, sem_in.at[9])
        whole(gw, d - 1, sem_send.at[16])

    @pl.when(jnp.logical_not(shared))
    def _():
        whole(gw, own_piece - 2, sem_in.at[9])
        whole(gw, 2 * (d - 1), sem_send.at[16])


def run_layer(n, d, x, cot, cond, lens, conv, proj, bias):
    clips, r, slot = x.shape
    mel = cond.shape[1]
    t = slot // n
    sub = min(256, t)
    blocks = slot // sub
    piece = WIDE // d
    width = RESIDUAL_WIDTH
    band = GH // clips
    any_spec = pl.BlockSpec(memory_space=pltpu.HBM)
    vmem = pl.BlockSpec(memory_space=pltpu.VMEM)
    smem = pl.BlockSpec(memory_space=pltpu.SMEM)
    dma = pltpu.SemaphoreType.DMA
    return pl.pallas_call(
        functools.partial(layer_kernel, n, d, clips, slot, sub, mel),
        out_shape=(
            jax.ShapeDtypeStruct((clips, 2, r, slot), BF),
            jax.ShapeDtypeStruct((clips, r, slot), BF),
            jax.ShapeDtypeStruct((clips, mel, t), BF),
            jax.ShapeDtypeStruct((2, r, WIDE), BF),
        ),
        in_specs=[any_spec, any_spec, any_spec, smem, any_spec, any_spec, vmem],
        out_specs=(pl.BlockSpec(memory_space=pl.ANY),) * 3 + (vmem,),
        scratch_shapes=[
            pltpu.VMEM(conv.shape, F32),
            pltpu.VMEM((8, LANES), F32),
            pltpu.VMEM((width, LANES + slot), BF),
            pltpu.VMEM((2, HALF, slot), BF),
            pltpu.VMEM((LANES, slot), BF),
            pltpu.VMEM((HALF, slot), BF),
            pltpu.VMEM((2 * r, WIDE), BF),
            pltpu.VMEM((GH, WIDE), BF),
            pltpu.VMEM((USED, GH), BF),
            pltpu.VMEM((2 * GH, sub + LANES), BF),
            pltpu.VMEM((GH, WIDE), F32),
            pltpu.VMEM((2 * HALF, LANES), F32),
            pltpu.VMEM((SLOTS, 2, HALF, sub), BF),
            pltpu.VMEM((SLOTS, HALF, sub), BF),
            pltpu.VMEM((mel, slot), BF),
            pltpu.VMEM((mel, slot // 2), BF),
            pltpu.VMEM((clips - 1, band, WIDE), BF),
            pltpu.VMEM((d - 1, band, piece), BF),
            pltpu.VMEM((band, piece), BF),
            pltpu.VMEM((band, piece), BF),
            dma((SLOTS,)),
            dma((SLOTS,)),
            dma((18,)),
            dma((blocks,)),
            dma((blocks,)),
            dma((blocks,)),
            dma((blocks,)),
            dma((blocks,)),
            dma((blocks,)),
            dma((blocks,)),
            dma((POSTS,)),
            dma((SLOTS,)),
            dma((SLOTS,)),
            dma((11,)),
            dma((d - 1,)),
            dma((2,)),
        ],
        compiler_params=pltpu.CompilerParams(
            collective_id=0, has_side_effects=True, vmem_limit_bytes=50 << 20
        ),
    )(x, cot, cond, lens, conv, proj, bias)


def adamw(master, first_old, second_old, gradient, step_rate, power_one, power_two):
    first_new = BETA_ONE * first_old + (1.0 - BETA_ONE) * gradient
    second_new = BETA_TWO * second_old + (1.0 - BETA_TWO) * gradient * gradient
    first_hat = first_new / (1.0 - power_one)
    second_hat = second_new / (1.0 - power_two)
    renewed = master - step_rate * (
        first_hat / (jnp.sqrt(second_hat) + EPSILON) + WEIGHT_DECAY * master
    )
    return (renewed, first_new, second_new)


def finish_kernel(
    taps, span,
    lo, gio, cot, gco, gw, cw, cm, cv, ow, om, ov, bw, bm, bv,
    lo_out, gi_out, gc_out, cw_out, ow_out, bw_out, cm_out, om_out, bm_out, cv_out, ov_out, bv_out,
    cl_out, ol_out, bl_out,
    lo_v, gi_v, gco_v, gc_v, gw_v, conv_v, convl_v, proj_v, projl_v,
    sem_lo, sem_small, sem_out,
):
    clips, r, slot = gio.shape
    parts = slot // span
    power_one = jnp.float32(BETA_ONE**STEP)
    power_two = jnp.float32(BETA_TWO**STEP)

    small = [
        pltpu.make_async_copy(src, dst, sem_small.at[i])
        for i, (src, dst) in enumerate(
            [(gw, gw_v), (gco, gco_v)]
        )
    ]
    blocks = [(c, slice(p * span, (p + 1) * span)) for c in range(clips) for p in range(parts)]
    loads = [
        (
            pltpu.make_async_copy(lo.at[c, :, :, at], lo_v.at[c, :, :, at], sem_lo.at[i]),
        )
        for i, (c, at) in enumerate(blocks)
    ]
    for copy in small[:5]:
        copy.start()
    for load in loads[:2]:
        for copy in load:
            copy.start()
    for copy in small[5:]:
        copy.start()
    for load in loads[2:]:
        for copy in load:
            copy.start()

    stores = []

    def store(src, dst):
        copy = pltpu.make_async_copy(src, dst, sem_out.at[len(stores)])
        copy.start()
        stores.append(copy)

    def block(i):
        c, at = blocks[i]
        gi_v[c, :, at] = cot[c, 0, :, at].astype(F32) + gio[c, :, at].astype(F32)
        store(gi_v.at[c, :, at], gi_out.at[c, :, at])
        loads[i][0].wait()
        store(lo_v.at[c, :, :, at], lo_out.at[c, :, :, at])

    block(0)
    for copy in small[:5]:
        copy.wait()
    gc_v[...] = gco_v[...].astype(F32)
    store(gc_v, gc_out)
    for q in range(2):
        w, m, v = adamw(cw[q], cm[q], cv[q], gw_v[0, :, q * KP:q * KP + taps].astype(F32),
                        CONV_RATE, power_one, power_two)
        conv_v[0, q], conv_v[1, q], conv_v[2, q] = w, m, v
        convl_v[q] = w.astype(BF)
    for i, dst in enumerate((cw_out, cm_out, cv_out)):
        store(conv_v.at[i], dst)
    store(convl_v, cl_out)
    block(1)
    for copy in small[5:]:
        copy.wait()
    for q in range(4):
        at = slice(q * HALF, (q + 1) * HALF)
        from_at = OUT_AT + q // 2 * HALF
        w, m, v = adamw(ow[:, at], om[:, at], ov[:, at],
                        gw_v[q % 2, :, from_at:from_at + HALF].astype(F32), OUT_RATE, power_one, power_two)
        proj_v[0, :, at], proj_v[1, :, at], proj_v[2, :, at] = w, m, v
        projl_v[:, at] = w.astype(BF)
    for i, dst in enumerate((ow_out, om_out, ov_out)):
        store(proj_v.at[i], dst)
    store(projl_v, ol_out)
    spot = lax.broadcasted_iota(jnp.int32, (r, LANES), 1)
    last = taps - 1024
    sums = gw_v[0, :, USED:USED + LANES].astype(F32) + gw_v[1, :, USED:USED + LANES].astype(F32)
    columns = (
        gw_v[0, :, 1024:KP].astype(F32)[:, last:last + 1],
        gw_v[0, :, KP + 1024:OUT_AT].astype(F32)[:, last:last + 1],
        sums[:, 0:1],
        sums[:, 1:2],
    )
    table = jnp.zeros((r, LANES), F32)
    for i, column in enumerate(columns):
        table = jnp.where(spot == i, column, table)
    w, m, v = adamw(bw[...], bm[...], bv[...], table.T[0:4], BIAS_RATE, power_one, power_two)
    bw_out[...], bm_out[...], bv_out[...] = w, m, v
    bl_out[...] = w.astype(BF)
    for i in range(2, len(blocks)):
        block(i)
    for copy in stores:
        copy.wait()


def finish(lo, gio, cot, gco, gw, conv, proj, bias):
    clips, r, slot = gio.shape
    taps = conv[0].shape[2]
    span = 2048
    count = clips * (slot // span)
    any_spec = pl.BlockSpec(memory_space=pltpu.HBM)
    vmem = pl.BlockSpec(memory_space=pltpu.VMEM)
    dma = pltpu.SemaphoreType.DMA

    def like(a, dtype=None):
        return jax.ShapeDtypeStruct(a.shape, dtype or a.dtype)

    trio = [like(conv[0]), like(proj[0]), like(bias[0])]
    return pl.pallas_call(
        functools.partial(finish_kernel, taps, span),
        out_shape=[like(lo), like(gio, F32), like(gco, F32)] + trio * 3
        + [like(a, BF) for a in (conv[0], proj[0], bias[0])],
        in_specs=[any_spec] + [vmem] * 2 + [any_spec] * 2 + [vmem] * 9,
        out_specs=[any_spec] * 3 + [any_spec, any_spec, vmem] * 4,
        scratch_shapes=[
            pltpu.VMEM(lo.shape, BF),
            pltpu.VMEM(gio.shape, F32),
            pltpu.VMEM(gco.shape, BF),
            pltpu.VMEM(gco.shape, F32),
            pltpu.VMEM(gw.shape, BF),
            pltpu.VMEM((3, *conv[0].shape), F32),
            pltpu.VMEM(conv[0].shape, BF),
            pltpu.VMEM((3, *proj[0].shape), F32),
            pltpu.VMEM(proj[0].shape, BF),
            dma((count,)),
            dma((2,)),
            dma((2 * count + 9,)),
        ],
        compiler_params=pltpu.CompilerParams(vmem_limit_bytes=24 << 20),
    )(lo, gio, cot, gco, gw, *conv, *proj, *bias)


def per_device(
    n, d,
    inputs, conditioning, lengths, cotangent, conv_weight, out_weight, biases,
    conv_first, out_first, bias_first, conv_second, out_second, bias_second,
):
    conv = [jnp.transpose(a, (1, 2, 0)) for a in (conv_weight, conv_first, conv_second)]
    proj = [out_weight, out_first, out_second]
    bias = [biases, bias_first, bias_second]
    cond = jnp.transpose(conditioning, (0, 2, 1))
    def pinned(a):
        return pltpu.with_memory_space_constraint(a, pltpu.HBM)

    lo, gio, gco, gw = run_layer(
        n, d, pinned(inputs), pinned(cotangent), pinned(cond), pinned(lengths), pinned(conv[0]), pinned(proj[0]), pinned(bias[0])
    )
    lo = pinned(lo)
    outs = finish(lo, gio, cotangent, gco, gw, conv, proj, bias)
    layer_out, grad_input, grad_cond = outs[:3]
    news = [jnp.transpose(a, (2, 0, 1)) if i % 3 == 0 else a for i, a in enumerate(outs[3:])]
    return (layer_out, grad_input, jnp.transpose(grad_cond, (0, 2, 1)), *news)


def solution(mesh):
    in_specs = (
        P("dp", "mp", None),
        P("dp", "mp", None),
        P("dp"),
        P("dp", None, "mp", None),
        P(None, None, "mp"),
        P("mp", None),
        P(None, "mp"),
        P(None, None, "mp"),
        P("mp", None),
        P(None, "mp"),
        P(None, None, "mp"),
        P("mp", None),
        P(None, "mp"),
    )
    out_specs = (
        P("dp", None, "mp", None),
        P("dp", "mp", None),
        P("dp", "mp", None),
        P(None, None, "mp"),
        P("mp", None),
        P(None, "mp"),
        P(None, None, "mp"),
        P("mp", None),
        P(None, "mp"),
        P(None, None, "mp"),
        P("mp", None),
        P(None, "mp"),
        P(None, None, "mp"),
        P("mp", None),
        P(None, "mp"),
    )
    return jax.shard_map(
        functools.partial(per_device, mesh.shape["mp"], mesh.shape["dp"]),
        mesh=mesh, in_specs=in_specs, out_specs=out_specs, check_vma=False,
    )
```
